128 devices in a mesh: comp: 2 (over core), face: 8 (over z_lo, y), tile: 8 (over z_hi, x).
Axes of the slice: x: 4, y: 4, z: 4 (z_hi: 2, z_lo: 2; z = z_hi * 2 + z_lo), core: 2. Of those that a mesh axis runs over, the one named last changes fastest.
Arguments:
- tokens: bfloat16 [2, 512, 128, 512], P('comp', 'tile', 'face'), may hold values from -6 to 6
- norm_gains: bfloat16 [2, 3, 512], P('comp'), may hold values from 0.5 to 1.5
- qkv_weight: bfloat16 [2, 512, 1536], P('comp'), may hold values from -0.25 to 0.25
- out_weight: bfloat16 [2, 512, 512], P('comp'), may hold values from -0.25 to 0.25
- cross_query: bfloat16 [2, 512, 512], P('comp'), may hold values from -0.25 to 0.25
- cross_kv: bfloat16 [2, 512, 1024], P('comp'), may hold values from -0.25 to 0.25
- cross_out: bfloat16 [2, 512, 512], P('comp'), may hold values from -0.25 to 0.25
- up_weight: bfloat16 [2, 512, 2048], P('comp'), may hold values from -0.25 to 0.25
- down_weight: bfloat16 [2, 2048, 512], P('comp'), may hold values from -0.125 to 0.125
- intersection_list: int32 [2, 64, 8, 4], P(None, 'tile', 'face'), may hold values from 0 to 7, all different within a row
- land_bands: int32 [8, 8], replicated, may hold values from 0 to 7
Outputs:
- evolved: bfloat16 [2, 512, 128, 512], P('comp', 'tile', 'face')
The draws below stay inside these ranges and needn't reach their ends.
Inputs may be any that keep to these rules, and one draw needn't show every extreme that they name: `intersection_list`: each band names 4 different bands of the other component's tile. `land_bands`: the land bands of an ocean tile are its first ones.
All inputs are finite; a program needn't handle non-finite values.
Results may differ from the reference program's by a relative error of at most 0.0045.
Values may be sent and summed in bfloat16 or wider, within the bound.
No kernel may reach another device: no remote copies, remote signals or barrier semaphores. Data moves between devices by JAX's collectives and lax.ppermute only.
A program may use at most 128 MiB of HBM per device.

```python
import jax
import jax.numpy as jnp
from jax import lax

D = 512
FF = 2048
HEADS = 8
RX = 16
BR = 8
NB = 8
KC = 4
RY = 64
NLAT = 512
NLON = 128
N_FACE = 8
N_TILE = 8


def set_ends(result, own_key, least, largest):
    dims = result.shape
    index_at = [jax.random.randint(jax.random.fold_in(own_key, axis), (), 0, dims[axis]) for axis in range(len(dims))]
    result = result.at[tuple(index_at)].set(least)
    longest = dims.index(max(dims))
    index_at[longest] = (index_at[longest] + 1) % dims[longest]
    return result.at[tuple(index_at)].set(largest)


def block_levels(stream_key, shape, cuts, smallest, largest):
    level = 1.0
    for position, parts in cuts:
        draws = jax.random.uniform(jax.random.fold_in(jax.random.fold_in(stream_key, 6), position), (parts,), jnp.float32, smallest / len(cuts), largest / len(cuts))
        level = level * jnp.repeat(jnp.exp(draws), shape[position] // parts).reshape((-1,) + (1,) * (len(shape) - 1 - position))
    return level


def distinct(stream_key, rows, count, top, lift):
    order = jax.random.permutation(jax.random.fold_in(stream_key, 1), count)
    favour = order
    for power in range(3):
        favour = favour * favour // count
    favour = favour * lift // count
    lots = jax.random.randint(jax.random.fold_in(stream_key, 2), (rows, count), 0, 4096) + favour
    fixed_rows = jax.random.permutation(jax.random.fold_in(stream_key, 3), rows)[jnp.arange(count) % rows]
    lots = jnp.where(jnp.arange(rows)[:, None] == fixed_rows[None, :], 1 << 14, lots)
    score = lots * count + jnp.arange(count)
    return lax.top_k(score.astype(jnp.int32), top)[1].astype(jnp.int32)


def noise(own_key, shape, scale, limit, split=(), held_as=jnp.bfloat16):
    drawn = jax.random.normal(own_key, shape, jnp.float32) * scale
    if len(split) > 0:
        drawn = block_levels(own_key, shape, split, -0.22, 0.18) * drawn
    return jnp.clip(drawn, min=-limit, max=limit).astype(held_as)


def setup_inputs(seed: int = 0) -> dict:
    key_of = jax.random.split(jax.random.key(seed), 12)
    tokens = noise(key_of[0], (2, NLAT, NLON, D), 1.0, 6.0, ((0, 2), (1, 8), (2, 8)))
    norm_gains = jnp.clip(1.0 + 0.1 * jax.random.normal(key_of[1], (2, 3, D), jnp.float32), 0.5, 1.5).astype(jnp.bfloat16)
    qkv_weight = noise(key_of[2], (2, D, 3 * D), D ** -0.5, 0.25, ((0, 2),))
    out_weight = noise(key_of[3], (2, D, D), D ** -0.5, 0.25, ((0, 2),))
    cross_query = noise(key_of[4], (2, D, D), D ** -0.5, 0.25, ((0, 2),))
    cross_kv = noise(key_of[5], (2, D, 2 * D), D ** -0.5, 0.25, ((0, 2),))
    cross_out = noise(key_of[6], (2, D, D), D ** -0.5, 0.25, ((0, 2),))
    up_weight = noise(key_of[7], (2, D, FF), D ** -0.5, 0.25, ((0, 2),))
    down_weight = noise(key_of[8], (2, FF, D), FF ** -0.5, 0.125, ((0, 2),))
    intersection_list = distinct(key_of[9], 2 * (NB * N_TILE) * N_FACE, NB, KC, 0).reshape((2, NB * N_TILE, N_FACE, KC))
    land_bands = set_ends(jax.random.randint(key_of[10], (N_TILE, N_FACE), 0, NB), jax.random.fold_in(key_of[10], 1), 0, NB - 1).astype(jnp.int32)
    return {"tokens": tokens, "norm_gains": norm_gains, "qkv_weight": qkv_weight, "out_weight": out_weight, "cross_query": cross_query, "cross_kv": cross_kv, "cross_out": cross_out, "up_weight": up_weight, "down_weight": down_weight, "intersection_list": intersection_list, "land_bands": land_bands}


EPSILON = 1e-05

def norm_round(values, gain):
    mean_square = lax.optimization_barrier(jnp.mean(values * values, axis=-1, keepdims=True))
    return (values * lax.rsqrt(mean_square + EPSILON) * gain.astype(jnp.float32)).astype(jnp.bfloat16)

def attend(queries, key_rows, value_rows, usable):
    blocks, count_q, feat_width = queries.shape
    count_k = key_rows.shape[1]
    head_dim = feat_width // HEADS
    score_scale = head_dim ** (-0.5)
    q_heads = queries.astype(jnp.float32).reshape(blocks, count_q, HEADS, head_dim)
    k_heads = key_rows.astype(jnp.float32).reshape(blocks, count_k, HEADS, head_dim)
    v_heads = value_rows.astype(jnp.float32).reshape(blocks, count_k, HEADS, head_dim)
    scores = jnp.einsum('bqhd,bkhd->bhqk', q_heads, k_heads) * score_scale
    scores = jnp.where(usable[:, None, None, :], scores, -1e+30)
    highest = jnp.maximum(lax.optimization_barrier(jnp.max(scores, axis=-1, keepdims=True)), 0.0)
    exp_terms = jnp.exp(scores - highest)
    denominator = lax.optimization_barrier(jnp.sum(exp_terms, axis=-1, keepdims=True)) + jnp.exp(-highest)
    weights = (exp_terms / denominator).astype(jnp.bfloat16)
    blended = jnp.einsum('bhqk,bkhd->bqhd', weights.astype(jnp.float32), v_heads)
    return blended.reshape(blocks, count_q, feat_width).astype(jnp.bfloat16)

def window_bands(array_in):
    grouped = array_in.reshape((NB + 2, BR) + array_in.shape[1:])
    joined = jnp.concatenate([grouped[0:NB], grouped[1:NB + 1], grouped[2:NB + 2]], axis=1)
    return joined.reshape((NB, -1) + array_in.shape[2:])

def to_blocks(grid):
    last_dim = grid.shape[-1]
    pieces = grid.reshape(N_TILE, NB, BR, N_FACE, RX, last_dim)
    return pieces.transpose(0, 3, 1, 2, 4, 5).reshape(N_TILE * N_FACE, NB, BR * RX, last_dim)

def from_blocks(blocked):
    last_dim = blocked.shape[-1]
    pieces = blocked.reshape(N_TILE, N_FACE, NB, BR, RX, last_dim)
    return pieces.transpose(0, 2, 3, 1, 4, 5).reshape(NLAT, NLON, last_dim)

def reference(tokens, norm_gains, qkv_weight, out_weight, cross_query, cross_kv, cross_out, up_weight, down_weight, intersection_list, land_bands):
    land_flat = land_bands.reshape(N_TILE * N_FACE)
    grid_rows = jnp.arange(NLAT, dtype=jnp.int32)
    grid_cols = jnp.arange(NLON, dtype=jnp.int32)
    land_grid = land_bands[grid_rows // RY][:, grid_cols // RX]
    sea_live = (grid_rows % RY // BR)[:, None] >= land_grid
    rows_pad = jnp.arange(NLAT + 2 * BR, dtype=jnp.int32) - BR
    lat_ok = (rows_pad >= 0) & (rows_pad < NLAT)
    rows_in = jnp.clip(rows_pad, 0, NLAT - 1)
    cols_pad = (jnp.arange(NLON + 2 * BR, dtype=jnp.int32) - BR) % NLON
    land_pad = land_bands[rows_in // RY][:, cols_pad // RX]
    sea_pad = (rows_in % RY // BR)[:, None] >= land_pad
    residuals = []
    window_parts = []
    cross_queries = []
    cross_pairs = []
    for component in range(2):
        residual_in = tokens[component].astype(jnp.float32)
        attn_input = norm_round(residual_in, norm_gains[component, 0]).reshape(NLAT * NLON, D)
        cross_input = norm_round(residual_in, norm_gains[component, 1]).reshape(NLAT * NLON, D)
        projected = jnp.dot(attn_input, qkv_weight[component], preferred_element_type=jnp.float32).astype(jnp.bfloat16).reshape(NLAT, NLON, 3 * D)
        pair_rows = projected[:, :, D:]
        pair_rows = jnp.concatenate([pair_rows[:, NLON - BR:], pair_rows, pair_rows[:, :BR]], axis=1)
        pair_rows = jnp.pad(pair_rows, ((BR, BR), (0, 0), (0, 0)))
        if component == 1:
            usable = lat_ok[:, None] & sea_pad
        else:
            usable = lat_ok[:, None] & jnp.ones_like(sea_pad)
        queries = projected[:, :, :D]

        def tile_window(tile_pos):
            tile_row = tile_pos // N_FACE
            tile_col = tile_pos % N_FACE
            row_start = (tile_row * RY).astype(jnp.int32)
            col_start = (tile_col * RX).astype(jnp.int32)
            zero_start = (tile_row * 0).astype(jnp.int32)
            pair_tile = lax.dynamic_slice(pair_rows, (row_start, col_start, zero_start), (RY + 2 * BR, RX + 2 * BR, 2 * D))
            usable_tile = lax.dynamic_slice(usable, (row_start, col_start), (RY + 2 * BR, RX + 2 * BR))
            query_tile = lax.dynamic_slice(queries, (row_start, col_start, zero_start), (RY, RX, D))
            pair_win = window_bands(pair_tile)
            return attend(query_tile.reshape(NB, BR * RX, D), pair_win[:, :, :D], pair_win[:, :, D:], window_bands(usable_tile))
        window_out = lax.map(tile_window, jnp.arange(N_TILE * N_FACE, dtype=jnp.int32))
        window_parts.append(from_blocks(window_out).reshape(NLAT * NLON, D))
        cq_grid = jnp.dot(cross_input, cross_query[component], preferred_element_type=jnp.float32).astype(jnp.bfloat16)
        ckv_grid = jnp.dot(cross_input, cross_kv[component], preferred_element_type=jnp.float32).astype(jnp.bfloat16)
        cross_queries.append(to_blocks(cq_grid.reshape(NLAT, NLON, D)))
        cross_pairs.append(to_blocks(ckv_grid.reshape(NLAT, NLON, 2 * D)))
        residuals.append(residual_in.reshape(NLAT * NLON, D))
    results = []
    for component in range(2):
        partner = 1 - component
        link_table = intersection_list[component].reshape(N_TILE, NB, N_FACE, KC).transpose(0, 2, 1, 3).reshape(N_TILE * N_FACE, NB, KC)
        partner_pairs = cross_pairs[partner]
        own_queries = cross_queries[component]

        def tile_cross(tile_pos):
            chosen = link_table[tile_pos]
            picked = jnp.take(partner_pairs[tile_pos], chosen, axis=0).reshape(NB, KC * BR * RX, 2 * D)
            key_floor = land_flat[tile_pos] * partner
            usable_keys = jnp.repeat(chosen >= key_floor, BR * RX, axis=1)
            return attend(own_queries[tile_pos], picked[:, :, :D], picked[:, :, D:], usable_keys)
        cross_res = from_blocks(lax.map(tile_cross, jnp.arange(N_TILE * N_FACE, dtype=jnp.int32))).reshape(NLAT * NLON, D)
        if component == 1:
            live_mask = jnp.where(sea_live, jnp.float32(1.0), jnp.float32(0.0)).reshape(NLAT * NLON, 1)
        else:
            live_mask = jnp.ones((NLAT * NLON, 1), jnp.float32)
        update = jnp.dot(window_parts[component], out_weight[component], preferred_element_type=jnp.float32)
        update = update + jnp.dot(cross_res, cross_out[component], preferred_element_type=jnp.float32)
        middle = residuals[component] + live_mask * update
        mlp_input = norm_round(middle, norm_gains[component, 2])
        hidden = jax.nn.silu(jnp.dot(mlp_input, up_weight[component], preferred_element_type=jnp.float32)).astype(jnp.bfloat16)
        result_rows = middle + live_mask * jnp.dot(hidden, down_weight[component], preferred_element_type=jnp.float32)
        results.append(result_rows.astype(jnp.bfloat16).reshape(NLAT, NLON, D))
    return jnp.stack(results)
```

```python
import jax
import jax.numpy as jnp
from jax import lax
from jax.experimental import pallas as pl
from jax.experimental.pallas import tpu as pltpu
from jax.sharding import PartitionSpec as P

D = 512
FF = 2048
HEADS = 8
PAIRS = HEADS // 2
LANES = 128
RX = 16
BR = 8
NB = 8
KC = 4
CELLS = BR * RX
ROWS = NB * CELLS
SIDE = BR * BR
GROUP = CELLS + 2 * SIDE
WINDOW = 3 * GROUP

EPSILON = 1e-05
Q_SCALE = 1.4426950408889634 / 8.0
LIMIT = 2.0**100
BF = jnp.bfloat16
F32 = jnp.float32
MIB = 1 << 20


def norm_round(values, gain):
    mean_square = jnp.mean(values * values, axis=-1, keepdims=True)
    return (values * lax.rsqrt(mean_square + EPSILON) * gain.astype(F32)).astype(BF)


def mm(a, b):
    return jnp.dot(a, b, preferred_element_type=F32)


def mm_nt(a, b):
    return lax.dot_general(a, b, (((1,), (1,)), ((), ())), preferred_element_type=F32)


def low_half(rows):
    return lax.broadcasted_iota(jnp.int32, (rows, LANES), 1) < LANES // 2


def augment(values, flag, out_ref, row, rows):
    lo = low_half(rows)
    one = jnp.ones((rows, LANES), BF)
    keep = flag.astype(F32).astype(BF)
    for p in range(PAIRS):
        pair = values[:, p * LANES : (p + 1) * LANES]
        even = jnp.where(lo, pair, one) * keep
        odd = jnp.where(lo, one, pair) * keep
        out_ref[pl.ds(row, rows), pl.ds(2 * p * LANES, LANES)] = even
        out_ref[pl.ds(row, rows), pl.ds((2 * p + 1) * LANES, LANES)] = odd


def attend_pair(pair, keys, even_values, odd_values, mask=None):
    lo = low_half(CELLS)
    zero = jnp.zeros_like(pair)
    stacked = jnp.concatenate([jnp.where(lo, pair, zero), jnp.where(lo, zero, pair)], axis=0)
    scores = mm_nt(stacked, keys)
    if mask is None:
        extra = 1.0
    else:
        scores = jnp.where(mask > 0.5, scores, -1e30)
        highest = jnp.maximum(jnp.max(scores, axis=-1, keepdims=True), 0.0)
        scores = scores - highest
        extra = jnp.exp2(-highest)
        extra = jnp.where(lo, extra[:CELLS], extra[CELLS:])
    terms = jnp.exp2(scores).astype(BF)
    even = mm(terms[:CELLS], even_values)
    odd = mm(terms[CELLS:], odd_values)
    sums = jnp.where(lo, odd, even)
    below = pltpu.roll(sums, LANES // 2, 1) + extra
    return (jnp.where(lo, even, odd) / below).astype(BF), sums


def kernel_cross_kv(x_ref, gain_ref, weight_ref, out_ref):
    cross_input = norm_round(x_ref[...].astype(F32), gain_ref[1:2, :])
    out_ref[...] = mm(cross_input, weight_ref[...]).astype(BF)


def kernel_own(x_ref, gain_ref, qkv_ref, cq_ref, q_ref, k_ref, v_ref, c_ref):
    values = x_ref[...].astype(F32)
    mean_square = jnp.mean(values * values, axis=-1, keepdims=True)
    unit = values * lax.rsqrt(mean_square + EPSILON)
    attn_input = (unit * gain_ref[0:1, :].astype(F32)).astype(BF)
    cross_input = (unit * gain_ref[1:2, :].astype(F32)).astype(BF)
    q_ref[...] = (mm(attn_input, qkv_ref[:, :D]) * Q_SCALE).astype(BF)
    k_ref[...] = mm(attn_input, qkv_ref[:, D : 2 * D]).astype(BF)
    v_ref[...] = mm(attn_input, qkv_ref[:, 2 * D :]).astype(BF)
    c_ref[...] = (mm(cross_input, cq_ref[...]) * Q_SCALE).astype(BF)


def kernel_cross(links_ref, land_ref, q_ref, kv_ref, out_ref, va_ref, bad_ref):
    component = lax.axis_index("comp")
    own_land = land_ref[lax.axis_index("tile"), lax.axis_index("face")]
    floor = jnp.where(component == 1, 0, own_land)

    def prepare(j, carry):
        row = pl.multiple_of(j * CELLS, CELLS)
        augment(kv_ref[pl.ds(row, CELLS), D:], j >= floor, va_ref, row, CELLS)
        return carry

    lax.fori_loop(0, NB, prepare, 0)
    bad_ref[...] = jnp.zeros_like(bad_ref)

    def band(exact):
        def body(i, carry):
            row = pl.multiple_of(i * CELLS, CELLS)
            picks = [links_ref[component, i, 0, k] for k in range(KC)]
            rows = [pl.multiple_of(j * CELLS, CELLS) for j in picks]
            mask = None
            if exact:
                mask = jnp.concatenate(
                    [jnp.full((1, CELLS), (j >= floor).astype(F32)) for j in picks], axis=1
                )
            for p in range(PAIRS):
                pair = q_ref[pl.ds(row, CELLS), pl.ds(p * LANES, LANES)]
                keys = jnp.concatenate(
                    [kv_ref[pl.ds(r, CELLS), pl.ds(p * LANES, LANES)] for r in rows], axis=0
                )
                even, odd = [
                    jnp.concatenate(
                        [va_ref[pl.ds(r, CELLS), pl.ds((2 * p + h) * LANES, LANES)] for r in rows],
                        axis=0,
                    )
                    for h in range(2)
                ]
                result, sums = attend_pair(pair, keys, even, odd, mask)
                out_ref[pl.ds(row, CELLS), pl.ds(p * LANES, LANES)] = result
                if not exact:
                    bad_ref[...] += jnp.where(sums < LIMIT, 0.0, 1.0)
            return carry

        return body

    lax.fori_loop(0, NB, band(False), 0)

    @pl.when(jnp.sum(bad_ref[...]) > 0.0)
    def _():
        lax.fori_loop(0, NB, band(True), 0)


def kernel_window(
    land_ref,
    x_ref,
    north_ref,
    south_ref,
    west_ref,
    east_ref,
    gain_ref,
    qkv_ref,
    q_ref,
    k_ref,
    v_ref,
    cross_ref,
    out_w_ref,
    cross_w_ref,
    up_ref,
    down_ref,
    out_ref,
    keys_ref,
    va_ref,
    win_ref,
    bad_ref,
):
    is_air = lax.axis_index("comp") == 0
    tile_row = lax.axis_index("tile")
    tile_col = lax.axis_index("face")
    columns = (tile_col, (tile_col + 7) % 8, (tile_col + 1) % 8)

    def flags(r):
        inside_row = jnp.where(r == 0, tile_row - 1, jnp.where(r == NB + 1, tile_row + 1, tile_row))
        lat_ok = (inside_row >= 0) & (inside_row < 8)
        safe_row = jnp.clip(inside_row, 0, 7)
        index = jnp.where(r == 0, NB - 1, jnp.where(r == NB + 1, 0, r - 1))
        return [lat_ok & (is_air | (index >= land_ref[safe_row, c])) for c in columns]

    def project(rows_x, r, offset, parts):
        normed = norm_round(rows_x.astype(F32), gain_ref[0:1, :])
        start = pl.multiple_of(r * GROUP, GROUP) + offset
        keys_ref[pl.ds(start, rows_x.shape[0]), :] = mm(normed, qkv_ref[:, D : 2 * D]).astype(BF)
        values = mm(normed, qkv_ref[:, 2 * D :]).astype(BF)
        at = 0
        for rows, flag in parts:
            augment(values[at : at + rows], flag, va_ref, start + at, rows)
            at += rows

    def sides(r, carry):
        _, west_ok, east_ok = flags(r)
        at = pl.multiple_of(r * SIDE, SIDE)
        rows_x = jnp.concatenate([west_ref[pl.ds(at, SIDE), :], east_ref[pl.ds(at, SIDE), :]], axis=0)
        project(rows_x, r, CELLS, ((SIDE, west_ok), (SIDE, east_ok)))
        return carry

    lax.fori_loop(0, NB + 2, sides, 0)
    project(north_ref[...], 0, 0, ((CELLS, flags(0)[0]),))
    project(south_ref[...], NB + 1, 0, ((CELLS, flags(NB + 1)[0]),))

    def own(i, carry):
        row = pl.multiple_of(i * CELLS, CELLS)
        start = pl.multiple_of((i + 1) * GROUP, GROUP)
        keys_ref[pl.ds(start, CELLS), :] = k_ref[pl.ds(row, CELLS), :]
        augment(v_ref[pl.ds(row, CELLS), :], flags(i + 1)[0], va_ref, start, CELLS)
        return carry

    lax.fori_loop(0, NB, own, 0)
    bad_ref[...] = jnp.zeros_like(bad_ref)

    def band(exact):
        def body(i, carry):
            row = pl.multiple_of(i * CELLS, CELLS)
            start = pl.multiple_of(i * GROUP, GROUP)
            mask = None
            if exact:
                pieces = []
                for b in range(3):
                    for rows, flag in zip((CELLS, SIDE, SIDE), flags(i + b)):
                        pieces.append(jnp.full((1, rows), flag.astype(F32)))
                mask = jnp.concatenate(pieces, axis=1)
            for p in range(PAIRS):
                pair = q_ref[pl.ds(row, CELLS), pl.ds(p * LANES, LANES)]
                keys = keys_ref[pl.ds(start, WINDOW), pl.ds(p * LANES, LANES)]
                even = va_ref[pl.ds(start, WINDOW), pl.ds(2 * p * LANES, LANES)]
                odd = va_ref[pl.ds(start, WINDOW), pl.ds((2 * p + 1) * LANES, LANES)]
                result, sums = attend_pair(pair, keys, even, odd, mask)
                win_ref[pl.ds(row, CELLS), pl.ds(p * LANES, LANES)] = result
                if not exact:
                    bad_ref[...] += jnp.where(sums < LIMIT, 0.0, 1.0)
            return carry

        return body

    lax.fori_loop(0, NB, band(False), 0)

    @pl.when(jnp.sum(bad_ref[...]) > 0.0)
    def _():
        lax.fori_loop(0, NB, band(True), 0)

    chunk = 256
    own_land = land_ref[tile_row, tile_col]

    def feed(c, carry):
        row = pl.multiple_of(c * chunk, chunk)
        at = pl.ds(row, chunk)
        index = (row + lax.broadcasted_iota(jnp.int32, (chunk, 1), 0)) // CELLS
        live = jnp.where(is_air | (index >= own_land), 1.0, 0.0)
        update = mm(win_ref[at, :], out_w_ref[...]) + mm(cross_ref[at, :], cross_w_ref[...])
        middle = x_ref[at, :].astype(F32) + live * update
        mlp_input = norm_round(middle, gain_ref[2:3, :])
        half = 0.5 * mm(mlp_input, up_ref[...])
        hidden = (half + half * jnp.tanh(half)).astype(BF)
        out_ref[at, :] = (middle + live * mm(hidden, down_ref[...])).astype(BF)
        return carry

    lax.fori_loop(0, ROWS // chunk, feed, 0)


VMEM = pl.BlockSpec(memory_space=pltpu.VMEM)
SMEM = pl.BlockSpec(memory_space=pltpu.SMEM)


def array(*shape, dtype=BF):
    return jax.ShapeDtypeStruct(shape, dtype)


def cost(macs, size, exps=0):
    return pl.CostEstimate(flops=2 * macs, bytes_accessed=size, transcendentals=exps)


def per_device(
    tokens,
    norm_gains,
    qkv_weight,
    out_weight,
    cross_query,
    cross_kv,
    cross_out,
    up_weight,
    down_weight,
    intersection_list,
    land_bands,
):
    grid_x = tokens[0]
    x = grid_x.reshape(ROWS, D)
    gains = norm_gains[0]
    up_ring = [(i, i + 1) for i in range(7)]
    down_ring = [(i + 1, i) for i in range(7)]
    east_ring = [(i, (i + 1) % 8) for i in range(8)]
    west_ring = [((i + 1) % 8, i) for i in range(8)]

    north = lax.ppermute(grid_x[-BR:], "tile", up_ring)
    south = lax.ppermute(grid_x[:BR], "tile", down_ring)

    half = ROWS // 2
    pair_out = pl.pallas_call(
        kernel_cross_kv,
        grid=(2,),
        in_specs=[
            pl.BlockSpec((half, D), lambda i: (i, 0)),
            pl.BlockSpec((3, D), lambda i: (0, 0)),
            pl.BlockSpec((D, 2 * D), lambda i: (0, 0)),
        ],
        out_specs=pl.BlockSpec((half, 2 * D), lambda i: (i, 0)),
        out_shape=array(ROWS, 2 * D),
        cost_estimate=cost(ROWS * D * 2 * D, 4 * MIB),
        compiler_params=pltpu.CompilerParams(vmem_limit_bytes=24 * MIB),
        name="cross_kv",
    )(x, gains, cross_kv[0])
    partner = lax.ppermute(pair_out, "comp", [(0, 1), (1, 0)])

    tall = jnp.concatenate([north, grid_x, south], axis=0)
    west = lax.ppermute(tall[:, RX - BR :], "face", east_ring).reshape((NB + 2) * SIDE, D)
    east = lax.ppermute(tall[:, :BR], "face", west_ring).reshape((NB + 2) * SIDE, D)

    block = pl.BlockSpec((half, D), lambda i: (i, 0))
    q, k, v, cross_q = pl.pallas_call(
        kernel_own,
        grid=(2,),
        in_specs=[
            block,
            pl.BlockSpec((3, D), lambda i: (0, 0)),
            pl.BlockSpec((D, 3 * D), lambda i: (0, 0)),
            pl.BlockSpec((D, D), lambda i: (0, 0)),
        ],
        out_specs=[block] * 4,
        out_shape=[array(ROWS, D)] * 4,
        cost_estimate=cost(ROWS * D * 4 * D, 7 * MIB),
        compiler_params=pltpu.CompilerParams(vmem_limit_bytes=24 * MIB),
        name="own",
    )(x, gains, qkv_weight[0], cross_query[0])

    cross = pl.pallas_call(
        kernel_cross,
        in_specs=[SMEM, SMEM, VMEM, VMEM],
        out_specs=VMEM,
        out_shape=array(ROWS, D),
        scratch_shapes=[pltpu.VMEM((ROWS, HEADS * LANES), BF), pltpu.VMEM((CELLS, LANES), F32)],
        cost_estimate=cost(8 * ROWS * 512 * D, 4 * MIB, ROWS * HEADS * 512),
        compiler_params=pltpu.CompilerParams(vmem_limit_bytes=24 * MIB),
        name="cross",
    )(intersection_list, land_bands, cross_q, partner)

    padded_rows = (NB + 2) * GROUP
    result = pl.pallas_call(
        kernel_window,
        in_specs=[SMEM] + [VMEM] * 15,
        out_specs=VMEM,
        out_shape=array(ROWS, D),
        scratch_shapes=[
            pltpu.VMEM((padded_rows, D), BF),
            pltpu.VMEM((padded_rows, HEADS * LANES), BF),
            pltpu.VMEM((ROWS, D), BF),
            pltpu.VMEM((CELLS, LANES), F32),
        ],
        cost_estimate=cost(6 << 30, 12 * MIB, ROWS * HEADS * WINDOW),
        compiler_params=pltpu.CompilerParams(vmem_limit_bytes=40 * MIB),
        name="window",
    )(
        land_bands,
        x,
        north.reshape(CELLS, D),
        south.reshape(CELLS, D),
        west,
        east,
        gains,
        qkv_weight[0],
        q,
        k,
        v,
        cross,
        out_weight[0],
        cross_out[0],
        up_weight[0],
        down_weight[0],
    )
    return result.reshape(1, NB * BR, RX, D)


def solution(mesh):
    placed = (
        P("comp", "tile", "face", None),
        P("comp", None, None),
        P("comp", None, None),
        P("comp", None, None),
        P("comp", None, None),
        P("comp", None, None),
        P("comp", None, None),
        P("comp", None, None),
        P("comp", None, None),
        P(None, "tile", "face", None),
        P(),
    )
    return jax.shard_map(
        per_device,
        mesh=mesh,
        in_specs=placed,
        out_specs=P("comp", "tile", "face", None),
        check_vma=False,
    )
```

```python
import jax
import jax.numpy as jnp
from jax import lax
from jax.experimental import pallas as pl
from jax.experimental.pallas import tpu as pltpu
from jax.sharding import PartitionSpec as P

D = 512
FF = 2048
HEADS = 8
PAIRS = HEADS // 2
LANES = 128
RX = 16
BR = 8
NB = 8
KC = 4
CELLS = BR * RX
ROWS = NB * CELLS
SIDE = BR * BR
GROUP = CELLS + 2 * SIDE
WINDOW = 3 * GROUP

EPSILON = 1e-05
Q_SCALE = 1.4426950408889634 / 8.0
LIMIT = 2.0**100
BF = jnp.bfloat16
F32 = jnp.float32
MIB = 1 << 20


def norm_round(values, gain):
    mean_square = jnp.mean(values * values, axis=-1, keepdims=True)
    return (values * lax.rsqrt(mean_square + EPSILON) * gain.astype(F32)).astype(BF)


def mm(a, b):
    return jnp.dot(a, b, preferred_element_type=F32)


def mm_nt(a, b):
    return lax.dot_general(a, b, (((1,), (1,)), ((), ())), preferred_element_type=F32)


def low_half(rows):
    return lax.broadcasted_iota(jnp.int32, (rows, LANES), 1) < LANES // 2


def augment(values, flag, out_ref, row, rows):
    lo = low_half(rows)
    one = jnp.ones((rows, LANES), BF)
    keep = flag.astype(F32).astype(BF)
    for p in range(PAIRS):
        pair = values[:, p * LANES : (p + 1) * LANES]
        even = jnp.where(lo, pair, one) * keep
        odd = jnp.where(lo, one, pair) * keep
        out_ref[pl.ds(row, rows), pl.ds(2 * p * LANES, LANES)] = even
        out_ref[pl.ds(row, rows), pl.ds((2 * p + 1) * LANES, LANES)] = odd


def attend_pair(pair, keys, even_values, odd_values, mask=None):
    lo = low_half(CELLS)
    zero = jnp.zeros_like(pair)
    stacked = jnp.concatenate([jnp.where(lo, pair, zero), jnp.where(lo, zero, pair)], axis=0)
    scores = mm_nt(stacked, keys)
    if mask is None:
        extra = 1.0
    else:
        scores = jnp.where(mask > 0.5, scores, -1e30)
        highest = jnp.maximum(jnp.max(scores, axis=-1, keepdims=True), 0.0)
        scores = scores - highest
        extra = jnp.exp2(-highest)
        extra = jnp.where(lo, extra[:CELLS], extra[CELLS:])
    terms = jnp.exp2(scores).astype(BF)
    even = mm(terms[:CELLS], even_values)
    odd = mm(terms[CELLS:], odd_values)
    sums = jnp.where(lo, odd, even)
    below = pltpu.roll(sums, LANES // 2, 1) + extra
    return (jnp.where(lo, even, odd) / below).astype(BF), sums


def kernel_cross_kv(x_ref, gain_ref, weight_ref, out_ref):
    cross_input = norm_round(x_ref[...].astype(F32), gain_ref[1:2, :])
    out_ref[...] = mm(cross_input, weight_ref[...]).astype(BF)


def kernel_own(x_ref, gain_ref, qkv_ref, cq_ref, q_ref, k_ref, v_ref, c_ref):
    values = x_ref[...].astype(F32)
    mean_square = jnp.mean(values * values, axis=-1, keepdims=True)
    unit = values * lax.rsqrt(mean_square + EPSILON)
    attn_input = (unit * gain_ref[0:1, :].astype(F32)).astype(BF)
    cross_input = (unit * gain_ref[1:2, :].astype(F32)).astype(BF)
    q_ref[...] = (mm(attn_input, qkv_ref[:, :D]) * Q_SCALE).astype(BF)
    k_ref[...] = mm(attn_input, qkv_ref[:, D : 2 * D]).astype(BF)
    v_ref[...] = mm(attn_input, qkv_ref[:, 2 * D :]).astype(BF)
    c_ref[...] = (mm(cross_input, cq_ref[...]) * Q_SCALE).astype(BF)


def kernel_cross(links_ref, land_ref, q_ref, kv_ref, out_ref, va_ref, bad_ref):
    component = lax.axis_index("comp")
    own_land = land_ref[lax.axis_index("tile"), lax.axis_index("face")]
    floor = jnp.where(component == 1, 0, own_land)

    def prepare(j, carry):
        row = pl.multiple_of(j * CELLS, CELLS)
        augment(kv_ref[pl.ds(row, CELLS), D:], j >= floor, va_ref, row, CELLS)
        return carry

    lax.fori_loop(0, NB, prepare, 0)
    bad_ref[...] = jnp.zeros_like(bad_ref)

    def band(exact):
        def body(i, carry):
            row = pl.multiple_of(i * CELLS, CELLS)
            picks = [links_ref[component, i, 0, k] for k in range(KC)]
            rows = [pl.multiple_of(j * CELLS, CELLS) for j in picks]
            mask = None
            if exact:
                mask = jnp.concatenate(
                    [jnp.full((1, CELLS), (j >= floor).astype(F32)) for j in picks], axis=1
                )
            for p in range(PAIRS):
                pair = q_ref[pl.ds(row, CELLS), pl.ds(p * LANES, LANES)]
                keys = jnp.concatenate(
                    [kv_ref[pl.ds(r, CELLS), pl.ds(p * LANES, LANES)] for r in rows], axis=0
                )
                even, odd = [
                    jnp.concatenate(
                        [va_ref[pl.ds(r, CELLS), pl.ds((2 * p + h) * LANES, LANES)] for r in rows],
                        axis=0,
                    )
                    for h in range(2)
                ]
                result, sums = attend_pair(pair, keys, even, odd, mask)
                out_ref[pl.ds(row, CELLS), pl.ds(p * LANES, LANES)] = result
                if not exact:
                    bad_ref[...] += jnp.where(sums < LIMIT, 0.0, 1.0)
            return carry

        return body

    lax.fori_loop(0, NB, band(False), 0)

    @pl.when(jnp.sum(bad_ref[...]) > 0.0)
    def _():
        lax.fori_loop(0, NB, band(True), 0)


def kernel_window(
    land_ref,
    x_ref,
    north_ref,
    south_ref,
    west_ref,
    east_ref,
    gain_ref,
    qkv_ref,
    q_ref,
    k_ref,
    v_ref,
    cross_ref,
    out_w_ref,
    cross_w_ref,
    up_ref,
    down_ref,
    out_ref,
    keys_ref,
    va_ref,
    win_ref,
    bad_ref,
):
    is_air = lax.axis_index("comp") == 0
    tile_row = lax.axis_index("tile")
    tile_col = lax.axis_index("face")
    columns = (tile_col, (tile_col + 7) % 8, (tile_col + 1) % 8)

    def flags(r):
        inside_row = jnp.where(r == 0, tile_row - 1, jnp.where(r == NB + 1, tile_row + 1, tile_row))
        lat_ok = (inside_row >= 0) & (inside_row < 8)
        safe_row = jnp.clip(inside_row, 0, 7)
        index = jnp.where(r == 0, NB - 1, jnp.where(r == NB + 1, 0, r - 1))
        return [lat_ok & (is_air | (index >= land_ref[safe_row, c])) for c in columns]

    def project(rows_x, r, offset, parts):
        normed = norm_round(rows_x.astype(F32), gain_ref[0:1, :])
        start = pl.multiple_of(r * GROUP, GROUP) + offset
        keys_ref[pl.ds(start, rows_x.shape[0]), :] = mm(normed, qkv_ref[:, D : 2 * D]).astype(BF)
        values = mm(normed, qkv_ref[:, 2 * D :]).astype(BF)
        at = 0
        for rows, flag in parts:
            augment(values[at : at + rows], flag, va_ref, start + at, rows)
            at += rows

    def sides(r, carry):
        _, west_ok, east_ok = flags(r)
        at = pl.multiple_of(r * SIDE, SIDE)
        rows_x = jnp.concatenate([west_ref[pl.ds(at, SIDE), :], east_ref[pl.ds(at, SIDE), :]], axis=0)
        project(rows_x, r, CELLS, ((SIDE, west_ok), (SIDE, east_ok)))
        return carry

    lax.fori_loop(0, NB + 2, sides, 0)
    project(north_ref[...], 0, 0, ((CELLS, flags(0)[0]),))
    project(south_ref[...], NB + 1, 0, ((CELLS, flags(NB + 1)[0]),))

    def own(i, carry):
        row = pl.multiple_of(i * CELLS, CELLS)
        start = pl.multiple_of((i + 1) * GROUP, GROUP)
        keys_ref[pl.ds(start, CELLS), :] = k_ref[pl.ds(row, CELLS), :]
        augment(v_ref[pl.ds(row, CELLS), :], flags(i + 1)[0], va_ref, start, CELLS)
        return carry

    lax.fori_loop(0, NB, own, 0)
    bad_ref[...] = jnp.zeros_like(bad_ref)

    def band(exact):
        def body(i, carry):
            row = pl.multiple_of(i * CELLS, CELLS)
            start = pl.multiple_of(i * GROUP, GROUP)
            mask = None
            if exact:
                pieces = []
                for b in range(3):
                    for rows, flag in zip((CELLS, SIDE, SIDE), flags(i + b)):
                        pieces.append(jnp.full((1, rows), flag.astype(F32)))
                mask = jnp.concatenate(pieces, axis=1)
            for p in range(PAIRS):
                pair = q_ref[pl.ds(row, CELLS), pl.ds(p * LANES, LANES)]
                keys = keys_ref[pl.ds(start, WINDOW), pl.ds(p * LANES, LANES)]
                even = va_ref[pl.ds(start, WINDOW), pl.ds(2 * p * LANES, LANES)]
                odd = va_ref[pl.ds(start, WINDOW), pl.ds((2 * p + 1) * LANES, LANES)]
                result, sums = attend_pair(pair, keys, even, odd, mask)
                win_ref[pl.ds(row, CELLS), pl.ds(p * LANES, LANES)] = result
                if not exact:
                    bad_ref[...] += jnp.where(sums < LIMIT, 0.0, 1.0)
            return carry

        return body

    lax.fori_loop(0, NB, band(False), 0)

    @pl.when(jnp.sum(bad_ref[...]) > 0.0)
    def _():
        lax.fori_loop(0, NB, band(True), 0)

    chunk = 256
    own_land = land_ref[tile_row, tile_col]

    def feed(c, carry):
        row = pl.multiple_of(c * chunk, chunk)
        at = pl.ds(row, chunk)
        index = (row + lax.broadcasted_iota(jnp.int32, (chunk, 1), 0)) // CELLS
        live = jnp.where(is_air | (index >= own_land), 1.0, 0.0)
        update = mm(win_ref[at, :], out_w_ref[...]) + mm(cross_ref[at, :], cross_w_ref[...])
        middle = x_ref[at, :].astype(F32) + live * update
        mlp_input = norm_round(middle, gain_ref[2:3, :])
        half = 0.5 * mm(mlp_input, up_ref[...])
        hidden = (half + half * jnp.tanh(half)).astype(BF)
        out_ref[at, :] = (middle + live * mm(hidden, down_ref[...])).astype(BF)
        return carry

    lax.fori_loop(0, ROWS // chunk, feed, 0)


VMEM = pl.BlockSpec(memory_space=pltpu.VMEM)
SMEM = pl.BlockSpec(memory_space=pltpu.SMEM)


def array(*shape, dtype=BF):
    return jax.ShapeDtypeStruct(shape, dtype)


def cost(macs, size, exps=0):
    return pl.CostEstimate(flops=2 * macs, bytes_accessed=size, transcendentals=exps)


def per_device(
    tokens,
    norm_gains,
    qkv_weight,
    out_weight,
    cross_query,
    cross_kv,
    cross_out,
    up_weight,
    down_weight,
    intersection_list,
    land_bands,
):
    grid_x = tokens[0]
    x = grid_x.reshape(ROWS, D)
    gains = norm_gains[0]
    up_ring = [(i, i + 1) for i in range(7)]
    down_ring = [(i + 1, i) for i in range(7)]
    east_ring = [(i, (i + 1) % 8) for i in range(8)]
    west_ring = [((i + 1) % 8, i) for i in range(8)]

    top, bottom, x = lax.optimization_barrier((grid_x[:BR], grid_x[-BR:], x))
    north = lax.ppermute(bottom, "tile", up_ring)
    south = lax.ppermute(top, "tile", down_ring)

    half = ROWS // 2
    pair_out = pl.pallas_call(
        kernel_cross_kv,
        grid=(2,),
        in_specs=[
            pl.BlockSpec((half, D), lambda i: (i, 0)),
            pl.BlockSpec((3, D), lambda i: (0, 0)),
            pl.BlockSpec((D, 2 * D), lambda i: (0, 0)),
        ],
        out_specs=pl.BlockSpec((half, 2 * D), lambda i: (i, 0)),
        out_shape=array(ROWS, 2 * D),
        cost_estimate=cost(ROWS * D * 2 * D, 4 * MIB),
        compiler_params=pltpu.CompilerParams(vmem_limit_bytes=24 * MIB),
        name="cross_kv",
    )(x, gains, cross_kv[0])
    tall = jnp.concatenate([north, grid_x, south], axis=0)
    west_edge, east_edge, pair_out = lax.optimization_barrier(
        (tall[:, :BR], tall[:, RX - BR :], pair_out)
    )
    west = lax.ppermute(east_edge, "face", east_ring).reshape((NB + 2) * SIDE, D)
    east = lax.ppermute(west_edge, "face", west_ring).reshape((NB + 2) * SIDE, D)
    partner = lax.ppermute(pair_out, "comp", [(0, 1), (1, 0)])

    block = pl.BlockSpec((half, D), lambda i: (i, 0))
    q, k, v, cross_q = pl.pallas_call(
        kernel_own,
        grid=(2,),
        in_specs=[
            block,
            pl.BlockSpec((3, D), lambda i: (0, 0)),
            pl.BlockSpec((D, 3 * D), lambda i: (0, 0)),
            pl.BlockSpec((D, D), lambda i: (0, 0)),
        ],
        out_specs=[block] * 4,
        out_shape=[array(ROWS, D)] * 4,
        cost_estimate=cost(ROWS * D * 4 * D, 7 * MIB),
        compiler_params=pltpu.CompilerParams(vmem_limit_bytes=24 * MIB),
        name="own",
    )(x, gains, qkv_weight[0], cross_query[0])

    cross = pl.pallas_call(
        kernel_cross,
        in_specs=[SMEM, SMEM, VMEM, VMEM],
        out_specs=VMEM,
        out_shape=array(ROWS, D),
        scratch_shapes=[pltpu.VMEM((ROWS, HEADS * LANES), BF), pltpu.VMEM((CELLS, LANES), F32)],
        cost_estimate=cost(8 * ROWS * 512 * D, 4 * MIB, ROWS * HEADS * 512),
        compiler_params=pltpu.CompilerParams(vmem_limit_bytes=24 * MIB),
        name="cross",
    )(intersection_list, land_bands, cross_q, partner)

    padded_rows = (NB + 2) * GROUP
    result = pl.pallas_call(
        kernel_window,
        in_specs=[SMEM] + [VMEM] * 15,
        out_specs=VMEM,
        out_shape=array(ROWS, D),
        scratch_shapes=[
            pltpu.VMEM((padded_rows, D), BF),
            pltpu.VMEM((padded_rows, HEADS * LANES), BF),
            pltpu.VMEM((ROWS, D), BF),
            pltpu.VMEM((CELLS, LANES), F32),
        ],
        cost_estimate=cost(6 << 30, 12 * MIB, ROWS * HEADS * WINDOW),
        compiler_params=pltpu.CompilerParams(vmem_limit_bytes=40 * MIB),
        name="window",
    )(
        land_bands,
        x,
        north.reshape(CELLS, D),
        south.reshape(CELLS, D),
        west,
        east,
        gains,
        qkv_weight[0],
        q,
        k,
        v,
        cross,
        out_weight[0],
        cross_out[0],
        up_weight[0],
        down_weight[0],
    )
    return result.reshape(1, NB * BR, RX, D)


def solution(mesh):
    placed = (
        P("comp", "tile", "face", None),
        P("comp", None, None),
        P("comp", None, None),
        P("comp", None, None),
        P("comp", None, None),
        P("comp", None, None),
        P("comp", None, None),
        P("comp", None, None),
        P("comp", None, None),
        P(None, "tile", "face", None),
        P(),
    )
    return jax.shard_map(
        per_device,
        mesh=mesh,
        in_specs=placed,
        out_specs=P("comp", "tile", "face", None),
        check_vma=False,
    )
```

```python
import jax
import jax.numpy as jnp
from jax import lax
from jax.experimental import pallas as pl
from jax.experimental.pallas import tpu as pltpu
from jax.sharding import PartitionSpec as P

D = 512
FF = 2048
HEADS = 8
PAIRS = HEADS // 2
LANES = 128
RX = 16
BR = 8
NB = 8
KC = 4
CELLS = BR * RX
ROWS = NB * CELLS
SIDE = BR * BR
GROUP = CELLS + 2 * SIDE
WINDOW = 3 * GROUP
EXTRA = 16
VROWS = LANES + EXTRA

EPSILON = 1e-05
Q_SCALE = 1.4426950408889634 / 8.0
LIMIT = 2.0**100
BF = jnp.bfloat16
F32 = jnp.float32
MIB = 1 << 20


def norm_round(values, gain):
    mean_square = jnp.mean(values * values, axis=-1, keepdims=True)
    return (values * lax.rsqrt(mean_square + EPSILON) * gain.astype(F32)).astype(BF)


def mm(a, b):
    return jnp.dot(a, b, preferred_element_type=F32)


def mm_nt(a, b):
    return lax.dot_general(a, b, (((1,), (1,)), ((), ())), preferred_element_type=F32)


def mm_tn(a, b):
    return lax.dot_general(a, b, (((0,), (0,)), ((), ())), preferred_element_type=F32)


def mm_tt(a, b):
    return lax.dot_general(a, b, (((0,), (1,)), ((), ())), preferred_element_type=F32)


def augment(values_t, flag, out_ref, lane):
    keep = flag.astype(F32).astype(BF)
    for p in range(PAIRS):
        rows = values_t[p * LANES : (p + 1) * LANES]
        out_ref[pl.ds(p * VROWS, LANES), pl.ds(lane, CELLS)] = rows * keep
        out_ref[pl.ds(p * VROWS + LANES, EXTRA), pl.ds(lane, CELLS)] = (
            jnp.ones((EXTRA, CELLS), BF) * keep
        )


def score(pair, keys):
    low = lax.broadcasted_iota(jnp.int32, pair.shape, 1) < LANES // 2
    zero = jnp.zeros_like(pair)
    stacked = jnp.concatenate([jnp.where(low, pair, zero), jnp.where(low, zero, pair)], axis=0)
    return mm_nt(keys, stacked)


def blend(values_t, terms, extra):
    both = mm(values_t, terms)
    sums = both[LANES : LANES + 8]
    share = 1.0 / (sums + extra)
    half = LANES // 2
    result = jnp.concatenate(
        [both[:half, :CELLS] * share[:1, :CELLS], both[half:LANES, CELLS:] * share[:1, CELLS:]],
        axis=0,
    )
    return result.astype(BF), sums


def attention(queries, keys, values, penalties, out_ref, bad_ref):
    bad_ref[...] = jnp.zeros_like(bad_ref)

    def terms_of(i, p):
        return jnp.exp2(score(queries(i, p), keys(i, p))).astype(BF)

    steps = [(i, p) for i in range(NB) for p in range(PAIRS)]
    following = terms_of(*steps[0])
    for n, (i, p) in enumerate(steps):
        terms = following
        if n + 1 < len(steps):
            following = terms_of(*steps[n + 1])
        result, sums = blend(values(i, p), terms, 1.0)
        out_ref[pl.ds(p * LANES, LANES), pl.ds(i * CELLS, CELLS)] = result
        bad_ref[...] += jnp.where(sums < LIMIT, 0.0, 1.0)

    @pl.when(jnp.sum(bad_ref[...]) > 0.0)
    def _():
        def band(i, carry):
            lane = pl.multiple_of(i * CELLS, CELLS)
            for p in range(PAIRS):
                scores = score(queries(i, p), keys(i, p))
                at = 0
                pieces = []
                for rows, penalty in penalties(i):
                    pieces.append(scores[at : at + rows] + penalty)
                    at += rows
                scores = jnp.concatenate(pieces, axis=0)
                highest = jnp.maximum(jnp.max(scores, axis=0, keepdims=True), 0.0)
                terms = jnp.exp2(scores - highest).astype(BF)
                result, _ = blend(values(i, p), terms, jnp.exp2(-highest))
                out_ref[pl.ds(p * LANES, LANES), pl.ds(lane, CELLS)] = result
            return carry

        lax.fori_loop(0, NB, band, 0)


def aligned(i, size):
    return i * size if isinstance(i, int) else pl.multiple_of(i * size, size)


def kernel_cross_kv(x_ref, gain_ref, weight_ref, out_ref):
    cross_input = norm_round(x_ref[...].astype(F32), gain_ref[1:2, :])
    out_ref[:, :D] = mm(cross_input, weight_ref[:, :D]).astype(BF)
    out_ref[:, D:] = mm_tt(weight_ref[:, D:], cross_input).astype(BF)


def kernel_own(x_ref, gain_ref, qkv_ref, cq_ref, q_ref, k_ref, v_ref, c_ref):
    values = x_ref[...].astype(F32)
    mean_square = jnp.mean(values * values, axis=-1, keepdims=True)
    unit = values * lax.rsqrt(mean_square + EPSILON)
    attn_input = (unit * gain_ref[0:1, :].astype(F32)).astype(BF)
    cross_input = (unit * gain_ref[1:2, :].astype(F32)).astype(BF)
    q_ref[...] = (mm(attn_input, qkv_ref[:, :D]) * Q_SCALE).astype(BF)
    k_ref[...] = mm(attn_input, qkv_ref[:, D : 2 * D]).astype(BF)
    v_ref[...] = mm_tt(qkv_ref[:, 2 * D :], attn_input).astype(BF)
    c_ref[...] = (mm(cross_input, cq_ref[...]) * Q_SCALE).astype(BF)


def kernel_cross(links_ref, land_ref, q_ref, kv_ref, out_ref, va_ref, bad_ref):
    component = lax.axis_index("comp")
    own_land = land_ref[lax.axis_index("tile"), lax.axis_index("face")]
    floor = jnp.where(component == 1, 0, own_land)

    for j in range(NB):
        row, lane = (j // 4) * D, D + (j % 4) * CELLS
        augment(kv_ref[row : row + D, lane : lane + CELLS], j >= floor, va_ref, j * CELLS)

    def picks(i):
        return [links_ref[component, i, 0, k] for k in range(KC)]

    def queries(i, p):
        return q_ref[pl.ds(aligned(i, CELLS), CELLS), pl.ds(p * LANES, LANES)]

    def keys(i, p):
        return jnp.concatenate(
            [kv_ref[pl.ds(aligned(j, CELLS), CELLS), pl.ds(p * LANES, LANES)] for j in picks(i)],
            axis=0,
        )

    def values(i, p):
        return jnp.concatenate(
            [va_ref[pl.ds(p * VROWS, VROWS), pl.ds(aligned(j, CELLS), CELLS)] for j in picks(i)],
            axis=1,
        )

    def penalties(i):
        return [(CELLS, jnp.where(j >= floor, 0.0, -1e30)) for j in picks(i)]

    attention(queries, keys, values, penalties, out_ref, bad_ref)


def kernel_window(
    land_ref,
    x_ref,
    north_ref,
    south_ref,
    west_ref,
    east_ref,
    gain_ref,
    qkv_ref,
    q_ref,
    k_ref,
    v_ref,
    cross_ref,
    out_w_ref,
    cross_w_ref,
    up_ref,
    down_ref,
    out_ref,
    keys_ref,
    va_ref,
    win_ref,
    bad_ref,
):
    is_air = lax.axis_index("comp") == 0
    tile_row = lax.axis_index("tile")
    tile_col = lax.axis_index("face")
    columns = (tile_col, (tile_col + 7) % 8, (tile_col + 1) % 8)

    def flags(r):
        inside_row = jnp.where(r == 0, tile_row - 1, jnp.where(r == NB + 1, tile_row + 1, tile_row))
        lat_ok = (inside_row >= 0) & (inside_row < 8)
        safe_row = jnp.clip(inside_row, 0, 7)
        index = jnp.where(r == 0, NB - 1, jnp.where(r == NB + 1, 0, r - 1))
        return [lat_ok & (is_air | (index >= land_ref[safe_row, c])) for c in columns]

    def project(rows_x):
        normed = norm_round(rows_x.astype(F32), gain_ref[0:1, :])
        keys = mm(normed, qkv_ref[:, D : 2 * D]).astype(BF)
        return keys, mm_tt(qkv_ref[:, 2 * D :], normed).astype(BF)

    def put(r, offset, keys, values_t, flag):
        keys_ref[pl.ds(r * GROUP + offset, CELLS), :] = keys
        augment(values_t, flag, va_ref, r * GROUP + offset)

    west_lane = lax.broadcasted_iota(jnp.int32, (1, CELLS), 1) < SIDE
    bands = NB + 2
    blocks = 2
    for b in range(blocks):
        members = range(b * bands // blocks, (b + 1) * bands // blocks)
        rows_x = []
        for r in members:
            rows_x += [west_ref[r * SIDE : (r + 1) * SIDE, :], east_ref[r * SIDE : (r + 1) * SIDE, :]]
        keys, values_t = project(jnp.concatenate(rows_x, axis=0))
        for n, r in enumerate(members):
            _, west_ok, east_ok = flags(r)
            at = slice(n * CELLS, (n + 1) * CELLS)
            flag = jnp.where(west_lane, west_ok.astype(F32), east_ok.astype(F32))
            put(r, CELLS, keys[at], values_t[:, at], flag)
    keys, values_t = project(jnp.concatenate([north_ref[...], south_ref[...]], axis=0))
    put(0, 0, keys[:CELLS], values_t[:, :CELLS], flags(0)[0])
    put(NB + 1, 0, keys[CELLS:], values_t[:, CELLS:], flags(NB + 1)[0])
    for i in range(NB):
        at = slice(i * CELLS, (i + 1) * CELLS)
        put(i + 1, 0, k_ref[at, :], v_ref[:, at], flags(i + 1)[0])

    def queries(i, p):
        return q_ref[pl.ds(aligned(i, CELLS), CELLS), pl.ds(p * LANES, LANES)]

    def keys_of(i, p):
        return keys_ref[pl.ds(aligned(i, GROUP), WINDOW), pl.ds(p * LANES, LANES)]

    def values_of(i, p):
        return va_ref[pl.ds(p * VROWS, VROWS), pl.ds(aligned(i, GROUP), WINDOW)]

    def penalties(i):
        pieces = []
        for b in range(3):
            for rows, flag in zip((CELLS, SIDE, SIDE), flags(i + b)):
                pieces.append((rows, jnp.where(flag, 0.0, -1e30)))
        return pieces

    attention(queries, keys_of, values_of, penalties, win_ref, bad_ref)

    chunk = 512
    own_land = land_ref[tile_row, tile_col]
    for c in range(ROWS // chunk):
        at = slice(c * chunk, (c + 1) * chunk)
        index = (c * chunk + lax.broadcasted_iota(jnp.int32, (chunk, 1), 0)) // CELLS
        live = jnp.where(is_air | (index >= own_land), 1.0, 0.0)
        update = mm_tn(win_ref[:, at], out_w_ref[...]) + mm_tn(cross_ref[:, at], cross_w_ref[...])
        middle = x_ref[at, :].astype(F32) + live * update
        mlp_input = norm_round(middle, gain_ref[2:3, :])
        half = 0.5 * mm(mlp_input, up_ref[...])
        hidden = (half + half * jnp.tanh(half)).astype(BF)
        out_ref[at, :] = (middle + live * mm(hidden, down_ref[...])).astype(BF)


VMEM = pl.BlockSpec(memory_space=pltpu.VMEM)
SMEM = pl.BlockSpec(memory_space=pltpu.SMEM)


def array(*shape, dtype=BF):
    return jax.ShapeDtypeStruct(shape, dtype)


def cost(macs, size, exps=0):
    return pl.CostEstimate(flops=2 * macs, bytes_accessed=size, transcendentals=exps)


def per_device(
    tokens,
    norm_gains,
    qkv_weight,
    out_weight,
    cross_query,
    cross_kv,
    cross_out,
    up_weight,
    down_weight,
    intersection_list,
    land_bands,
):
    grid_x = tokens[0]
    x = grid_x.reshape(ROWS, D)
    gains = norm_gains[0]
    up_ring = [(i, i + 1) for i in range(7)]
    down_ring = [(i + 1, i) for i in range(7)]
    east_ring = [(i, (i + 1) % 8) for i in range(8)]
    west_ring = [((i + 1) % 8, i) for i in range(8)]

    top, bottom, x = lax.optimization_barrier((grid_x[:BR], grid_x[-BR:], x))
    north = lax.ppermute(bottom, "tile", up_ring)
    south = lax.ppermute(top, "tile", down_ring)

    half = ROWS // 2
    pair_out = pl.pallas_call(
        kernel_cross_kv,
        grid=(2,),
        in_specs=[
            pl.BlockSpec((half, D), lambda i: (i, 0)),
            pl.BlockSpec((3, D), lambda i: (0, 0)),
            pl.BlockSpec((D, 2 * D), lambda i: (0, 0)),
        ],
        out_specs=pl.BlockSpec((half, 2 * D), lambda i: (i, 0)),
        out_shape=array(ROWS, 2 * D),
        cost_estimate=cost(ROWS * D * 2 * D, 4 * MIB),
        compiler_params=pltpu.CompilerParams(vmem_limit_bytes=24 * MIB),
        name="cross_kv",
    )(x, gains, cross_kv[0])
    tall = jnp.concatenate([north, grid_x, south], axis=0)
    west_edge, east_edge, pair_out = lax.optimization_barrier(
        (tall[:, :BR], tall[:, RX - BR :], pair_out)
    )
    west = lax.ppermute(east_edge, "face", east_ring).reshape((NB + 2) * SIDE, D)
    east = lax.ppermute(west_edge, "face", west_ring).reshape((NB + 2) * SIDE, D)
    partner = lax.ppermute(pair_out, "comp", [(0, 1), (1, 0)])

    block = pl.BlockSpec((half, D), lambda i: (i, 0))
    q, k, v, cross_q = pl.pallas_call(
        kernel_own,
        grid=(2,),
        in_specs=[
            block,
            pl.BlockSpec((3, D), lambda i: (0, 0)),
            pl.BlockSpec((D, 3 * D), lambda i: (0, 0)),
            pl.BlockSpec((D, D), lambda i: (0, 0)),
        ],
        out_specs=[block, block, pl.BlockSpec((D, half), lambda i: (0, i)), block],
        out_shape=[array(ROWS, D), array(ROWS, D), array(D, ROWS), array(ROWS, D)],
        cost_estimate=cost(ROWS * D * 4 * D, 7 * MIB),
        compiler_params=pltpu.CompilerParams(vmem_limit_bytes=24 * MIB),
        name="own",
    )(x, gains, qkv_weight[0], cross_query[0])

    cross = pl.pallas_call(
        kernel_cross,
        in_specs=[SMEM, SMEM, VMEM, VMEM],
        out_specs=VMEM,
        out_shape=array(D, ROWS),
        scratch_shapes=[pltpu.VMEM((PAIRS * VROWS, ROWS), BF), pltpu.VMEM((8, 2 * CELLS), F32)],
        cost_estimate=cost(8 * ROWS * 512 * D, 4 * MIB, ROWS * HEADS * 512),
        compiler_params=pltpu.CompilerParams(vmem_limit_bytes=24 * MIB),
        name="cross",
    )(intersection_list, land_bands, cross_q, partner)

    padded_rows = (NB + 2) * GROUP
    result = pl.pallas_call(
        kernel_window,
        in_specs=[SMEM] + [VMEM] * 15,
        out_specs=VMEM,
        out_shape=array(ROWS, D),
        scratch_shapes=[
            pltpu.VMEM((padded_rows, D), BF),
            pltpu.VMEM((PAIRS * VROWS, padded_rows), BF),
            pltpu.VMEM((D, ROWS), BF),
            pltpu.VMEM((8, 2 * CELLS), F32),
        ],
        cost_estimate=cost(6 << 30, 12 * MIB, ROWS * HEADS * WINDOW),
        compiler_params=pltpu.CompilerParams(vmem_limit_bytes=40 * MIB),
        name="window",
    )(
        land_bands,
        x,
        north.reshape(CELLS, D),
        south.reshape(CELLS, D),
        west,
        east,
        gains,
        qkv_weight[0],
        q,
        k,
        v,
        cross,
        out_weight[0],
        cross_out[0],
        up_weight[0],
        down_weight[0],
    )
    return result.reshape(1, NB * BR, RX, D)


def solution(mesh):
    placed = (
        P("comp", "tile", "face", None),
        P("comp", None, None),
        P("comp", None, None),
        P("comp", None, None),
        P("comp", None, None),
        P("comp", None, None),
        P("comp", None, None),
        P("comp", None, None),
        P("comp", None, None),
        P(None, "tile", "face", None),
        P(),
    )
    return jax.shard_map(
        per_device,
        mesh=mesh,
        in_specs=placed,
        out_specs=P("comp", "tile", "face", None),
        check_vma=False,
    )
```

```python
import jax
import jax.numpy as jnp
from jax import lax
from jax.experimental import pallas as pl
from jax.experimental.pallas import tpu as pltpu
from jax.sharding import PartitionSpec as P

D = 512
FF = 2048
HEADS = 8
PAIRS = HEADS // 2
LANES = 128
RX = 16
BR = 8
NB = 8
KC = 4
CELLS = BR * RX
ROWS = NB * CELLS
SIDE = BR * BR
GROUP = CELLS + 2 * SIDE
WINDOW = 3 * GROUP
EXTRA = 16
VROWS = LANES + EXTRA

EPSILON = 1e-05
Q_SCALE = 1.4426950408889634 / 8.0
LIMIT = 2.0**100
BF = jnp.bfloat16
F32 = jnp.float32
MIB = 1 << 20


def norm_round(values, gain):
    mean_square = jnp.mean(values * values, axis=-1, keepdims=True)
    return (values * lax.rsqrt(mean_square + EPSILON) * gain.astype(F32)).astype(BF)


def mm(a, b):
    return jnp.dot(a, b, preferred_element_type=F32)


def mm_nt(a, b):
    return lax.dot_general(a, b, (((1,), (1,)), ((), ())), preferred_element_type=F32)


def mm_tn(a, b):
    return lax.dot_general(a, b, (((0,), (0,)), ((), ())), preferred_element_type=F32)


def mm_tt(a, b):
    return lax.dot_general(a, b, (((0,), (1,)), ((), ())), preferred_element_type=F32)


def augment(values_t, flag, out_ref, lane):
    keep = flag.astype(F32).astype(BF)
    for p in range(PAIRS):
        rows = values_t[p * LANES : (p + 1) * LANES]
        out_ref[pl.ds(p * VROWS, LANES), pl.ds(lane, CELLS)] = rows * keep
        out_ref[pl.ds(p * VROWS + LANES, EXTRA), pl.ds(lane, CELLS)] = (
            jnp.ones((EXTRA, CELLS), BF) * keep
        )


def score(pair, keys):
    low = lax.broadcasted_iota(jnp.int32, pair.shape, 1) < LANES // 2
    zero = jnp.zeros_like(pair)
    stacked = jnp.concatenate([jnp.where(low, pair, zero), jnp.where(low, zero, pair)], axis=0)
    return mm_nt(keys, stacked)


def blend(values_t, terms, extra):
    both = mm(values_t, terms)
    sums = both[LANES : LANES + 8]
    share = 1.0 / (sums + extra)
    half = LANES // 2
    result = jnp.concatenate(
        [both[:half, :CELLS] * share[:1, :CELLS], both[half:LANES, CELLS:] * share[:1, CELLS:]],
        axis=0,
    )
    return result.astype(BF), sums


def attention(queries, keys, values, penalties, out_ref, bad_ref):
    bad_ref[...] = jnp.zeros_like(bad_ref)

    def terms_of(i, p):
        return jnp.exp2(score(queries(i, p), keys(i, p))).astype(BF)

    steps = [(i, p) for i in range(NB) for p in range(PAIRS)]
    following = terms_of(*steps[0])
    for n, (i, p) in enumerate(steps):
        terms = following
        if n + 1 < len(steps):
            following = terms_of(*steps[n + 1])
        result, sums = blend(values(i, p), terms, 1.0)
        out_ref[pl.ds(p * LANES, LANES), pl.ds(i * CELLS, CELLS)] = result
        bad_ref[...] += jnp.where(sums < LIMIT, 0.0, 1.0)

    @pl.when(jnp.sum(bad_ref[...]) > 0.0)
    def _():
        def band(i, carry):
            lane = pl.multiple_of(i * CELLS, CELLS)
            for p in range(PAIRS):
                scores = score(queries(i, p), keys(i, p))
                at = 0
                pieces = []
                for rows, penalty in penalties(i):
                    pieces.append(scores[at : at + rows] + penalty)
                    at += rows
                scores = jnp.concatenate(pieces, axis=0)
                highest = jnp.maximum(jnp.max(scores, axis=0, keepdims=True), 0.0)
                terms = jnp.exp2(scores - highest).astype(BF)
                result, _ = blend(values(i, p), terms, jnp.exp2(-highest))
                out_ref[pl.ds(p * LANES, LANES), pl.ds(lane, CELLS)] = result
            return carry

        lax.fori_loop(0, NB, band, 0)


def aligned(i, size):
    return i * size if isinstance(i, int) else pl.multiple_of(i * size, size)


def kernel_cross_kv(x_ref, gain_ref, weight_ref, out_ref):
    cross_input = norm_round(x_ref[...].astype(F32), gain_ref[1:2, :])
    out_ref[:, :D] = mm(cross_input, weight_ref[:, :D]).astype(BF)
    out_ref[:, D:] = mm_tt(weight_ref[:, D:], cross_input).astype(BF)


def kernel_own(x_ref, gain_ref, qkv_ref, cq_ref, q_ref, k_ref, v_ref, c_ref):
    values = x_ref[...].astype(F32)
    mean_square = jnp.mean(values * values, axis=-1, keepdims=True)
    unit = values * lax.rsqrt(mean_square + EPSILON)
    attn_input = (unit * gain_ref[0:1, :].astype(F32)).astype(BF)
    cross_input = (unit * gain_ref[1:2, :].astype(F32)).astype(BF)
    q_ref[...] = (mm(attn_input, qkv_ref[:, :D]) * Q_SCALE).astype(BF)
    k_ref[...] = mm(attn_input, qkv_ref[:, D : 2 * D]).astype(BF)
    v_ref[...] = mm_tt(qkv_ref[:, 2 * D :], attn_input).astype(BF)
    c_ref[...] = (mm(cross_input, cq_ref[...]) * Q_SCALE).astype(BF)


def kernel_cross(
    links_ref,
    land_ref,
    q_ref,
    kv_ref,
    win_ref,
    x_ref,
    gain_ref,
    out_w_ref,
    cross_w_ref,
    up_ref,
    down_ref,
    out_ref,
    cross_ref,
    va_ref,
    bad_ref,
):
    component = lax.axis_index("comp")
    own_land = land_ref[lax.axis_index("tile"), lax.axis_index("face")]
    floor = jnp.where(component == 1, 0, own_land)

    for j in range(NB):
        row, lane = (j // 4) * D, D + (j % 4) * CELLS
        augment(kv_ref[row : row + D, lane : lane + CELLS], j >= floor, va_ref, j * CELLS)

    def picks(i):
        return [links_ref[component, i, 0, k] for k in range(KC)]

    def queries(i, p):
        return q_ref[pl.ds(aligned(i, CELLS), CELLS), pl.ds(p * LANES, LANES)]

    def keys(i, p):
        return jnp.concatenate(
            [kv_ref[pl.ds(aligned(j, CELLS), CELLS), pl.ds(p * LANES, LANES)] for j in picks(i)],
            axis=0,
        )

    def values(i, p):
        return jnp.concatenate(
            [va_ref[pl.ds(p * VROWS, VROWS), pl.ds(aligned(j, CELLS), CELLS)] for j in picks(i)],
            axis=1,
        )

    def penalties(i):
        return [(CELLS, jnp.where(j >= floor, 0.0, -1e30)) for j in picks(i)]

    attention(queries, keys, values, penalties, cross_ref, bad_ref)

    chunk = 512
    is_air = component == 0
    for c in range(ROWS // chunk):
        at = slice(c * chunk, (c + 1) * chunk)
        index = (c * chunk + lax.broadcasted_iota(jnp.int32, (chunk, 1), 0)) // CELLS
        live = jnp.where(is_air | (index >= own_land), 1.0, 0.0)
        update = mm_tn(win_ref[:, at], out_w_ref[...]) + mm_tn(cross_ref[:, at], cross_w_ref[...])
        middle = x_ref[at, :].astype(F32) + live * update
        mlp_input = norm_round(middle, gain_ref[2:3, :])
        half = 0.5 * mm(mlp_input, up_ref[...])
        hidden = (half + half * jnp.tanh(half)).astype(BF)
        out_ref[at, :] = (middle + live * mm(hidden, down_ref[...])).astype(BF)


def kernel_window(
    land_ref,
    north_ref,
    south_ref,
    west_ref,
    east_ref,
    corner_west_ref,
    corner_east_ref,
    gain_ref,
    qkv_ref,
    q_ref,
    k_ref,
    v_ref,
    win_ref,
    keys_ref,
    va_ref,
    bad_ref,
):
    is_air = lax.axis_index("comp") == 0
    tile_row = lax.axis_index("tile")
    tile_col = lax.axis_index("face")
    columns = (tile_col, (tile_col + 7) % 8, (tile_col + 1) % 8)

    def flags(r):
        inside_row = jnp.where(r == 0, tile_row - 1, jnp.where(r == NB + 1, tile_row + 1, tile_row))
        lat_ok = (inside_row >= 0) & (inside_row < 8)
        safe_row = jnp.clip(inside_row, 0, 7)
        index = jnp.where(r == 0, NB - 1, jnp.where(r == NB + 1, 0, r - 1))
        return [lat_ok & (is_air | (index >= land_ref[safe_row, c])) for c in columns]

    def project(rows_x):
        normed = norm_round(rows_x.astype(F32), gain_ref[0:1, :])
        keys = mm(normed, qkv_ref[:, D : 2 * D]).astype(BF)
        return keys, mm_tt(qkv_ref[:, 2 * D :], normed).astype(BF)

    def put(r, offset, keys, values_t, flag):
        keys_ref[pl.ds(r * GROUP + offset, CELLS), :] = keys
        augment(values_t, flag, va_ref, r * GROUP + offset)

    west_lane = lax.broadcasted_iota(jnp.int32, (1, CELLS), 1) < SIDE
    bands = NB + 2
    blocks = 2
    for b in range(blocks):
        members = range(b * bands // blocks, (b + 1) * bands // blocks)
        rows_x = []
        for r in members:
            for side_ref, corner_ref in ((west_ref, corner_west_ref), (east_ref, corner_east_ref)):
                if 1 <= r <= NB:
                    rows_x.append(side_ref[(r - 1) * SIDE : r * SIDE, :])
                else:
                    rows_x.append(corner_ref[min(r, 1) * SIDE : (min(r, 1) + 1) * SIDE, :])
        keys, values_t = project(jnp.concatenate(rows_x, axis=0))
        for n, r in enumerate(members):
            _, west_ok, east_ok = flags(r)
            at = slice(n * CELLS, (n + 1) * CELLS)
            flag = jnp.where(west_lane, west_ok.astype(F32), east_ok.astype(F32))
            put(r, CELLS, keys[at], values_t[:, at], flag)
    keys, values_t = project(jnp.concatenate([north_ref[...], south_ref[...]], axis=0))
    put(0, 0, keys[:CELLS], values_t[:, :CELLS], flags(0)[0])
    put(NB + 1, 0, keys[CELLS:], values_t[:, CELLS:], flags(NB + 1)[0])
    for i in range(NB):
        at = slice(i * CELLS, (i + 1) * CELLS)
        put(i + 1, 0, k_ref[at, :], v_ref[:, at], flags(i + 1)[0])

    def queries(i, p):
        return q_ref[pl.ds(aligned(i, CELLS), CELLS), pl.ds(p * LANES, LANES)]

    def keys_of(i, p):
        return keys_ref[pl.ds(aligned(i, GROUP), WINDOW), pl.ds(p * LANES, LANES)]

    def values_of(i, p):
        return va_ref[pl.ds(p * VROWS, VROWS), pl.ds(aligned(i, GROUP), WINDOW)]

    def penalties(i):
        pieces = []
        for b in range(3):
            for rows, flag in zip((CELLS, SIDE, SIDE), flags(i + b)):
                pieces.append((rows, jnp.where(flag, 0.0, -1e30)))
        return pieces

    attention(queries, keys_of, values_of, penalties, win_ref, bad_ref)


VMEM = pl.BlockSpec(memory_space=pltpu.VMEM)
SMEM = pl.BlockSpec(memory_space=pltpu.SMEM)


def array(*shape, dtype=BF):
    return jax.ShapeDtypeStruct(shape, dtype)


def cost(macs, size, exps=0):
    return pl.CostEstimate(flops=2 * macs, bytes_accessed=size, transcendentals=exps)


def per_device(
    tokens,
    norm_gains,
    qkv_weight,
    out_weight,
    cross_query,
    cross_kv,
    cross_out,
    up_weight,
    down_weight,
    intersection_list,
    land_bands,
):
    grid_x = tokens[0]
    x = grid_x.reshape(ROWS, D)
    gains = norm_gains[0]
    up_ring = [(i, i + 1) for i in range(7)]
    down_ring = [(i + 1, i) for i in range(7)]
    east_ring = [(i, (i + 1) % 8) for i in range(8)]
    west_ring = [((i + 1) % 8, i) for i in range(8)]

    top, bottom, west_edge, east_edge, x_first = lax.optimization_barrier(
        (grid_x[:BR], grid_x[-BR:], grid_x[:, :BR], grid_x[:, -BR:], x)
    )
    west = lax.ppermute(east_edge, "face", east_ring)
    east = lax.ppermute(west_edge, "face", west_ring)
    north = lax.ppermute(bottom, "tile", up_ring)
    south = lax.ppermute(top, "tile", down_ring)

    steps = 4
    part = ROWS // steps
    block = pl.BlockSpec((part, D), lambda i: (i, 0))
    streamed = pltpu.CompilerParams(vmem_limit_bytes=56 * MIB)
    q, k, v, cross_q = pl.pallas_call(
        kernel_own,
        grid=(steps,),
        in_specs=[
            block,
            pl.BlockSpec((3, D), lambda i: (0, 0)),
            pl.BlockSpec((D, 3 * D), lambda i: (0, 0)),
            pl.BlockSpec((D, D), lambda i: (0, 0)),
        ],
        out_specs=[block, block, pl.BlockSpec((D, part), lambda i: (0, i)), block],
        out_shape=[array(ROWS, D), array(ROWS, D), array(D, ROWS), array(ROWS, D)],
        cost_estimate=cost(ROWS * D * 4 * D, 7 * MIB),
        compiler_params=streamed,
        name="own",
    )(x_first, gains, qkv_weight[0], cross_query[0])

    west_corner, east_corner = [
        jnp.concatenate([north[:, cut], south[:, cut]], axis=0)
        for cut in (slice(0, BR), slice(RX - BR, RX))
    ]
    west_corner, east_corner, q, x_second = lax.optimization_barrier(
        (west_corner, east_corner, q, x)
    )

    pair_out = pl.pallas_call(
        kernel_cross_kv,
        grid=(2,),
        in_specs=[
            pl.BlockSpec((ROWS // 2, D), lambda i: (i, 0)),
            pl.BlockSpec((3, D), lambda i: (0, 0)),
            pl.BlockSpec((D, 2 * D), lambda i: (0, 0)),
        ],
        out_specs=pl.BlockSpec((ROWS // 2, 2 * D), lambda i: (i, 0)),
        out_shape=array(ROWS, 2 * D),
        cost_estimate=cost(ROWS * D * 2 * D, 4 * MIB),
        compiler_params=streamed,
        name="cross_kv",
    )(x_second, gains, cross_kv[0])

    corner_west = lax.ppermute(east_corner, "face", east_ring)
    corner_east = lax.ppermute(west_corner, "face", west_ring)
    west, east, corner_west, corner_east, pair_out = lax.optimization_barrier(
        (west, east, corner_west, corner_east, pair_out)
    )
    partner = lax.ppermute(pair_out, "comp", [(0, 1), (1, 0)])

    padded_rows = (NB + 2) * GROUP
    window = pl.pallas_call(
        kernel_window,
        in_specs=[SMEM] + [VMEM] * 11,
        out_specs=VMEM,
        out_shape=array(D, ROWS),
        scratch_shapes=[
            pltpu.VMEM((padded_rows, D), BF),
            pltpu.VMEM((PAIRS * VROWS, padded_rows), BF),
            pltpu.VMEM((8, 2 * CELLS), F32),
        ],
        cost_estimate=cost(4 << 30, 7 * MIB, ROWS * HEADS * WINDOW),
        compiler_params=pltpu.CompilerParams(vmem_limit_bytes=32 * MIB),
        name="window",
    )(
        land_bands,
        north.reshape(CELLS, D),
        south.reshape(CELLS, D),
        west.reshape(NB * SIDE, D),
        east.reshape(NB * SIDE, D),
        corner_west.reshape(2 * SIDE, D),
        corner_east.reshape(2 * SIDE, D),
        gains,
        qkv_weight[0],
        q,
        k,
        v,
    )

    result = pl.pallas_call(
        kernel_cross,
        in_specs=[SMEM] * 2 + [VMEM] * 9,
        out_specs=VMEM,
        out_shape=array(ROWS, D),
        scratch_shapes=[
            pltpu.VMEM((D, ROWS), BF),
            pltpu.VMEM((PAIRS * VROWS, ROWS), BF),
            pltpu.VMEM((8, 2 * CELLS), F32),
        ],
        cost_estimate=cost(5 << 30, 11 * MIB, ROWS * HEADS * 512),
        compiler_params=pltpu.CompilerParams(vmem_limit_bytes=40 * MIB),
        name="cross",
    )(
        intersection_list,
        land_bands,
        cross_q,
        partner,
        window,
        x,
        gains,
        out_weight[0],
        cross_out[0],
        up_weight[0],
        down_weight[0],
    )
    return result.reshape(1, NB * BR, RX, D)


def solution(mesh):
    placed = (
        P("comp", "tile", "face", None),
        P("comp", None, None),
        P("comp", None, None),
        P("comp", None, None),
        P("comp", None, None),
        P("comp", None, None),
        P("comp", None, None),
        P("comp", None, None),
        P("comp", None, None),
        P(None, "tile", "face", None),
        P(),
    )
    return jax.shard_map(
        per_device,
        mesh=mesh,
        in_specs=placed,
        out_specs=P("comp", "tile", "face", None),
        check_vma=False,
    )
```

```python
import jax
import jax.numpy as jnp
from jax import lax
from jax.experimental import pallas as pl
from jax.experimental.pallas import tpu as pltpu
from jax.sharding import PartitionSpec as P

D = 512
FF = 2048
HEADS = 8
PAIRS = HEADS // 2
LANES = 128
RX = 16
BR = 8
NB = 8
KC = 4
CELLS = BR * RX
ROWS = NB * CELLS
SIDE = BR * BR
GROUP = CELLS + 2 * SIDE
WINDOW = 3 * GROUP
EXTRA = 16
VROWS = LANES + EXTRA

EPSILON = 1e-05
Q_SCALE = 1.4426950408889634 / 8.0
LIMIT = 2.0**100
BF = jnp.bfloat16
F32 = jnp.float32
MIB = 1 << 20


def norm_round(values, gain):
    mean_square = jnp.mean(values * values, axis=-1, keepdims=True)
    return (values * lax.rsqrt(mean_square + EPSILON) * gain.astype(F32)).astype(BF)


def mm(a, b):
    return jnp.dot(a, b, preferred_element_type=F32)


def mm_nt(a, b):
    return lax.dot_general(a, b, (((1,), (1,)), ((), ())), preferred_element_type=F32)


def mm_tn(a, b):
    return lax.dot_general(a, b, (((0,), (0,)), ((), ())), preferred_element_type=F32)


def mm_tt(a, b):
    return lax.dot_general(a, b, (((0,), (1,)), ((), ())), preferred_element_type=F32)


def augment(values_t, flag, out_ref, lane):
    keep = flag.astype(F32).astype(BF)
    for p in range(PAIRS):
        rows = values_t[p * LANES : (p + 1) * LANES]
        out_ref[pl.ds(p * VROWS, LANES), pl.ds(lane, CELLS)] = rows * keep
        out_ref[pl.ds(p * VROWS + LANES, EXTRA), pl.ds(lane, CELLS)] = (
            jnp.ones((EXTRA, CELLS), BF) * keep
        )


def score(pair, keys):
    low = lax.broadcasted_iota(jnp.int32, pair.shape, 1) < LANES // 2
    zero = jnp.zeros_like(pair)
    stacked = jnp.concatenate([jnp.where(low, pair, zero), jnp.where(low, zero, pair)], axis=0)
    return mm_nt(keys, stacked)


def blend(values_t, terms, extra):
    both = mm(values_t, terms)
    sums = both[LANES : LANES + 8]
    share = 1.0 / (sums + extra)
    half = LANES // 2
    result = jnp.concatenate(
        [both[:half, :CELLS] * share[:1, :CELLS], both[half:LANES, CELLS:] * share[:1, CELLS:]],
        axis=0,
    )
    return result.astype(BF), sums


def attention(queries, keys, values, penalties, out_ref, bad_ref):
    bad_ref[...] = jnp.zeros_like(bad_ref)

    def terms_of(i, p):
        return jnp.exp2(score(queries(i, p), keys(i, p))).astype(BF)

    steps = [(i, p) for i in range(NB) for p in range(PAIRS)]
    following = terms_of(*steps[0])
    for n, (i, p) in enumerate(steps):
        terms = following
        if n + 1 < len(steps):
            following = terms_of(*steps[n + 1])
        result, sums = blend(values(i, p), terms, 1.0)
        out_ref[pl.ds(p * LANES, LANES), pl.ds(i * CELLS, CELLS)] = result
        bad_ref[...] += jnp.where(sums < LIMIT, 0.0, 1.0)

    @pl.when(jnp.sum(bad_ref[...]) > 0.0)
    def _():
        def band(i, carry):
            lane = pl.multiple_of(i * CELLS, CELLS)
            for p in range(PAIRS):
                scores = score(queries(i, p), keys(i, p))
                at = 0
                pieces = []
                for rows, penalty in penalties(i):
                    pieces.append(scores[at : at + rows] + penalty)
                    at += rows
                scores = jnp.concatenate(pieces, axis=0)
                highest = jnp.maximum(jnp.max(scores, axis=0, keepdims=True), 0.0)
                terms = jnp.exp2(scores - highest).astype(BF)
                result, _ = blend(values(i, p), terms, jnp.exp2(-highest))
                out_ref[pl.ds(p * LANES, LANES), pl.ds(lane, CELLS)] = result
            return carry

        lax.fori_loop(0, NB, band, 0)


def aligned(i, size):
    return i * size if isinstance(i, int) else pl.multiple_of(i * size, size)


def start_all(sem, *moves):
    copies = [pltpu.make_async_copy(src, dst, sem.at[n]) for n, (src, dst) in enumerate(moves)]
    for copy in copies:
        copy.start()
    return copies


def wait_all(copies):
    for copy in copies:
        copy.wait()


def kernel_edges(x_hbm, west_hbm, east_hbm, north_hbm, south_hbm, sem):
    copies = start_all(
        sem,
        (x_hbm.at[:, pl.ds(0, BR)], west_hbm),
        (x_hbm.at[:, pl.ds(RX - BR, BR)], east_hbm),
        (x_hbm.at[pl.ds(0, BR)], north_hbm),
        (x_hbm.at[pl.ds(NB * BR - BR, BR)], south_hbm),
    )
    wait_all(copies)


def normed_rows(copies, x_ref, gain, out_ref):
    half = ROWS // 2
    for h in range(2):
        copies[h].wait()
        at = slice(h * half, (h + 1) * half)
        out_ref[at, :] = norm_round(x_ref[at, :].astype(F32), gain)


def halves(src, dst, size):
    return [(src.at[pl.ds(h * size, size)], dst.at[pl.ds(h * size, size)]) for h in range(2)]


def kernel_own(gain_ref, x_hbm, qkv_hbm, own_hbm, x_ref, qkv_ref, rows_ref, own_ref, sem, out_sem):
    half = ROWS // 2
    parts = [(qkv_hbm.at[:, pl.ds(n * D, D)], qkv_ref.at[:, pl.ds(n * D, D)]) for n in range(3)]
    copies = start_all(sem, *halves(x_hbm, x_ref, half), *parts)
    normed_rows(copies, x_ref, gain_ref[0:1, :], rows_ref)
    leaving = []

    def leave(n):
        at = pl.ds(n * ROWS, ROWS)
        copy = pltpu.make_async_copy(own_ref.at[at], own_hbm.at[at], out_sem.at[n])
        copy.start()
        leaving.append(copy)

    copies[2].wait()
    own_ref[:ROWS, :] = (mm(rows_ref[...], qkv_ref[:, :D]) * Q_SCALE).astype(BF)
    leave(0)
    copies[3].wait()
    own_ref[ROWS : 2 * ROWS, :] = mm(rows_ref[...], qkv_ref[:, D : 2 * D]).astype(BF)
    leave(1)
    copies[4].wait()
    for h in range(2):
        at = slice(2 * ROWS + h * half, 2 * ROWS + (h + 1) * half)
        rows = rows_ref[h * half : (h + 1) * half, :]
        own_ref[at, :] = mm_tt(qkv_ref[:, 2 * D :], rows).astype(BF)
    leave(2)
    wait_all(leaving)


def kernel_pair(gain_ref, x_hbm, ckv_hbm, cq_hbm, query_hbm, pair_hbm, x_ref, w_ref, rows_ref, own_ref, sem, out_sem):
    half = ROWS // 2
    parts = [(ckv_hbm.at[:, pl.ds(n * D, D)], w_ref.at[:, pl.ds(n * D, D)]) for n in range(2)]
    copies = start_all(
        sem, *halves(x_hbm, x_ref, half), *parts, (cq_hbm, w_ref.at[:, pl.ds(2 * D, D)])
    )
    normed_rows(copies, x_ref, gain_ref[1:2, :], rows_ref)
    leaving = []

    def leave(n, src, dst):
        copy = pltpu.make_async_copy(src, dst, out_sem.at[n])
        copy.start()
        leaving.append(copy)

    copies[2].wait()
    own_ref[:ROWS, :] = mm(rows_ref[...], w_ref[:, :D]).astype(BF)
    leave(0, own_ref.at[pl.ds(0, ROWS)], pair_hbm.at[pl.ds(0, ROWS)])
    copies[3].wait()
    for h in range(2):
        at = slice(ROWS + h * half, ROWS + (h + 1) * half)
        rows = rows_ref[h * half : (h + 1) * half, :]
        own_ref[at, :] = mm_tt(w_ref[:, D : 2 * D], rows).astype(BF)
    leave(1, own_ref.at[pl.ds(ROWS, ROWS)], pair_hbm.at[pl.ds(ROWS, ROWS)])
    copies[4].wait()
    own_ref[2 * ROWS :, :] = (mm(rows_ref[...], w_ref[:, 2 * D :]) * Q_SCALE).astype(BF)
    leave(2, own_ref.at[pl.ds(2 * ROWS, ROWS)], query_hbm)
    wait_all(leaving)


def kernel_window(
    land_ref,
    gain_ref,
    own_hbm,
    north_hbm,
    south_hbm,
    west_hbm,
    east_hbm,
    corner_west_hbm,
    corner_east_hbm,
    qkv_hbm,
    win_hbm,
    keys_ref,
    va_ref,
    win_ref,
    bad_ref,
    qkv_ref,
    sides_ref,
    polar_ref,
    q_ref,
    v_ref,
    sem,
    out_sem,
):
    bands = NB + 2
    left, right = pl.ds(0, SIDE), pl.ds(SIDE, SIDE)
    copies = start_all(
        sem,
        (west_hbm, sides_ref.at[pl.ds(1, NB), left]),
        (east_hbm, sides_ref.at[pl.ds(1, NB), right]),
        (corner_west_hbm.at[pl.ds(0, 1)], sides_ref.at[pl.ds(0, 1), left]),
        (corner_east_hbm.at[pl.ds(0, 1)], sides_ref.at[pl.ds(0, 1), right]),
        (corner_west_hbm.at[pl.ds(1, 1)], sides_ref.at[pl.ds(NB + 1, 1), left]),
        (corner_east_hbm.at[pl.ds(1, 1)], sides_ref.at[pl.ds(NB + 1, 1), right]),
        (qkv_hbm.at[:, pl.ds(D, 2 * D)], qkv_ref),
        (north_hbm, polar_ref.at[pl.ds(0, 1)]),
        (south_hbm, polar_ref.at[pl.ds(1, 1)]),
        (own_hbm.at[pl.ds(2 * NB, NB)], v_ref),
        (own_hbm.at[pl.ds(NB, NB)], keys_ref.at[pl.ds(1, NB), pl.ds(0, CELLS)]),
        (own_hbm.at[pl.ds(0, NB)], q_ref),
    )
    is_air = lax.axis_index("comp") == 0
    tile_row = lax.axis_index("tile")
    tile_col = lax.axis_index("face")
    columns = (tile_col, (tile_col + 7) % 8, (tile_col + 1) % 8)

    def flags(r):
        inside_row = jnp.where(r == 0, tile_row - 1, jnp.where(r == NB + 1, tile_row + 1, tile_row))
        lat_ok = (inside_row >= 0) & (inside_row < 8)
        safe_row = jnp.clip(inside_row, 0, 7)
        index = jnp.where(r == 0, NB - 1, jnp.where(r == NB + 1, 0, r - 1))
        return [lat_ok & (is_air | (index >= land_ref[safe_row, c])) for c in columns]

    def project(rows_x):
        normed = norm_round(rows_x.astype(F32), gain_ref[0:1, :])
        keys = mm(normed, qkv_ref[:, :D]).astype(BF)
        return keys, mm_tt(qkv_ref[:, D:], normed).astype(BF)

    west_lane = lax.broadcasted_iota(jnp.int32, (1, CELLS), 1) < SIDE
    wait_all(copies[:7])
    blocks = 2
    for b in range(blocks):
        members = range(b * bands // blocks, (b + 1) * bands // blocks)
        keys, values_t = project(sides_ref[members[0] : members[-1] + 1].reshape(-1, D))
        for n, r in enumerate(members):
            _, west_ok, east_ok = flags(r)
            at = slice(n * CELLS, (n + 1) * CELLS)
            keys_ref[r, CELLS:, :] = keys[at]
            flag = jnp.where(west_lane, west_ok.astype(F32), east_ok.astype(F32))
            augment(values_t[:, at], flag, va_ref, r * GROUP + CELLS)
    wait_all(copies[7:10])
    keys, values_t = project(polar_ref[...].reshape(2 * CELLS, D))
    for n, r in enumerate((0, bands - 1)):
        at = slice(n * CELLS, (n + 1) * CELLS)
        keys_ref[r, :CELLS, :] = keys[at]
        augment(values_t[:, at], flags(r)[0], va_ref, r * GROUP)
    for i in range(NB):
        rows = v_ref[i // 4 * 4 : i // 4 * 4 + 4, :, i % 4 * CELLS : (i % 4 + 1) * CELLS]
        augment(rows.reshape(D, CELLS), flags(i + 1)[0], va_ref, (i + 1) * GROUP)
    wait_all(copies[10:])

    def queries(i, p):
        return q_ref[i, :, pl.ds(p * LANES, LANES)]

    def keys_of(i, p):
        return keys_ref[pl.ds(i, 3), :, pl.ds(p * LANES, LANES)].reshape(WINDOW, LANES)

    def values_of(i, p):
        return va_ref[pl.ds(p * VROWS, VROWS), pl.ds(aligned(i, GROUP), WINDOW)]

    def penalties(i):
        pieces = []
        for b in range(3):
            for rows, flag in zip((CELLS, SIDE, SIDE), flags(i + b)):
                pieces.append((rows, jnp.where(flag, 0.0, -1e30)))
        return pieces

    attention(queries, keys_of, values_of, penalties, win_ref, bad_ref)
    copy = pltpu.make_async_copy(win_ref, win_hbm, out_sem)
    copy.start()
    copy.wait()


def kernel_cross(
    links_ref,
    land_ref,
    gain_ref,
    pair_hbm,
    q_hbm,
    win_hbm,
    x_hbm,
    out_w_hbm,
    cross_w_hbm,
    up_hbm,
    down_hbm,
    out_hbm,
    cross_ref,
    va_ref,
    bad_ref,
    pair_ref,
    q_ref,
    win_ref,
    x_ref,
    out_w_ref,
    cross_w_ref,
    up_ref,
    down_ref,
    out_ref,
    sem,
    out_sem,
):
    half = ROWS // 2
    copies = start_all(
        sem,
        (q_hbm, q_ref),
        *halves(pair_hbm, pair_ref, ROWS),
        (out_w_hbm, out_w_ref),
        (cross_w_hbm, cross_w_ref),
        (win_hbm, win_ref),
        (x_hbm, x_ref),
        (up_hbm, up_ref),
        (down_hbm, down_ref),
    )
    component = lax.axis_index("comp")
    own_land = land_ref[lax.axis_index("tile"), lax.axis_index("face")]
    floor = jnp.where(component == 1, 0, own_land)
    wait_all(copies[:3])
    for j in range(NB):
        row, lane = ROWS + (j // 4) * D, (j % 4) * CELLS
        augment(pair_ref[row : row + D, lane : lane + CELLS], j >= floor, va_ref, j * CELLS)

    def picks(i):
        return [links_ref[component, k, i] for k in range(KC)]

    def queries(i, p):
        return q_ref[pl.ds(aligned(i, CELLS), CELLS), pl.ds(p * LANES, LANES)]

    def keys(i, p):
        return jnp.concatenate(
            [pair_ref[pl.ds(aligned(j, CELLS), CELLS), pl.ds(p * LANES, LANES)] for j in picks(i)],
            axis=0,
        )

    def values(i, p):
        return jnp.concatenate(
            [va_ref[pl.ds(p * VROWS, VROWS), pl.ds(aligned(j, CELLS), CELLS)] for j in picks(i)],
            axis=1,
        )

    def penalties(i):
        return [(CELLS, jnp.where(j >= floor, 0.0, -1e30)) for j in picks(i)]

    attention(queries, keys, values, penalties, cross_ref, bad_ref)
    wait_all(copies[3:])
    leaving = []
    is_air = component == 0
    for c in range(2):
        at = slice(c * half, (c + 1) * half)
        index = (c * half + lax.broadcasted_iota(jnp.int32, (half, 1), 0)) // CELLS
        live = jnp.where(is_air | (index >= own_land), 1.0, 0.0)
        update = mm_tn(win_ref[:, at], out_w_ref[...]) + mm_tn(cross_ref[:, at], cross_w_ref[...])
        middle = x_ref[at, :].astype(F32) + live * update
        mlp_input = norm_round(middle, gain_ref[2:3, :])
        gate = 0.5 * mm(mlp_input, up_ref[...])
        hidden = (gate + gate * jnp.tanh(gate)).astype(BF)
        out_ref[at, :] = (middle + live * mm(hidden, down_ref[...])).astype(BF)
        rows = pl.ds(c * half, half)
        copy = pltpu.make_async_copy(out_ref.at[rows], out_hbm.at[rows], out_sem.at[c])
        copy.start()
        leaving.append(copy)
    wait_all(leaving)


VMEM = pl.BlockSpec(memory_space=pltpu.VMEM)
ANY = pl.BlockSpec(memory_space=pl.ANY)
HBM = pl.BlockSpec(memory_space=pltpu.HBM)
SMEM = pl.BlockSpec(memory_space=pltpu.SMEM)


def array(*shape):
    return jax.ShapeDtypeStruct(shape, BF)


def vmem(*shape):
    return pltpu.VMEM(shape, BF)


def cost(macs, size, exps=0):
    return pl.CostEstimate(flops=2 * macs, bytes_accessed=size, transcendentals=exps)


def per_device(
    tokens,
    norm_gains,
    qkv_weight,
    out_weight,
    cross_query,
    cross_kv,
    cross_out,
    up_weight,
    down_weight,
    intersection_list,
    land_bands,
):
    grid_x = tokens[0]
    x = grid_x.reshape(ROWS, D)
    gains = norm_gains[0]
    up_ring = [(i, i + 1) for i in range(7)]
    down_ring = [(i + 1, i) for i in range(7)]
    east_ring = [(i, (i + 1) % 8) for i in range(8)]
    west_ring = [((i + 1) % 8, i) for i in range(8)]

    params = pltpu.CompilerParams(vmem_limit_bytes=60 * MIB)
    dma = pltpu.SemaphoreType.DMA
    tall, wide = array(NB * BR, BR, D), array(BR, RX, D)
    edges = pl.pallas_call(
        kernel_edges,
        in_specs=[HBM],
        out_specs=[HBM] * 4,
        out_shape=[tall, tall, wide, wide],
        scratch_shapes=[dma((4,))],
        compiler_params=params,
        name="edges",
    )(grid_x)
    west_edge, east_edge, top, bottom, x_first = lax.optimization_barrier((*edges, x))
    west = lax.ppermute(east_edge, "face", east_ring)
    east = lax.ppermute(west_edge, "face", west_ring)
    north = lax.ppermute(bottom, "tile", up_ring)
    south = lax.ppermute(top, "tile", down_ring)

    own = pl.pallas_call(
        kernel_own,
        in_specs=[VMEM] + [HBM] * 2,
        out_specs=HBM,
        out_shape=array(3 * ROWS, D),
        scratch_shapes=[vmem(ROWS, D), vmem(D, 3 * D), vmem(ROWS, D), vmem(3 * ROWS, D), dma((5,)), dma((3,))],
        cost_estimate=cost(ROWS * D * 3 * D, 6 * MIB),
        compiler_params=params,
        name="own",
    )(gains, x_first, qkv_weight[0])

    west_corner, east_corner = [
        jnp.concatenate([north[:, cut], south[:, cut]], axis=0)
        for cut in (slice(0, BR), slice(RX - BR, RX))
    ]
    west_corner, east_corner, own, x_second = lax.optimization_barrier(
        (west_corner, east_corner, own, x)
    )
    corner_west = lax.ppermute(east_corner, "face", east_ring)
    corner_east = lax.ppermute(west_corner, "face", west_ring)

    cross_q, pair_out = pl.pallas_call(
        kernel_pair,
        in_specs=[VMEM] + [HBM] * 3,
        out_specs=[HBM] * 2,
        out_shape=[array(ROWS, D), array(2 * ROWS, D)],
        scratch_shapes=[vmem(ROWS, D), vmem(D, 3 * D), vmem(ROWS, D), vmem(3 * ROWS, D), dma((5,)), dma((3,))],
        cost_estimate=cost(ROWS * D * 3 * D, 6 * MIB),
        compiler_params=params,
        name="pair",
    )(gains, x_second, cross_kv[0], cross_query[0])

    west, east, corner_west, corner_east, pair_out = lax.optimization_barrier(
        (west, east, corner_west, corner_east, pair_out)
    )
    partner = lax.ppermute(pair_out, "comp", [(0, 1), (1, 0)])

    window = pl.pallas_call(
        kernel_window,
        in_specs=[SMEM] + [VMEM, HBM] + [ANY] * 6 + [HBM],
        out_specs=HBM,
        out_shape=array(D, ROWS),
        scratch_shapes=[
            vmem(NB + 2, GROUP, D),
            vmem(PAIRS * VROWS, (NB + 2) * GROUP),
            vmem(D, ROWS),
            pltpu.VMEM((8, 2 * CELLS), F32),
            vmem(D, 2 * D),
            vmem(NB + 2, 2 * SIDE, D),
            vmem(2, CELLS, D),
            vmem(NB, CELLS, D),
            vmem(NB, CELLS, D),
            dma((12,)),
            dma,
        ],
        cost_estimate=cost(4 << 30, 7 * MIB, ROWS * HEADS * WINDOW),
        compiler_params=params,
        name="window",
    )(
        land_bands,
        gains,
        own.reshape(3 * NB, CELLS, D),
        north.reshape(1, CELLS, D),
        south.reshape(1, CELLS, D),
        west.reshape(NB, SIDE, D),
        east.reshape(NB, SIDE, D),
        corner_west.reshape(2, SIDE, D),
        corner_east.reshape(2, SIDE, D),
        qkv_weight[0],
    )

    result = pl.pallas_call(
        kernel_cross,
        in_specs=[SMEM] * 2 + [VMEM, ANY] + [HBM] * 7,
        out_specs=HBM,
        out_shape=array(ROWS, D),
        scratch_shapes=[
            vmem(D, ROWS),
            vmem(PAIRS * VROWS, ROWS),
            pltpu.VMEM((8, 2 * CELLS), F32),
            vmem(2 * ROWS, D),
            vmem(ROWS, D),
            vmem(D, ROWS),
            vmem(ROWS, D),
            vmem(D, D),
            vmem(D, D),
            vmem(D, FF),
            vmem(FF, D),
            vmem(ROWS, D),
            dma((9,)),
            dma((2,)),
        ],
        cost_estimate=cost(5 << 30, 11 * MIB, ROWS * HEADS * 512),
        compiler_params=params,
        name="cross",
    )(
        intersection_list.transpose(0, 2, 3, 1).reshape(2, KC, NB),
        land_bands,
        gains,
        partner,
        cross_q,
        window,
        x,
        out_weight[0],
        cross_out[0],
        up_weight[0],
        down_weight[0],
    )
    return result.reshape(1, NB * BR, RX, D)


def solution(mesh):
    placed = (
        P("comp", "tile", "face", None),
        P("comp", None, None),
        P("comp", None, None),
        P("comp", None, None),
        P("comp", None, None),
        P("comp", None, None),
        P("comp", None, None),
        P("comp", None, None),
        P("comp", None, None),
        P(None, "tile", "face", None),
        P(),
    )
    return jax.shard_map(
        per_device,
        mesh=mesh,
        in_specs=placed,
        out_specs=P("comp", "tile", "face", None),
        check_vma=False,
    )
```

```python
import jax
import jax.numpy as jnp
from jax import lax
from jax.experimental import pallas as pl
from jax.experimental.pallas import tpu as pltpu
from jax.sharding import PartitionSpec as P

D = 512
FF = 2048
HEADS = 8
PAIRS = HEADS // 2
LANES = 128
RX = 16
BR = 8
NB = 8
KC = 4
CELLS = BR * RX
ROWS = NB * CELLS
SIDE = BR * BR
GROUP = CELLS + 2 * SIDE
WINDOW = 3 * GROUP
EXTRA = 16
VROWS = LANES + EXTRA

EPSILON = 1e-05
Q_SCALE = 1.4426950408889634 / 8.0
LIMIT = 2.0**100
BF = jnp.bfloat16
F32 = jnp.float32
MIB = 1 << 20


def norm_round(values, gain):
    mean_square = jnp.mean(values * values, axis=-1, keepdims=True)
    return (values * lax.rsqrt(mean_square + EPSILON) * gain.astype(F32)).astype(BF)


def mm(a, b):
    return jnp.dot(a, b, preferred_element_type=F32)


def mm_nt(a, b):
    return lax.dot_general(a, b, (((1,), (1,)), ((), ())), preferred_element_type=F32)


def mm_tn(a, b):
    return lax.dot_general(a, b, (((0,), (0,)), ((), ())), preferred_element_type=F32)


def mm_tt(a, b):
    return lax.dot_general(a, b, (((0,), (1,)), ((), ())), preferred_element_type=F32)


def augment(values_t, flag, out_ref, lane):
    keep = flag.astype(F32).astype(BF)
    for p in range(PAIRS):
        rows = values_t[p * LANES : (p + 1) * LANES]
        out_ref[pl.ds(p * VROWS, LANES), pl.ds(lane, CELLS)] = rows * keep
        out_ref[pl.ds(p * VROWS + LANES, EXTRA), pl.ds(lane, CELLS)] = (
            jnp.ones((EXTRA, CELLS), BF) * keep
        )


def score(pair, keys):
    low = lax.broadcasted_iota(jnp.int32, pair.shape, 1) < LANES // 2
    zero = jnp.zeros_like(pair)
    stacked = jnp.concatenate([jnp.where(low, pair, zero), jnp.where(low, zero, pair)], axis=0)
    return mm_nt(keys, stacked)


def blend(values_t, terms, extra):
    both = mm(values_t, terms)
    sums = both[LANES : LANES + 8]
    share = 1.0 / (sums + extra)
    half = LANES // 2
    result = jnp.concatenate(
        [both[:half, :CELLS] * share[:1, :CELLS], both[half:LANES, CELLS:] * share[:1, CELLS:]],
        axis=0,
    )
    return result.astype(BF), sums


def attention(queries, keys, values, penalties, out_ref, bad_ref):
    bad_ref[...] = jnp.zeros_like(bad_ref)

    def terms_of(i, p):
        return jnp.exp2(score(queries(i, p), keys(i, p))).astype(BF)

    steps = [(i, p) for i in range(NB) for p in range(PAIRS)]
    following = terms_of(*steps[0])
    for n, (i, p) in enumerate(steps):
        terms = following
        if n + 1 < len(steps):
            following = terms_of(*steps[n + 1])
        result, sums = blend(values(i, p), terms, 1.0)
        out_ref[pl.ds(p * LANES, LANES), pl.ds(i * CELLS, CELLS)] = result
        bad_ref[...] += jnp.where(sums < LIMIT, 0.0, 1.0)

    @pl.when(jnp.sum(bad_ref[...]) > 0.0)
    def _():
        def band(i, carry):
            lane = pl.multiple_of(i * CELLS, CELLS)
            for p in range(PAIRS):
                scores = score(queries(i, p), keys(i, p))
                at = 0
                pieces = []
                for rows, penalty in penalties(i):
                    pieces.append(scores[at : at + rows] + penalty)
                    at += rows
                scores = jnp.concatenate(pieces, axis=0)
                highest = jnp.maximum(jnp.max(scores, axis=0, keepdims=True), 0.0)
                terms = jnp.exp2(scores - highest).astype(BF)
                result, _ = blend(values(i, p), terms, jnp.exp2(-highest))
                out_ref[pl.ds(p * LANES, LANES), pl.ds(lane, CELLS)] = result
            return carry

        lax.fori_loop(0, NB, band, 0)


def aligned(i, size):
    return i * size if isinstance(i, int) else pl.multiple_of(i * size, size)


def kernel_cross_kv(x_ref, gain_ref, weight_ref, out_ref):
    cross_input = norm_round(x_ref[...].astype(F32), gain_ref[1:2, :])
    out_ref[:, :D] = mm(cross_input, weight_ref[:, :D]).astype(BF)
    out_ref[:, D:] = mm_tt(weight_ref[:, D:], cross_input).astype(BF)


def kernel_cross(
    links_ref,
    land_ref,
    q_ref,
    kv_ref,
    win_ref,
    x_ref,
    gain_ref,
    out_w_ref,
    cross_w_ref,
    up_ref,
    down_ref,
    out_ref,
    cross_ref,
    va_ref,
    bad_ref,
):
    component = lax.axis_index("comp")
    own_land = land_ref[lax.axis_index("tile"), lax.axis_index("face")]
    floor = jnp.where(component == 1, 0, own_land)

    for j in range(NB):
        row, lane = (j // 4) * D, D + (j % 4) * CELLS
        augment(kv_ref[row : row + D, lane : lane + CELLS], j >= floor, va_ref, j * CELLS)

    def picks(i):
        return [links_ref[component, k, i] for k in range(KC)]

    def queries(i, p):
        return q_ref[pl.ds(aligned(i, CELLS), CELLS), pl.ds(p * LANES, LANES)]

    def keys(i, p):
        return jnp.concatenate(
            [kv_ref[pl.ds(aligned(j, CELLS), CELLS), pl.ds(p * LANES, LANES)] for j in picks(i)],
            axis=0,
        )

    def values(i, p):
        return jnp.concatenate(
            [va_ref[pl.ds(p * VROWS, VROWS), pl.ds(aligned(j, CELLS), CELLS)] for j in picks(i)],
            axis=1,
        )

    def penalties(i):
        return [(CELLS, jnp.where(j >= floor, 0.0, -1e30)) for j in picks(i)]

    attention(queries, keys, values, penalties, cross_ref, bad_ref)

    chunk = 512
    is_air = component == 0
    for c in range(ROWS // chunk):
        at = slice(c * chunk, (c + 1) * chunk)
        index = (c * chunk + lax.broadcasted_iota(jnp.int32, (chunk, 1), 0)) // CELLS
        live = jnp.where(is_air | (index >= own_land), 1.0, 0.0)
        update = mm_tn(win_ref[:, at], out_w_ref[...]) + mm_tn(cross_ref[:, at], cross_w_ref[...])
        middle = x_ref[at, :].astype(F32) + live * update
        mlp_input = norm_round(middle, gain_ref[2:3, :])
        half = 0.5 * mm(mlp_input, up_ref[...])
        hidden = (half + half * jnp.tanh(half)).astype(BF)
        out_ref[at, :] = (middle + live * mm(hidden, down_ref[...])).astype(BF)


def kernel_window(
    land_ref,
    x_ref,
    face_a_ref,
    face_b_ref,
    tile_a_ref,
    tile_b_ref,
    corner_a_ref,
    corner_b_ref,
    gain_ref,
    qkv_ref,
    cq_ref,
    win_ref,
    query_ref,
    keys_ref,
    va_ref,
    q_ref,
    bad_ref,
):
    is_air = lax.axis_index("comp") == 0
    tile_row = lax.axis_index("tile")
    tile_col = lax.axis_index("face")
    columns = (tile_col, (tile_col + 7) % 8, (tile_col + 1) % 8)

    def flags(r):
        inside_row = jnp.where(r == 0, tile_row - 1, jnp.where(r == NB + 1, tile_row + 1, tile_row))
        lat_ok = (inside_row >= 0) & (inside_row < 8)
        safe_row = jnp.clip(inside_row, 0, 7)
        index = jnp.where(r == 0, NB - 1, jnp.where(r == NB + 1, 0, r - 1))
        return [lat_ok & (is_air | (index >= land_ref[safe_row, c])) for c in columns]

    def project(rows_x):
        normed = norm_round(rows_x.astype(F32), gain_ref[0:1, :])
        keys = mm(normed, qkv_ref[:, D : 2 * D]).astype(BF)
        return keys, mm_tt(qkv_ref[:, 2 * D :], normed).astype(BF)

    def put(r, offset, keys, values_t, flag):
        keys_ref[pl.ds(r * GROUP + offset, CELLS), :] = keys
        augment(values_t, flag, va_ref, r * GROUP + offset)

    values = x_ref[...].astype(F32)
    mean_square = jnp.mean(values * values, axis=-1, keepdims=True)
    unit = values * lax.rsqrt(mean_square + EPSILON)
    attn_input = (unit * gain_ref[0:1, :].astype(F32)).astype(BF)
    cross_input = (unit * gain_ref[1:2, :].astype(F32)).astype(BF)
    q_ref[...] = (mm(attn_input, qkv_ref[:, :D]) * Q_SCALE).astype(BF)
    keys = mm(attn_input, qkv_ref[:, D : 2 * D]).astype(BF)
    values_t = mm_tt(qkv_ref[:, 2 * D :], attn_input).astype(BF)
    for i in range(NB):
        at = slice(i * CELLS, (i + 1) * CELLS)
        put(i + 1, 0, keys[at], values_t[:, at], flags(i + 1)[0])
    query_ref[...] = (mm(cross_input, cq_ref[...]) * Q_SCALE).astype(BF)

    odd_row = tile_row % 2 == 1
    odd_col = tile_col % 2 == 1

    def sorted_pair(odd, a, b):
        return jnp.where(odd, a, b), jnp.where(odd, b, a)

    west, east = sorted_pair(odd_col, face_a_ref[...], face_b_ref[...])
    corners = [sorted_pair(odd_row, c[:SIDE], c[SIDE:]) for c in sorted_pair(odd_col, corner_a_ref[...], corner_b_ref[...])]
    west_lane = lax.broadcasted_iota(jnp.int32, (1, CELLS), 1) < SIDE
    bands = NB + 2
    blocks = 2
    for b in range(blocks):
        members = range(b * bands // blocks, (b + 1) * bands // blocks)
        rows_x = []
        for r in members:
            for side, corner in zip((west, east), corners):
                inside = side[(r - 1) * SIDE : r * SIDE]
                rows_x.append(inside if 1 <= r <= NB else corner[min(r, 1)])
        keys, values_t = project(jnp.concatenate(rows_x, axis=0))
        for n, r in enumerate(members):
            _, west_ok, east_ok = flags(r)
            at = slice(n * CELLS, (n + 1) * CELLS)
            flag = jnp.where(west_lane, west_ok.astype(F32), east_ok.astype(F32))
            put(r, CELLS, keys[at], values_t[:, at], flag)
    polar = sorted_pair(odd_row, tile_a_ref[...], tile_b_ref[...])
    keys, values_t = project(jnp.concatenate(polar, axis=0))
    put(0, 0, keys[:CELLS], values_t[:, :CELLS], flags(0)[0])
    put(bands - 1, 0, keys[CELLS:], values_t[:, CELLS:], flags(bands - 1)[0])

    def queries(i, p):
        return q_ref[pl.ds(aligned(i, CELLS), CELLS), pl.ds(p * LANES, LANES)]

    def keys_of(i, p):
        return keys_ref[pl.ds(aligned(i, GROUP), WINDOW), pl.ds(p * LANES, LANES)]

    def values_of(i, p):
        return va_ref[pl.ds(p * VROWS, VROWS), pl.ds(aligned(i, GROUP), WINDOW)]

    def penalties(i):
        pieces = []
        for b in range(3):
            for rows, flag in zip((CELLS, SIDE, SIDE), flags(i + b)):
                pieces.append((rows, jnp.where(flag, 0.0, -1e30)))
        return pieces

    attention(queries, keys_of, values_of, penalties, win_ref, bad_ref)


VMEM = pl.BlockSpec(memory_space=pltpu.VMEM)
SMEM = pl.BlockSpec(memory_space=pltpu.SMEM)


def array(*shape, dtype=BF):
    return jax.ShapeDtypeStruct(shape, dtype)


def cost(macs, size, exps=0):
    return pl.CostEstimate(flops=2 * macs, bytes_accessed=size, transcendentals=exps)


def per_device(
    tokens,
    norm_gains,
    qkv_weight,
    out_weight,
    cross_query,
    cross_kv,
    cross_out,
    up_weight,
    down_weight,
    intersection_list,
    land_bands,
):
    grid_x = tokens[0]
    x = grid_x.reshape(ROWS, D)
    gains = norm_gains[0]
    swap_a = [(i, i ^ 1) for i in range(8)]
    swap_b = [(i, (i + 1) % 8 if i % 2 else (i - 1) % 8) for i in range(8)]
    odd_row = lax.axis_index("tile") % 2 == 1
    odd_col = lax.axis_index("face") % 2 == 1

    def columns(block):
        low, high = block[:, :BR], block[:, RX - BR :]
        return jnp.where(odd_col, low, high), jnp.where(odd_col, high, low)

    top, bottom = grid_x[:BR], grid_x[NB * BR - BR :]
    face_src_a, face_src_b = columns(grid_x)
    tile_src_a, tile_src_b = jnp.where(odd_row, top, bottom), jnp.where(odd_row, bottom, top)
    face_src_a, face_src_b, tile_src_a, tile_src_b, x_first = lax.optimization_barrier(
        (face_src_a, face_src_b, tile_src_a, tile_src_b, x)
    )
    face_a = lax.ppermute(face_src_a, "face", swap_a)
    face_b = lax.ppermute(face_src_b, "face", swap_b)
    tile_a = lax.ppermute(tile_src_a, "tile", swap_a)
    tile_b = lax.ppermute(tile_src_b, "tile", swap_b)

    half = ROWS // 2
    pair_out = pl.pallas_call(
        kernel_cross_kv,
        grid=(2,),
        in_specs=[
            pl.BlockSpec((half, D), lambda i: (i, 0)),
            pl.BlockSpec((3, D), lambda i: (0, 0)),
            pl.BlockSpec((D, 2 * D), lambda i: (0, 0)),
        ],
        out_specs=pl.BlockSpec((half, 2 * D), lambda i: (i, 0)),
        out_shape=array(ROWS, 2 * D),
        cost_estimate=cost(ROWS * D * 2 * D, 4 * MIB),
        compiler_params=pltpu.CompilerParams(vmem_limit_bytes=24 * MIB),
        name="cross_kv",
    )(x_first, gains, cross_kv[0])

    corner_src_a, corner_src_b = columns(jnp.concatenate([tile_a, tile_b], axis=0))
    corner_src_a, corner_src_b, pair_out = lax.optimization_barrier(
        (corner_src_a, corner_src_b, pair_out)
    )
    corner_a = lax.ppermute(corner_src_a, "face", swap_a)
    corner_b = lax.ppermute(corner_src_b, "face", swap_b)
    face_a, face_b, corner_a, corner_b, pair_out = lax.optimization_barrier(
        (face_a, face_b, corner_a, corner_b, pair_out)
    )
    partner = lax.ppermute(pair_out, "comp", [(0, 1), (1, 0)])

    padded_rows = (NB + 2) * GROUP
    window, cross_q = pl.pallas_call(
        kernel_window,
        in_specs=[SMEM] + [VMEM] * 10,
        out_specs=[VMEM] * 2,
        out_shape=[array(D, ROWS), array(ROWS, D)],
        scratch_shapes=[
            pltpu.VMEM((padded_rows, D), BF),
            pltpu.VMEM((PAIRS * VROWS, padded_rows), BF),
            pltpu.VMEM((ROWS, D), BF),
            pltpu.VMEM((8, 2 * CELLS), F32),
        ],
        cost_estimate=cost(4 << 30, 7 * MIB, ROWS * HEADS * WINDOW),
        compiler_params=pltpu.CompilerParams(vmem_limit_bytes=28 * MIB),
        name="window",
    )(
        land_bands,
        x,
        face_a.reshape(NB * SIDE, D),
        face_b.reshape(NB * SIDE, D),
        tile_a.reshape(CELLS, D),
        tile_b.reshape(CELLS, D),
        corner_a.reshape(2 * SIDE, D),
        corner_b.reshape(2 * SIDE, D),
        gains,
        qkv_weight[0],
        cross_query[0],
    )

    result = pl.pallas_call(
        kernel_cross,
        in_specs=[SMEM] * 2 + [VMEM] * 9,
        out_specs=VMEM,
        out_shape=array(ROWS, D),
        scratch_shapes=[
            pltpu.VMEM((D, ROWS), BF),
            pltpu.VMEM((PAIRS * VROWS, ROWS), BF),
            pltpu.VMEM((8, 2 * CELLS), F32),
        ],
        cost_estimate=cost(5 << 30, 11 * MIB, ROWS * HEADS * 512),
        compiler_params=pltpu.CompilerParams(vmem_limit_bytes=24 * MIB),
        name="cross",
    )(
        intersection_list.transpose(0, 2, 3, 1).reshape(2, KC, NB),
        land_bands,
        cross_q,
        partner,
        window,
        x,
        gains,
        out_weight[0],
        cross_out[0],
        up_weight[0],
        down_weight[0],
    )
    return result.reshape(1, NB * BR, RX, D)


def solution(mesh):
    placed = (
        P("comp", "tile", "face", None),
        P("comp", None, None),
        P("comp", None, None),
        P("comp", None, None),
        P("comp", None, None),
        P("comp", None, None),
        P("comp", None, None),
        P("comp", None, None),
        P("comp", None, None),
        P(None, "tile", "face", None),
        P(),
    )
    return jax.shard_map(
        per_device,
        mesh=mesh,
        in_specs=placed,
        out_specs=P("comp", "tile", "face", None),
        check_vma=False,
    )
```

```python
import jax
import jax.numpy as jnp
from jax import lax
from jax.experimental import pallas as pl
from jax.experimental.pallas import tpu as pltpu
from jax.sharding import PartitionSpec as P

D = 512
FF = 2048
HEADS = 8
PAIRS = HEADS // 2
LANES = 128
RX = 16
BR = 8
NB = 8
KC = 4
CELLS = BR * RX
ROWS = NB * CELLS
SIDE = BR * BR
GROUP = CELLS + 2 * SIDE
WINDOW = 3 * GROUP
EXTRA = 16
VROWS = LANES + EXTRA

EPSILON = 1e-05
Q_SCALE = 1.4426950408889634 / 8.0
LIMIT = 2.0**100
BF = jnp.bfloat16
F32 = jnp.float32
MIB = 1 << 20


def norm_round(values, gain):
    mean_square = jnp.mean(values * values, axis=-1, keepdims=True)
    return (values * lax.rsqrt(mean_square + EPSILON) * gain.astype(F32)).astype(BF)


def mm(a, b):
    return jnp.dot(a, b, preferred_element_type=F32)


def mm_nt(a, b):
    return lax.dot_general(a, b, (((1,), (1,)), ((), ())), preferred_element_type=F32)


def mm_tn(a, b):
    return lax.dot_general(a, b, (((0,), (0,)), ((), ())), preferred_element_type=F32)


def mm_tt(a, b):
    return lax.dot_general(a, b, (((0,), (1,)), ((), ())), preferred_element_type=F32)


def augment(values_t, flag, out_ref, lane):
    keep = flag.astype(F32).astype(BF)
    for p in range(PAIRS):
        rows = values_t[p * LANES : (p + 1) * LANES]
        out_ref[pl.ds(p * VROWS, LANES), pl.ds(lane, CELLS)] = rows * keep
        out_ref[pl.ds(p * VROWS + LANES, EXTRA), pl.ds(lane, CELLS)] = (
            jnp.ones((EXTRA, CELLS), BF) * keep
        )


def score(pair, keys):
    low = lax.broadcasted_iota(jnp.int32, pair.shape, 1) < LANES // 2
    zero = jnp.zeros_like(pair)
    stacked = jnp.concatenate([jnp.where(low, pair, zero), jnp.where(low, zero, pair)], axis=0)
    return mm_nt(keys, stacked)


def blend(values_t, terms, extra):
    both = mm(values_t, terms)
    sums = both[LANES : LANES + 8]
    share = 1.0 / (sums + extra)
    half = LANES // 2
    result = jnp.concatenate(
        [both[:half, :CELLS] * share[:1, :CELLS], both[half:LANES, CELLS:] * share[:1, CELLS:]],
        axis=0,
    )
    return result.astype(BF), sums


def attention(count, queries, keys, values, penalties, lane, out_ref, bad_ref):
    bad_ref[...] = jnp.zeros_like(bad_ref)

    def terms_of(i, p):
        return jnp.exp2(score(queries(i, p), keys(i, p))).astype(BF)

    steps = [(i, p) for i in range(count) for p in range(PAIRS)]
    following = terms_of(*steps[0])
    for n, (i, p) in enumerate(steps):
        terms = following
        if n + 1 < len(steps):
            following = terms_of(*steps[n + 1])
        result, sums = blend(values(i, p), terms, 1.0)
        out_ref[pl.ds(p * LANES, LANES), pl.ds(lane(i), CELLS)] = result
        bad_ref[...] += jnp.where(sums < LIMIT, 0.0, 1.0)

    @pl.when(jnp.sum(bad_ref[...]) > 0.0)
    def _():
        def band(i, carry):
            for p in range(PAIRS):
                scores = score(queries(i, p), keys(i, p))
                at = 0
                pieces = []
                for rows, penalty in penalties(i):
                    pieces.append(scores[at : at + rows] + penalty)
                    at += rows
                scores = jnp.concatenate(pieces, axis=0)
                highest = jnp.maximum(jnp.max(scores, axis=0, keepdims=True), 0.0)
                terms = jnp.exp2(scores - highest).astype(BF)
                result, _ = blend(values(i, p), terms, jnp.exp2(-highest))
                out_ref[pl.ds(p * LANES, LANES), pl.ds(lane(i), CELLS)] = result
            return carry

        lax.fori_loop(0, count, band, 0)


def aligned(i, size):
    return i * size if isinstance(i, int) else pl.multiple_of(i * size, size)


def kernel_cross_kv(x_ref, gain_ref, weight_ref, out_ref):
    cross_input = norm_round(x_ref[...].astype(F32), gain_ref[1:2, :])
    out_ref[:, :D] = mm(cross_input, weight_ref[:, :D]).astype(BF)
    out_ref[:, D:] = mm_tt(weight_ref[:, D:], cross_input).astype(BF)


def kernel_own(x_ref, gain_ref, qkv_ref, cq_ref, q_ref, k_ref, v_ref, c_ref):
    values = x_ref[...].astype(F32)
    mean_square = jnp.mean(values * values, axis=-1, keepdims=True)
    unit = values * lax.rsqrt(mean_square + EPSILON)
    attn_input = (unit * gain_ref[0:1, :].astype(F32)).astype(BF)
    cross_input = (unit * gain_ref[1:2, :].astype(F32)).astype(BF)
    q_ref[...] = (mm(attn_input, qkv_ref[:, :D]) * Q_SCALE).astype(BF)
    k_ref[...] = mm(attn_input, qkv_ref[:, D : 2 * D]).astype(BF)
    v_ref[...] = mm_tt(qkv_ref[:, 2 * D :], attn_input).astype(BF)
    c_ref[...] = (mm(cross_input, cq_ref[...]) * Q_SCALE).astype(BF)


def kernel_cross(links_ref, land_ref, q_ref, kv_ref, out_ref, va_ref, bad_ref):
    component = lax.axis_index("comp")
    own_land = land_ref[lax.axis_index("tile"), lax.axis_index("face")]
    floor = jnp.where(component == 1, 0, own_land)

    for j in range(NB):
        row, lane = (j // 4) * D, D + (j % 4) * CELLS
        augment(kv_ref[row : row + D, lane : lane + CELLS], j >= floor, va_ref, j * CELLS)

    def picks(i):
        return [links_ref[component, k, i] for k in range(KC)]

    def queries(i, p):
        return q_ref[pl.ds(aligned(i, CELLS), CELLS), pl.ds(p * LANES, LANES)]

    def keys(i, p):
        return jnp.concatenate(
            [kv_ref[pl.ds(aligned(j, CELLS), CELLS), pl.ds(p * LANES, LANES)] for j in picks(i)],
            axis=0,
        )

    def values(i, p):
        return jnp.concatenate(
            [va_ref[pl.ds(p * VROWS, VROWS), pl.ds(aligned(j, CELLS), CELLS)] for j in picks(i)],
            axis=1,
        )

    def penalties(i):
        return [(CELLS, jnp.where(j >= floor, 0.0, -1e30)) for j in picks(i)]

    def lane(i):
        return aligned(i, CELLS)

    attention(NB, queries, keys, values, penalties, lane, out_ref, bad_ref)


def place(land_ref):
    is_air = lax.axis_index("comp") == 0
    tile_row = lax.axis_index("tile")
    tile_col = lax.axis_index("face")
    columns = (tile_col, (tile_col + 7) % 8, (tile_col + 1) % 8)

    def flags(r):
        inside_row = jnp.where(r == 0, tile_row - 1, jnp.where(r == NB + 1, tile_row + 1, tile_row))
        lat_ok = (inside_row >= 0) & (inside_row < 8)
        safe_row = jnp.clip(inside_row, 0, 7)
        index = jnp.where(r == 0, NB - 1, jnp.where(r == NB + 1, 0, r - 1))
        return [lat_ok & (is_air | (index >= land_ref[safe_row, c])) for c in columns]

    return is_air, tile_row % 2 == 1, tile_col % 2 == 1, flags


def sorted_pair(odd, a, b):
    return jnp.where(odd, a, b), jnp.where(odd, b, a)


def project(rows_x, gain_ref, qkv_ref):
    normed = norm_round(rows_x.astype(F32), gain_ref[0:1, :])
    keys = mm(normed, qkv_ref[:, D : 2 * D]).astype(BF)
    return keys, mm_tt(qkv_ref[:, 2 * D :], normed).astype(BF)


def side_flag(flags, r):
    _, west_ok, east_ok = flags(r)
    west_lane = lax.broadcasted_iota(jnp.int32, (1, CELLS), 1) < SIDE
    return jnp.where(west_lane, west_ok.astype(F32), east_ok.astype(F32))


def window_penalties(flags, i):
    pieces = []
    for b in range(3):
        for rows, flag in zip((CELLS, SIDE, SIDE), flags(i + b)):
            pieces.append((rows, jnp.where(flag, 0.0, -1e30)))
    return pieces


def kernel_window(
    land_ref,
    face_a_ref,
    face_b_ref,
    gain_ref,
    qkv_ref,
    q_ref,
    k_ref,
    v_ref,
    win_ref,
    edge_keys_ref,
    edge_va_ref,
    keys_ref,
    va_ref,
    bad_ref,
):
    _, _, odd_col, flags = place(land_ref)

    def put(r, offset, keys, values_t, flag):
        at = (r - 1) * GROUP + offset
        keys_ref[pl.ds(at, CELLS), :] = keys
        augment(values_t, flag, va_ref, at)

    west, east = sorted_pair(odd_col, face_a_ref[...], face_b_ref[...])
    blocks = 2
    for b in range(blocks):
        members = range(1 + b * NB // blocks, 1 + (b + 1) * NB // blocks)
        rows_x = []
        for r in members:
            rows_x += [side[(r - 1) * SIDE : r * SIDE] for side in (west, east)]
        keys, values_t = project(jnp.concatenate(rows_x, axis=0), gain_ref, qkv_ref)
        for n, r in enumerate(members):
            at = slice(n * CELLS, (n + 1) * CELLS)
            put(r, CELLS, keys[at], values_t[:, at], side_flag(flags, r))
    for i in range(NB):
        at = slice(i * CELLS, (i + 1) * CELLS)
        put(i + 1, 0, k_ref[at, :], v_ref[:, at], flags(i + 1)[0])
    for n, at in enumerate((0, (NB - 2) * GROUP)):
        to = slice(n * 2 * GROUP, (n + 1) * 2 * GROUP)
        edge_keys_ref[to, :] = keys_ref[at : at + 2 * GROUP, :]
        edge_va_ref[:, to] = va_ref[:, at : at + 2 * GROUP]

    def queries(n, p):
        return q_ref[pl.ds(aligned(n, CELLS) + CELLS, CELLS), pl.ds(p * LANES, LANES)]

    def keys_of(n, p):
        return keys_ref[pl.ds(aligned(n, GROUP), WINDOW), pl.ds(p * LANES, LANES)]

    def values_of(n, p):
        return va_ref[pl.ds(p * VROWS, VROWS), pl.ds(aligned(n, GROUP), WINDOW)]

    def penalties(n):
        return window_penalties(flags, n + 1)

    def lane(n):
        return aligned(n, CELLS) + CELLS

    attention(NB - 2, queries, keys_of, values_of, penalties, lane, win_ref, bad_ref)


def kernel_last(
    land_ref,
    tile_a_ref,
    tile_b_ref,
    edge_keys_ref,
    edge_va_ref,
    q_ref,
    win_ref,
    cross_ref,
    x_ref,
    gain_ref,
    qkv_ref,
    out_w_ref,
    cross_w_ref,
    up_ref,
    down_ref,
    out_ref,
    keys_ref,
    va_ref,
    full_ref,
    bad_ref,
):
    is_air, odd_row, odd_col, flags = place(land_ref)
    full_ref[:, CELLS : ROWS - CELLS] = win_ref[:, CELLS : ROWS - CELLS]
    rows_x = []
    for rows in sorted_pair(odd_row, tile_a_ref[...], tile_b_ref[...]):
        west, east = sorted_pair(odd_col, rows[CELLS : CELLS + SIDE], rows[CELLS + SIDE :])
        rows_x += [rows[:CELLS], west, east]
    new_keys, new_values = project(jnp.concatenate(rows_x, axis=0), gain_ref, qkv_ref)
    for n in range(2):
        new, held = n * WINDOW + n * 2 * GROUP, n * WINDOW + (1 - n) * GROUP
        src = slice(n * 2 * GROUP, (n + 1) * 2 * GROUP)
        keys_ref[new : new + GROUP, :] = new_keys[n * GROUP : (n + 1) * GROUP]
        keys_ref[held : held + 2 * GROUP, :] = edge_keys_ref[src, :]
        va_ref[:, held : held + 2 * GROUP] = edge_va_ref[:, src]
        r = n * (NB + 1)
        at = n * GROUP
        augment(new_values[:, at : at + CELLS], flags(r)[0], va_ref, new)
        augment(new_values[:, at + CELLS : at + GROUP], side_flag(flags, r), va_ref, new + CELLS)

    def queries(n, p):
        return q_ref[pl.ds(aligned(n, ROWS - CELLS), CELLS), pl.ds(p * LANES, LANES)]

    def keys_of(n, p):
        return keys_ref[pl.ds(aligned(n, WINDOW), WINDOW), pl.ds(p * LANES, LANES)]

    def values_of(n, p):
        return va_ref[pl.ds(p * VROWS, VROWS), pl.ds(aligned(n, WINDOW), WINDOW)]

    def penalties(n):
        return window_penalties(flags, n * (NB - 1))

    def lane(n):
        return aligned(n, ROWS - CELLS)

    attention(2, queries, keys_of, values_of, penalties, lane, full_ref, bad_ref)

    chunk = 512
    own_land = land_ref[lax.axis_index("tile"), lax.axis_index("face")]
    for c in range(ROWS // chunk):
        at = slice(c * chunk, (c + 1) * chunk)
        index = (c * chunk + lax.broadcasted_iota(jnp.int32, (chunk, 1), 0)) // CELLS
        live = jnp.where(is_air | (index >= own_land), 1.0, 0.0)
        update = mm_tn(full_ref[:, at], out_w_ref[...]) + mm_tn(cross_ref[:, at], cross_w_ref[...])
        middle = x_ref[at, :].astype(F32) + live * update
        mlp_input = norm_round(middle, gain_ref[2:3, :])
        gate = 0.5 * mm(mlp_input, up_ref[...])
        hidden = (gate + gate * jnp.tanh(gate)).astype(BF)
        out_ref[at, :] = (middle + live * mm(hidden, down_ref[...])).astype(BF)


VMEM = pl.BlockSpec(memory_space=pltpu.VMEM)
SMEM = pl.BlockSpec(memory_space=pltpu.SMEM)


def array(*shape, dtype=BF):
    return jax.ShapeDtypeStruct(shape, dtype)


def cost(macs, size, exps=0):
    return pl.CostEstimate(flops=2 * macs, bytes_accessed=size, transcendentals=exps)


def per_device(
    tokens,
    norm_gains,
    qkv_weight,
    out_weight,
    cross_query,
    cross_kv,
    cross_out,
    up_weight,
    down_weight,
    intersection_list,
    land_bands,
):
    grid_x = tokens[0]
    x = grid_x.reshape(ROWS, D)
    gains = norm_gains[0]
    swap_a = [(i, i ^ 1) for i in range(8)]
    swap_b = [(i, (i + 1) % 8 if i % 2 else (i - 1) % 8) for i in range(8)]
    odd_row = lax.axis_index("tile") % 2 == 1
    odd_col = lax.axis_index("face") % 2 == 1

    def columns(block):
        low, high = block[:, :BR], block[:, RX - BR :]
        return jnp.where(odd_col, low, high), jnp.where(odd_col, high, low)

    face_src_a, face_src_b, x_first = lax.optimization_barrier((*columns(grid_x), x))
    face_a = lax.ppermute(face_src_a, "face", swap_a).reshape(NB * SIDE, D)
    face_b = lax.ppermute(face_src_b, "face", swap_b).reshape(NB * SIDE, D)

    half = ROWS // 2
    block = pl.BlockSpec((half, D), lambda i: (i, 0))
    params = pltpu.CompilerParams(vmem_limit_bytes=24 * MIB)
    pair_out = pl.pallas_call(
        kernel_cross_kv,
        grid=(2,),
        in_specs=[
            block,
            pl.BlockSpec((3, D), lambda i: (0, 0)),
            pl.BlockSpec((D, 2 * D), lambda i: (0, 0)),
        ],
        out_specs=pl.BlockSpec((half, 2 * D), lambda i: (i, 0)),
        out_shape=array(ROWS, 2 * D),
        cost_estimate=cost(ROWS * D * 2 * D, 4 * MIB),
        compiler_params=params,
        name="cross_kv",
    )(x_first, gains, cross_kv[0])
    partner = lax.ppermute(pair_out, "comp", [(0, 1), (1, 0)])

    q, k, v, cross_q = pl.pallas_call(
        kernel_own,
        grid=(2,),
        in_specs=[
            block,
            pl.BlockSpec((3, D), lambda i: (0, 0)),
            pl.BlockSpec((D, 3 * D), lambda i: (0, 0)),
            pl.BlockSpec((D, D), lambda i: (0, 0)),
        ],
        out_specs=[block, block, pl.BlockSpec((D, half), lambda i: (0, i)), block],
        out_shape=[array(ROWS, D), array(ROWS, D), array(D, ROWS), array(ROWS, D)],
        cost_estimate=cost(ROWS * D * 4 * D, 7 * MIB),
        compiler_params=params,
        name="own",
    )(x_first, gains, qkv_weight[0], cross_query[0])

    bad = pltpu.VMEM((8, 2 * CELLS), F32)
    cross = pl.pallas_call(
        kernel_cross,
        in_specs=[SMEM] * 2 + [VMEM] * 2,
        out_specs=VMEM,
        out_shape=array(D, ROWS),
        scratch_shapes=[pltpu.VMEM((PAIRS * VROWS, ROWS), BF), bad],
        cost_estimate=cost(8 * ROWS * 512 * D, 4 * MIB, ROWS * HEADS * 512),
        compiler_params=params,
        name="cross",
    )(intersection_list.transpose(0, 2, 3, 1).reshape(2, KC, NB), land_bands, cross_q, partner)

    face_a, face_b, cross = lax.optimization_barrier((face_a, face_b, cross))
    top, bottom = [
        jnp.concatenate(
            [x[at * CELLS : (at + 1) * CELLS], *[f[at * SIDE : (at + 1) * SIDE] for f in (face_a, face_b)]],
            axis=0,
        )
        for at in (0, NB - 1)
    ]
    tile_a = lax.ppermute(jnp.where(odd_row, top, bottom), "tile", swap_a)
    tile_b = lax.ppermute(jnp.where(odd_row, bottom, top), "tile", swap_b)

    window, edge_keys, edge_va = pl.pallas_call(
        kernel_window,
        in_specs=[SMEM] + [VMEM] * 7,
        out_specs=[VMEM] * 3,
        out_shape=[array(D, ROWS), array(4 * GROUP, D), array(PAIRS * VROWS, 4 * GROUP)],
        scratch_shapes=[
            pltpu.VMEM((NB * GROUP, D), BF),
            pltpu.VMEM((PAIRS * VROWS, NB * GROUP), BF),
            bad,
        ],
        cost_estimate=cost(4 << 30, 7 * MIB, ROWS * HEADS * WINDOW),
        compiler_params=params,
        name="window",
    )(land_bands, face_a, face_b, gains, qkv_weight[0], q, k, v)

    result = pl.pallas_call(
        kernel_last,
        in_specs=[SMEM] + [VMEM] * 14,
        out_specs=VMEM,
        out_shape=array(ROWS, D),
        scratch_shapes=[
            pltpu.VMEM((2 * WINDOW, D), BF),
            pltpu.VMEM((PAIRS * VROWS, 2 * WINDOW), BF),
            pltpu.VMEM((D, ROWS), BF),
            bad,
        ],
        cost_estimate=cost(5 << 30, 11 * MIB, ROWS * HEADS * 512),
        compiler_params=pltpu.CompilerParams(vmem_limit_bytes=28 * MIB),
        name="last",
    )(
        land_bands,
        tile_a,
        tile_b,
        edge_keys,
        edge_va,
        q,
        window,
        cross,
        x,
        gains,
        qkv_weight[0],
        out_weight[0],
        cross_out[0],
        up_weight[0],
        down_weight[0],
    )
    return result.reshape(1, NB * BR, RX, D)


def solution(mesh):
    placed = (
        P("comp", "tile", "face", None),
        P("comp", None, None),
        P("comp", None, None),
        P("comp", None, None),
        P("comp", None, None),
        P("comp", None, None),
        P("comp", None, None),
        P("comp", None, None),
        P("comp", None, None),
        P(None, "tile", "face", None),
        P(),
    )
    return jax.shard_map(
        per_device,
        mesh=mesh,
        in_specs=placed,
        out_specs=P("comp", "tile", "face", None),
        check_vma=False,
    )
```

```python
import jax
import jax.numpy as jnp
from jax import lax
from jax.experimental import pallas as pl
from jax.experimental.pallas import tpu as pltpu
from jax.sharding import PartitionSpec as P

D = 512
FF = 2048
HEADS = 8
PAIRS = HEADS // 2
LANES = 128
RX = 16
BR = 8
NB = 8
KC = 4
CELLS = BR * RX
ROWS = NB * CELLS
SIDE = BR * BR
GROUP = CELLS + 2 * SIDE
WINDOW = 3 * GROUP
EXTRA = 16
VROWS = LANES + EXTRA

EPSILON = 1e-05
Q_SCALE = 1.4426950408889634 / 8.0
LIMIT = 2.0**100
BF = jnp.bfloat16
F32 = jnp.float32
MIB = 1 << 20


def norm_round(values, gain):
    mean_square = jnp.mean(values * values, axis=-1, keepdims=True)
    return (values * lax.rsqrt(mean_square + EPSILON) * gain.astype(F32)).astype(BF)


def mm(a, b):
    return jnp.dot(a, b, preferred_element_type=F32)


def mm_nt(a, b):
    return lax.dot_general(a, b, (((1,), (1,)), ((), ())), preferred_element_type=F32)


def mm_tn(a, b):
    return lax.dot_general(a, b, (((0,), (0,)), ((), ())), preferred_element_type=F32)


def mm_tt(a, b):
    return lax.dot_general(a, b, (((0,), (1,)), ((), ())), preferred_element_type=F32)


def augment(values_t, flag, out_ref, lane):
    keep = flag.astype(F32).astype(BF)
    for p in range(PAIRS):
        rows = values_t[p * LANES : (p + 1) * LANES]
        out_ref[pl.ds(p * VROWS, LANES), pl.ds(lane, CELLS)] = rows * keep
        out_ref[pl.ds(p * VROWS + LANES, EXTRA), pl.ds(lane, CELLS)] = (
            jnp.ones((EXTRA, CELLS), BF) * keep
        )


def score(pair, keys):
    low = lax.broadcasted_iota(jnp.int32, pair.shape, 1) < LANES // 2
    zero = jnp.zeros_like(pair)
    stacked = jnp.concatenate([jnp.where(low, pair, zero), jnp.where(low, zero, pair)], axis=0)
    return mm_nt(keys, stacked)


def blend(values_t, terms, extra):
    both = mm(values_t, terms)
    sums = both[LANES : LANES + 8]
    share = 1.0 / (sums + extra)
    half = LANES // 2
    result = jnp.concatenate(
        [both[:half, :CELLS] * share[:1, :CELLS], both[half:LANES, CELLS:] * share[:1, CELLS:]],
        axis=0,
    )
    return result.astype(BF), sums


def attention(count, queries, keys, values, penalties, lane, out_ref, bad_ref):
    bad_ref[...] = jnp.zeros_like(bad_ref)

    def terms_of(i, p):
        return jnp.exp2(score(queries(i, p), keys(i, p))).astype(BF)

    steps = [(i, p) for i in range(count) for p in range(PAIRS)]
    following = terms_of(*steps[0])
    for n, (i, p) in enumerate(steps):
        terms = following
        if n + 1 < len(steps):
            following = terms_of(*steps[n + 1])
        result, sums = blend(values(i, p), terms, 1.0)
        out_ref[pl.ds(p * LANES, LANES), pl.ds(lane(i), CELLS)] = result
        bad_ref[...] += jnp.where(sums < LIMIT, 0.0, 1.0)

    @pl.when(jnp.sum(bad_ref[...]) > 0.0)
    def _():
        def band(i, carry):
            for p in range(PAIRS):
                scores = score(queries(i, p), keys(i, p))
                at = 0
                pieces = []
                for rows, penalty in penalties(i):
                    pieces.append(scores[at : at + rows] + penalty)
                    at += rows
                scores = jnp.concatenate(pieces, axis=0)
                highest = jnp.maximum(jnp.max(scores, axis=0, keepdims=True), 0.0)
                terms = jnp.exp2(scores - highest).astype(BF)
                result, _ = blend(values(i, p), terms, jnp.exp2(-highest))
                out_ref[pl.ds(p * LANES, LANES), pl.ds(lane(i), CELLS)] = result
            return carry

        lax.fori_loop(0, count, band, 0)


def aligned(i, size):
    return i * size if isinstance(i, int) else pl.multiple_of(i * size, size)


def kernel_cross_kv(x_ref, gain_ref, weight_ref, out_ref):
    cross_input = norm_round(x_ref[...].astype(F32), gain_ref[1:2, :])
    out_ref[:, :D] = mm(cross_input, weight_ref[:, :D]).astype(BF)
    out_ref[:, D:] = mm_tt(weight_ref[:, D:], cross_input).astype(BF)


def kernel_own(x_ref, gain_ref, qkv_ref, cq_ref, q_ref, k_ref, v_ref, c_ref):
    values = x_ref[...].astype(F32)
    mean_square = jnp.mean(values * values, axis=-1, keepdims=True)
    unit = values * lax.rsqrt(mean_square + EPSILON)
    attn_input = (unit * gain_ref[0:1, :].astype(F32)).astype(BF)
    cross_input = (unit * gain_ref[1:2, :].astype(F32)).astype(BF)
    q_ref[...] = (mm(attn_input, qkv_ref[:, :D]) * Q_SCALE).astype(BF)
    k_ref[...] = mm(attn_input, qkv_ref[:, D : 2 * D]).astype(BF)
    v_ref[...] = mm_tt(qkv_ref[:, 2 * D :], attn_input).astype(BF)
    c_ref[...] = (mm(cross_input, cq_ref[...]) * Q_SCALE).astype(BF)


def kernel_cross(links_ref, land_ref, q_ref, kv_ref, out_ref, va_ref, bad_ref):
    component = lax.axis_index("comp")
    own_land = land_ref[lax.axis_index("tile"), lax.axis_index("face")]
    floor = jnp.where(component == 1, 0, own_land)

    for j in range(NB):
        row, lane = (j // 4) * D, D + (j % 4) * CELLS
        augment(kv_ref[row : row + D, lane : lane + CELLS], j >= floor, va_ref, j * CELLS)

    def picks(i):
        return [links_ref[component, k, i] for k in range(KC)]

    def queries(i, p):
        return q_ref[pl.ds(aligned(i, CELLS), CELLS), pl.ds(p * LANES, LANES)]

    def keys(i, p):
        return jnp.concatenate(
            [kv_ref[pl.ds(aligned(j, CELLS), CELLS), pl.ds(p * LANES, LANES)] for j in picks(i)],
            axis=0,
        )

    def values(i, p):
        return jnp.concatenate(
            [va_ref[pl.ds(p * VROWS, VROWS), pl.ds(aligned(j, CELLS), CELLS)] for j in picks(i)],
            axis=1,
        )

    def penalties(i):
        return [(CELLS, jnp.where(j >= floor, 0.0, -1e30)) for j in picks(i)]

    def lane(i):
        return aligned(i, CELLS)

    attention(NB, queries, keys, values, penalties, lane, out_ref, bad_ref)


def place(land_ref):
    is_air = lax.axis_index("comp") == 0
    tile_row = lax.axis_index("tile")
    tile_col = lax.axis_index("face")
    columns = (tile_col, (tile_col + 7) % 8, (tile_col + 1) % 8)

    def flags(r):
        inside_row = jnp.where(r == 0, tile_row - 1, jnp.where(r == NB + 1, tile_row + 1, tile_row))
        lat_ok = (inside_row >= 0) & (inside_row < 8)
        safe_row = jnp.clip(inside_row, 0, 7)
        index = jnp.where(r == 0, NB - 1, jnp.where(r == NB + 1, 0, r - 1))
        return [lat_ok & (is_air | (index >= land_ref[safe_row, c])) for c in columns]

    return is_air, flags


def project(rows_x, gain_ref, qkv_ref):
    normed = norm_round(rows_x.astype(F32), gain_ref[0:1, :])
    keys = mm(normed, qkv_ref[:, D : 2 * D]).astype(BF)
    return keys, mm_tt(qkv_ref[:, 2 * D :], normed).astype(BF)


def side_flag(flags, r):
    _, west_ok, east_ok = flags(r)
    west_lane = lax.broadcasted_iota(jnp.int32, (1, CELLS), 1) < SIDE
    return jnp.where(west_lane, west_ok.astype(F32), east_ok.astype(F32))


def window_penalties(flags, i):
    pieces = []
    for b in range(3):
        for rows, flag in zip((CELLS, SIDE, SIDE), flags(i + b)):
            pieces.append((rows, jnp.where(flag, 0.0, -1e30)))
    return pieces


def kernel_window(
    land_ref,
    west_ref,
    east_ref,
    gain_ref,
    qkv_ref,
    q_ref,
    k_ref,
    v_ref,
    win_ref,
    edge_keys_ref,
    edge_va_ref,
    keys_ref,
    va_ref,
    bad_ref,
):
    _, flags = place(land_ref)

    def put(r, offset, keys, values_t, flag):
        at = (r - 1) * GROUP + offset
        keys_ref[pl.ds(at, CELLS), :] = keys
        augment(values_t, flag, va_ref, at)

    blocks = 2
    for b in range(blocks):
        members = range(1 + b * NB // blocks, 1 + (b + 1) * NB // blocks)
        rows_x = []
        for r in members:
            rows_x += [ref[(r - 1) * SIDE : r * SIDE, :] for ref in (west_ref, east_ref)]
        keys, values_t = project(jnp.concatenate(rows_x, axis=0), gain_ref, qkv_ref)
        for n, r in enumerate(members):
            at = slice(n * CELLS, (n + 1) * CELLS)
            put(r, CELLS, keys[at], values_t[:, at], side_flag(flags, r))
    for i in range(NB):
        at = slice(i * CELLS, (i + 1) * CELLS)
        put(i + 1, 0, k_ref[at, :], v_ref[:, at], flags(i + 1)[0])
    for n, at in enumerate((0, (NB - 2) * GROUP)):
        to = slice(n * 2 * GROUP, (n + 1) * 2 * GROUP)
        edge_keys_ref[to, :] = keys_ref[at : at + 2 * GROUP, :]
        edge_va_ref[:, to] = va_ref[:, at : at + 2 * GROUP]

    def queries(n, p):
        return q_ref[pl.ds(aligned(n, CELLS) + CELLS, CELLS), pl.ds(p * LANES, LANES)]

    def keys_of(n, p):
        return keys_ref[pl.ds(aligned(n, GROUP), WINDOW), pl.ds(p * LANES, LANES)]

    def values_of(n, p):
        return va_ref[pl.ds(p * VROWS, VROWS), pl.ds(aligned(n, GROUP), WINDOW)]

    def penalties(n):
        return window_penalties(flags, n + 1)

    def lane(n):
        return aligned(n, CELLS) + CELLS

    attention(NB - 2, queries, keys_of, values_of, penalties, lane, win_ref, bad_ref)


def kernel_last(
    land_ref,
    north_ref,
    south_ref,
    edge_keys_ref,
    edge_va_ref,
    q_ref,
    win_ref,
    cross_ref,
    x_ref,
    gain_ref,
    qkv_ref,
    out_w_ref,
    cross_w_ref,
    up_ref,
    down_ref,
    out_ref,
    keys_ref,
    va_ref,
    full_ref,
    bad_ref,
):
    is_air, flags = place(land_ref)
    full_ref[:, CELLS : ROWS - CELLS] = win_ref[:, CELLS : ROWS - CELLS]
    rows_x = jnp.concatenate([north_ref[...], south_ref[...]], axis=0)
    new_keys, new_values = project(rows_x, gain_ref, qkv_ref)
    for n in range(2):
        new, held = n * WINDOW + n * 2 * GROUP, n * WINDOW + (1 - n) * GROUP
        src = slice(n * 2 * GROUP, (n + 1) * 2 * GROUP)
        keys_ref[new : new + GROUP, :] = new_keys[n * GROUP : (n + 1) * GROUP]
        keys_ref[held : held + 2 * GROUP, :] = edge_keys_ref[src, :]
        va_ref[:, held : held + 2 * GROUP] = edge_va_ref[:, src]
        r = n * (NB + 1)
        at = n * GROUP
        augment(new_values[:, at : at + CELLS], flags(r)[0], va_ref, new)
        augment(new_values[:, at + CELLS : at + GROUP], side_flag(flags, r), va_ref, new + CELLS)

    def queries(n, p):
        return q_ref[pl.ds(aligned(n, ROWS - CELLS), CELLS), pl.ds(p * LANES, LANES)]

    def keys_of(n, p):
        return keys_ref[pl.ds(aligned(n, WINDOW), WINDOW), pl.ds(p * LANES, LANES)]

    def values_of(n, p):
        return va_ref[pl.ds(p * VROWS, VROWS), pl.ds(aligned(n, WINDOW), WINDOW)]

    def penalties(n):
        return window_penalties(flags, n * (NB - 1))

    def lane(n):
        return aligned(n, ROWS - CELLS)

    attention(2, queries, keys_of, values_of, penalties, lane, full_ref, bad_ref)

    chunk = 512
    own_land = land_ref[lax.axis_index("tile"), lax.axis_index("face")]
    for c in range(ROWS // chunk):
        at = slice(c * chunk, (c + 1) * chunk)
        index = (c * chunk + lax.broadcasted_iota(jnp.int32, (chunk, 1), 0)) // CELLS
        live = jnp.where(is_air | (index >= own_land), 1.0, 0.0)
        update = mm_tn(full_ref[:, at], out_w_ref[...]) + mm_tn(cross_ref[:, at], cross_w_ref[...])
        middle = x_ref[at, :].astype(F32) + live * update
        mlp_input = norm_round(middle, gain_ref[2:3, :])
        gate = 0.5 * mm(mlp_input, up_ref[...])
        hidden = (gate + gate * jnp.tanh(gate)).astype(BF)
        out_ref[at, :] = (middle + live * mm(hidden, down_ref[...])).astype(BF)


VMEM = pl.BlockSpec(memory_space=pltpu.VMEM)
SMEM = pl.BlockSpec(memory_space=pltpu.SMEM)


def array(*shape, dtype=BF):
    return jax.ShapeDtypeStruct(shape, dtype)


def cost(macs, size, exps=0):
    return pl.CostEstimate(flops=2 * macs, bytes_accessed=size, transcendentals=exps)


def per_device(
    tokens,
    norm_gains,
    qkv_weight,
    out_weight,
    cross_query,
    cross_kv,
    cross_out,
    up_weight,
    down_weight,
    intersection_list,
    land_bands,
):
    grid_x = tokens[0]
    x = grid_x.reshape(ROWS, D)
    gains = norm_gains[0]
    forward = [(i, (i + 1) % 8) for i in range(8)]
    backward = [((i + 1) % 8, i) for i in range(8)]
    east_edge, west_edge, x_first = lax.optimization_barrier(
        (grid_x[:, RX - BR :], grid_x[:, :BR], x)
    )
    west = lax.ppermute(east_edge, "face", forward).reshape(NB * SIDE, D)
    east = lax.ppermute(west_edge, "face", backward).reshape(NB * SIDE, D)

    half = ROWS // 2
    block = pl.BlockSpec((half, D), lambda i: (i, 0))
    params = pltpu.CompilerParams(vmem_limit_bytes=24 * MIB)
    pair_out = pl.pallas_call(
        kernel_cross_kv,
        grid=(2,),
        in_specs=[
            block,
            pl.BlockSpec((3, D), lambda i: (0, 0)),
            pl.BlockSpec((D, 2 * D), lambda i: (0, 0)),
        ],
        out_specs=pl.BlockSpec((half, 2 * D), lambda i: (i, 0)),
        out_shape=array(ROWS, 2 * D),
        cost_estimate=cost(ROWS * D * 2 * D, 4 * MIB),
        compiler_params=params,
        name="cross_kv",
    )(x_first, gains, cross_kv[0])
    partner = lax.ppermute(pair_out, "comp", [(0, 1), (1, 0)])

    q, k, v, cross_q = pl.pallas_call(
        kernel_own,
        grid=(2,),
        in_specs=[
            block,
            pl.BlockSpec((3, D), lambda i: (0, 0)),
            pl.BlockSpec((D, 3 * D), lambda i: (0, 0)),
            pl.BlockSpec((D, D), lambda i: (0, 0)),
        ],
        out_specs=[block, block, pl.BlockSpec((D, half), lambda i: (0, i)), block],
        out_shape=[array(ROWS, D), array(ROWS, D), array(D, ROWS), array(ROWS, D)],
        cost_estimate=cost(ROWS * D * 4 * D, 7 * MIB),
        compiler_params=params,
        name="own",
    )(x_first, gains, qkv_weight[0], cross_query[0])

    bad = pltpu.VMEM((8, 2 * CELLS), F32)
    cross = pl.pallas_call(
        kernel_cross,
        in_specs=[SMEM] * 2 + [VMEM] * 2,
        out_specs=VMEM,
        out_shape=array(D, ROWS),
        scratch_shapes=[pltpu.VMEM((PAIRS * VROWS, ROWS), BF), bad],
        cost_estimate=cost(8 * ROWS * 512 * D, 4 * MIB, ROWS * HEADS * 512),
        compiler_params=params,
        name="cross",
    )(intersection_list.transpose(0, 2, 3, 1).reshape(2, KC, NB), land_bands, cross_q, partner)

    west, east, cross = lax.optimization_barrier((west, east, cross))
    top, bottom = [
        jnp.concatenate(
            [x[at * CELLS : (at + 1) * CELLS], *[side[at * SIDE : (at + 1) * SIDE] for side in (west, east)]],
            axis=0,
        )
        for at in (0, NB - 1)
    ]
    north = lax.ppermute(bottom, "tile", forward)
    south = lax.ppermute(top, "tile", backward)

    window, edge_keys, edge_va = pl.pallas_call(
        kernel_window,
        in_specs=[SMEM] + [VMEM] * 7,
        out_specs=[VMEM] * 3,
        out_shape=[array(D, ROWS), array(4 * GROUP, D), array(PAIRS * VROWS, 4 * GROUP)],
        scratch_shapes=[
            pltpu.VMEM((NB * GROUP, D), BF),
            pltpu.VMEM((PAIRS * VROWS, NB * GROUP), BF),
            bad,
        ],
        cost_estimate=cost(4 << 30, 7 * MIB, ROWS * HEADS * WINDOW),
        compiler_params=params,
        name="window",
    )(land_bands, west, east, gains, qkv_weight[0], q, k, v)

    result = pl.pallas_call(
        kernel_last,
        in_specs=[SMEM] + [VMEM] * 14,
        out_specs=VMEM,
        out_shape=array(ROWS, D),
        scratch_shapes=[
            pltpu.VMEM((2 * WINDOW, D), BF),
            pltpu.VMEM((PAIRS * VROWS, 2 * WINDOW), BF),
            pltpu.VMEM((D, ROWS), BF),
            bad,
        ],
        cost_estimate=cost(5 << 30, 11 * MIB, ROWS * HEADS * 512),
        compiler_params=pltpu.CompilerParams(vmem_limit_bytes=28 * MIB),
        name="last",
    )(
        land_bands,
        north,
        south,
        edge_keys,
        edge_va,
        q,
        window,
        cross,
        x,
        gains,
        qkv_weight[0],
        out_weight[0],
        cross_out[0],
        up_weight[0],
        down_weight[0],
    )
    return result.reshape(1, NB * BR, RX, D)


def solution(mesh):
    placed = (
        P("comp", "tile", "face", None),
        P("comp", None, None),
        P("comp", None, None),
        P("comp", None, None),
        P("comp", None, None),
        P("comp", None, None),
        P("comp", None, None),
        P("comp", None, None),
        P("comp", None, None),
        P(None, "tile", "face", None),
        P(),
    )
    return jax.shard_map(
        per_device,
        mesh=mesh,
        in_specs=placed,
        out_specs=P("comp", "tile", "face", None),
        check_vma=False,
    )
```

```python
import jax
import jax.numpy as jnp
from jax import lax
from jax.experimental import pallas as pl
from jax.experimental.pallas import tpu as pltpu
from jax.sharding import PartitionSpec as P

D = 512
FF = 2048
HEADS = 8
PAIRS = HEADS // 2
LANES = 128
RX = 16
BR = 8
NB = 8
KC = 4
CELLS = BR * RX
ROWS = NB * CELLS
SIDE = BR * BR
GROUP = CELLS + 2 * SIDE
WINDOW = 3 * GROUP
EXTRA = 16
VROWS = LANES + EXTRA

EPSILON = 1e-05
Q_SCALE = 1.4426950408889634 / 8.0
LIMIT = 2.0**100
BF = jnp.bfloat16
F32 = jnp.float32
MIB = 1 << 20


def norm_round(values, gain):
    mean_square = jnp.mean(values * values, axis=-1, keepdims=True)
    return (values * lax.rsqrt(mean_square + EPSILON) * gain.astype(F32)).astype(BF)


def mm(a, b):
    return jnp.dot(a, b, preferred_element_type=F32)


def mm_nt(a, b):
    return lax.dot_general(a, b, (((1,), (1,)), ((), ())), preferred_element_type=F32)


def mm_tn(a, b):
    return lax.dot_general(a, b, (((0,), (0,)), ((), ())), preferred_element_type=F32)


def mm_tt(a, b):
    return lax.dot_general(a, b, (((0,), (1,)), ((), ())), preferred_element_type=F32)


def augment(values_t, flag, out_ref, lane):
    keep = flag.astype(F32).astype(BF)
    for p in range(PAIRS):
        rows = values_t[p * LANES : (p + 1) * LANES]
        out_ref[pl.ds(p * VROWS, LANES), pl.ds(lane, CELLS)] = rows * keep
        out_ref[pl.ds(p * VROWS + LANES, EXTRA), pl.ds(lane, CELLS)] = (
            jnp.ones((EXTRA, CELLS), BF) * keep
        )


def score(pair, keys):
    low = lax.broadcasted_iota(jnp.int32, pair.shape, 1) < LANES // 2
    zero = jnp.zeros_like(pair)
    stacked = jnp.concatenate([jnp.where(low, pair, zero), jnp.where(low, zero, pair)], axis=0)
    return mm_nt(keys, stacked)


def blend(values_t, terms, extra):
    both = mm(values_t, terms)
    sums = both[LANES : LANES + 8]
    share = 1.0 / (sums + extra)
    half = LANES // 2
    result = jnp.concatenate(
        [both[:half, :CELLS] * share[:1, :CELLS], both[half:LANES, CELLS:] * share[:1, CELLS:]],
        axis=0,
    )
    return result.astype(BF), sums


def attention(count, queries, keys, values, penalties, lane, out_ref, bad_ref):
    bad_ref[...] = jnp.zeros_like(bad_ref)

    def terms_of(i, p):
        return jnp.exp2(score(queries(i, p), keys(i, p))).astype(BF)

    steps = [(i, p) for i in range(count) for p in range(PAIRS)]
    following = terms_of(*steps[0])
    for n, (i, p) in enumerate(steps):
        terms = following
        if n + 1 < len(steps):
            following = terms_of(*steps[n + 1])
        result, sums = blend(values(i, p), terms, 1.0)
        out_ref[pl.ds(p * LANES, LANES), pl.ds(lane(i), CELLS)] = result
        bad_ref[...] += jnp.where(sums < LIMIT, 0.0, 1.0)

    @pl.when(jnp.sum(bad_ref[...]) > 0.0)
    def _():
        def band(i, carry):
            for p in range(PAIRS):
                scores = score(queries(i, p), keys(i, p))
                at = 0
                pieces = []
                for rows, penalty in penalties(i):
                    pieces.append(scores[at : at + rows] + penalty)
                    at += rows
                scores = jnp.concatenate(pieces, axis=0)
                highest = jnp.maximum(jnp.max(scores, axis=0, keepdims=True), 0.0)
                terms = jnp.exp2(scores - highest).astype(BF)
                result, _ = blend(values(i, p), terms, jnp.exp2(-highest))
                out_ref[pl.ds(p * LANES, LANES), pl.ds(lane(i), CELLS)] = result
            return carry

        lax.fori_loop(0, count, band, 0)


def aligned(i, size):
    return i * size if isinstance(i, int) else pl.multiple_of(i * size, size)


def kernel_cross_kv(x_ref, gain_ref, weight_ref, out_ref):
    cross_input = norm_round(x_ref[...].astype(F32), gain_ref[1:2, :])
    out_ref[:, :D] = mm(cross_input, weight_ref[:, :D]).astype(BF)
    out_ref[:, D:] = mm_tt(weight_ref[:, D:], cross_input).astype(BF)


def kernel_own(x_ref, gain_ref, qkv_ref, cq_ref, q_ref, k_ref, v_ref, c_ref):
    values = x_ref[...].astype(F32)
    mean_square = jnp.mean(values * values, axis=-1, keepdims=True)
    unit = values * lax.rsqrt(mean_square + EPSILON)
    attn_input = (unit * gain_ref[0:1, :].astype(F32)).astype(BF)
    cross_input = (unit * gain_ref[1:2, :].astype(F32)).astype(BF)
    q_ref[...] = (mm(attn_input, qkv_ref[:, :D]) * Q_SCALE).astype(BF)
    k_ref[...] = mm(attn_input, qkv_ref[:, D : 2 * D]).astype(BF)
    v_ref[...] = mm_tt(qkv_ref[:, 2 * D :], attn_input).astype(BF)
    c_ref[...] = (mm(cross_input, cq_ref[...]) * Q_SCALE).astype(BF)


def kernel_cross(links_ref, land_ref, q_ref, kv_ref, cross_w_ref, out_ref, va_ref, cross_ref, bad_ref):
    component = lax.axis_index("comp")
    own_land = land_ref[lax.axis_index("tile"), lax.axis_index("face")]
    floor = jnp.where(component == 1, 0, own_land)

    for j in range(NB):
        row, lane = (j // 4) * D, D + (j % 4) * CELLS
        augment(kv_ref[row : row + D, lane : lane + CELLS], j >= floor, va_ref, j * CELLS)

    def picks(i):
        return [links_ref[component, k, i] for k in range(KC)]

    def queries(i, p):
        return q_ref[pl.ds(aligned(i, CELLS), CELLS), pl.ds(p * LANES, LANES)]

    def keys(i, p):
        return jnp.concatenate(
            [kv_ref[pl.ds(aligned(j, CELLS), CELLS), pl.ds(p * LANES, LANES)] for j in picks(i)],
            axis=0,
        )

    def values(i, p):
        return jnp.concatenate(
            [va_ref[pl.ds(p * VROWS, VROWS), pl.ds(aligned(j, CELLS), CELLS)] for j in picks(i)],
            axis=1,
        )

    def penalties(i):
        return [(CELLS, jnp.where(j >= floor, 0.0, -1e30)) for j in picks(i)]

    def lane(i):
        return aligned(i, CELLS)

    attention(NB, queries, keys, values, penalties, lane, cross_ref, bad_ref)
    out_ref[...] = mm_tn(cross_ref[...], cross_w_ref[...])


def place(land_ref):
    is_air = lax.axis_index("comp") == 0
    tile_row = lax.axis_index("tile")
    tile_col = lax.axis_index("face")
    columns = (tile_col, (tile_col + 7) % 8, (tile_col + 1) % 8)

    def flags(r):
        inside_row = jnp.where(r == 0, tile_row - 1, jnp.where(r == NB + 1, tile_row + 1, tile_row))
        lat_ok = (inside_row >= 0) & (inside_row < 8)
        safe_row = jnp.clip(inside_row, 0, 7)
        index = jnp.where(r == 0, NB - 1, jnp.where(r == NB + 1, 0, r - 1))
        return [lat_ok & (is_air | (index >= land_ref[safe_row, c])) for c in columns]

    return is_air, flags


def project(rows_x, gain_ref, qkv_ref):
    normed = norm_round(rows_x.astype(F32), gain_ref[0:1, :])
    keys = mm(normed, qkv_ref[:, D : 2 * D]).astype(BF)
    return keys, mm_tt(qkv_ref[:, 2 * D :], normed).astype(BF)


def side_flag(flags, r):
    _, west_ok, east_ok = flags(r)
    west_lane = lax.broadcasted_iota(jnp.int32, (1, CELLS), 1) < SIDE
    return jnp.where(west_lane, west_ok.astype(F32), east_ok.astype(F32))


def window_penalties(flags, i):
    pieces = []
    for b in range(3):
        for rows, flag in zip((CELLS, SIDE, SIDE), flags(i + b)):
            pieces.append((rows, jnp.where(flag, 0.0, -1e30)))
    return pieces


def finish(index, own_land, is_air, win_t, update, x_rows, gain_ref, out_w_ref, up_ref, down_ref):
    live = jnp.where(is_air | (index >= own_land), 1.0, 0.0)
    middle = x_rows.astype(F32) + live * (mm_tn(win_t, out_w_ref[...]) + update)
    mlp_input = norm_round(middle, gain_ref[2:3, :])
    gate = 0.5 * mm(mlp_input, up_ref[...])
    hidden = (gate + gate * jnp.tanh(gate)).astype(BF)
    return (middle + live * mm(hidden, down_ref[...])).astype(BF)


def kernel_window(
    land_ref,
    west_ref,
    east_ref,
    gain_ref,
    qkv_ref,
    q_ref,
    k_ref,
    v_ref,
    update_ref,
    x_ref,
    out_w_ref,
    up_ref,
    down_ref,
    out_ref,
    edge_keys_ref,
    edge_va_ref,
    keys_ref,
    va_ref,
    win_ref,
    bad_ref,
):
    is_air, flags = place(land_ref)

    def put(r, offset, keys, values_t, flag):
        at = (r - 1) * GROUP + offset
        keys_ref[pl.ds(at, CELLS), :] = keys
        augment(values_t, flag, va_ref, at)

    blocks = 2
    for b in range(blocks):
        members = range(1 + b * NB // blocks, 1 + (b + 1) * NB // blocks)
        rows_x = []
        for r in members:
            rows_x += [ref[(r - 1) * SIDE : r * SIDE, :] for ref in (west_ref, east_ref)]
        keys, values_t = project(jnp.concatenate(rows_x, axis=0), gain_ref, qkv_ref)
        for n, r in enumerate(members):
            at = slice(n * CELLS, (n + 1) * CELLS)
            put(r, CELLS, keys[at], values_t[:, at], side_flag(flags, r))
    for i in range(NB):
        at = slice(i * CELLS, (i + 1) * CELLS)
        put(i + 1, 0, k_ref[at, :], v_ref[:, at], flags(i + 1)[0])
    for n, at in enumerate((0, (NB - 2) * GROUP)):
        to = slice(n * 2 * GROUP, (n + 1) * 2 * GROUP)
        edge_keys_ref[to, :] = keys_ref[at : at + 2 * GROUP, :]
        edge_va_ref[:, to] = va_ref[:, at : at + 2 * GROUP]

    def queries(n, p):
        return q_ref[pl.ds(aligned(n, CELLS) + CELLS, CELLS), pl.ds(p * LANES, LANES)]

    def keys_of(n, p):
        return keys_ref[pl.ds(aligned(n, GROUP), WINDOW), pl.ds(p * LANES, LANES)]

    def values_of(n, p):
        return va_ref[pl.ds(p * VROWS, VROWS), pl.ds(aligned(n, GROUP), WINDOW)]

    def penalties(n):
        return window_penalties(flags, n + 1)

    def lane(n):
        return aligned(n, CELLS) + CELLS

    attention(NB - 2, queries, keys_of, values_of, penalties, lane, win_ref, bad_ref)

    own_land = land_ref[lax.axis_index("tile"), lax.axis_index("face")]
    chunk = (NB - 2) * CELLS // 2
    for c in range(2):
        start = CELLS + c * chunk
        at = slice(start, start + chunk)
        index = (start + lax.broadcasted_iota(jnp.int32, (chunk, 1), 0)) // CELLS
        out_ref[at, :] = finish(
            index,
            own_land,
            is_air,
            win_ref[:, at],
            update_ref[at, :],
            x_ref[at, :],
            gain_ref,
            out_w_ref,
            up_ref,
            down_ref,
        )


def kernel_last(
    land_ref,
    north_ref,
    south_ref,
    edge_keys_ref,
    edge_va_ref,
    q_ref,
    update_ref,
    x_ref,
    gain_ref,
    qkv_ref,
    out_w_ref,
    up_ref,
    down_ref,
    held_hbm,
    out_hbm,
    keys_ref,
    va_ref,
    win_ref,
    rows_ref,
    bad_ref,
    sem,
):
    del held_hbm
    is_air, flags = place(land_ref)
    rows_x = jnp.concatenate([north_ref[...], south_ref[...]], axis=0)
    new_keys, new_values = project(rows_x, gain_ref, qkv_ref)
    for n in range(2):
        new, held = n * WINDOW + n * 2 * GROUP, n * WINDOW + (1 - n) * GROUP
        src = slice(n * 2 * GROUP, (n + 1) * 2 * GROUP)
        keys_ref[new : new + GROUP, :] = new_keys[n * GROUP : (n + 1) * GROUP]
        keys_ref[held : held + 2 * GROUP, :] = edge_keys_ref[src, :]
        va_ref[:, held : held + 2 * GROUP] = edge_va_ref[:, src]
        r = n * (NB + 1)
        at = n * GROUP
        augment(new_values[:, at : at + CELLS], flags(r)[0], va_ref, new)
        augment(new_values[:, at + CELLS : at + GROUP], side_flag(flags, r), va_ref, new + CELLS)

    def queries(n, p):
        return q_ref[pl.ds(aligned(n, ROWS - CELLS), CELLS), pl.ds(p * LANES, LANES)]

    def keys_of(n, p):
        return keys_ref[pl.ds(aligned(n, WINDOW), WINDOW), pl.ds(p * LANES, LANES)]

    def values_of(n, p):
        return va_ref[pl.ds(p * VROWS, VROWS), pl.ds(aligned(n, WINDOW), WINDOW)]

    def penalties(n):
        return window_penalties(flags, n * (NB - 1))

    def lane(n):
        return aligned(n, CELLS)

    attention(2, queries, keys_of, values_of, penalties, lane, win_ref, bad_ref)

    def edge_rows(ref):
        return jnp.concatenate([ref[:CELLS, :], ref[ROWS - CELLS :, :]], axis=0)

    own_land = land_ref[lax.axis_index("tile"), lax.axis_index("face")]
    index = lax.broadcasted_iota(jnp.int32, (2 * CELLS, 1), 0) // CELLS * (NB - 1)
    rows_ref[...] = finish(
        index,
        own_land,
        is_air,
        win_ref[...],
        edge_rows(update_ref),
        edge_rows(x_ref),
        gain_ref,
        out_w_ref,
        up_ref,
        down_ref,
    )
    copies = []
    for n in range(2):
        copy = pltpu.make_async_copy(
            rows_ref.at[pl.ds(n * CELLS, CELLS)],
            out_hbm.at[pl.ds(n * (ROWS - CELLS), CELLS)],
            sem.at[n],
        )
        copy.start()
        copies.append(copy)
    for copy in copies:
        copy.wait()


VMEM = pl.BlockSpec(memory_space=pltpu.VMEM)
ANY = pl.BlockSpec(memory_space=pl.ANY)
SMEM = pl.BlockSpec(memory_space=pltpu.SMEM)


def array(*shape, dtype=BF):
    return jax.ShapeDtypeStruct(shape, dtype)


def cost(macs, size, exps=0):
    return pl.CostEstimate(flops=2 * macs, bytes_accessed=size, transcendentals=exps)


def per_device(
    tokens,
    norm_gains,
    qkv_weight,
    out_weight,
    cross_query,
    cross_kv,
    cross_out,
    up_weight,
    down_weight,
    intersection_list,
    land_bands,
):
    grid_x = tokens[0]
    x = grid_x.reshape(ROWS, D)
    gains = norm_gains[0]
    forward = [(i, (i + 1) % 8) for i in range(8)]
    backward = [((i + 1) % 8, i) for i in range(8)]
    east_edge, west_edge, x_first = lax.optimization_barrier(
        (grid_x[:, RX - BR :], grid_x[:, :BR], x)
    )
    west = lax.ppermute(east_edge, "face", forward).reshape(NB * SIDE, D)
    east = lax.ppermute(west_edge, "face", backward).reshape(NB * SIDE, D)

    half = ROWS // 2
    block = pl.BlockSpec((half, D), lambda i: (i, 0))
    params = pltpu.CompilerParams(vmem_limit_bytes=24 * MIB)
    pair_out = pl.pallas_call(
        kernel_cross_kv,
        grid=(2,),
        in_specs=[
            block,
            pl.BlockSpec((3, D), lambda i: (0, 0)),
            pl.BlockSpec((D, 2 * D), lambda i: (0, 0)),
        ],
        out_specs=pl.BlockSpec((half, 2 * D), lambda i: (i, 0)),
        out_shape=array(ROWS, 2 * D),
        cost_estimate=cost(ROWS * D * 2 * D, 4 * MIB),
        compiler_params=params,
        name="cross_kv",
    )(x_first, gains, cross_kv[0])
    partner = lax.ppermute(pair_out, "comp", [(0, 1), (1, 0)])

    q, k, v, cross_q = pl.pallas_call(
        kernel_own,
        grid=(2,),
        in_specs=[
            block,
            pl.BlockSpec((3, D), lambda i: (0, 0)),
            pl.BlockSpec((D, 3 * D), lambda i: (0, 0)),
            pl.BlockSpec((D, D), lambda i: (0, 0)),
        ],
        out_specs=[block, block, pl.BlockSpec((D, half), lambda i: (0, i)), block],
        out_shape=[array(ROWS, D), array(ROWS, D), array(D, ROWS), array(ROWS, D)],
        cost_estimate=cost(ROWS * D * 4 * D, 7 * MIB),
        compiler_params=params,
        name="own",
    )(x_first, gains, qkv_weight[0], cross_query[0])

    bad = pltpu.VMEM((8, 2 * CELLS), F32)
    update = pl.pallas_call(
        kernel_cross,
        in_specs=[SMEM] * 2 + [VMEM] * 3,
        out_specs=VMEM,
        out_shape=jax.ShapeDtypeStruct((ROWS, D), F32),
        scratch_shapes=[pltpu.VMEM((PAIRS * VROWS, ROWS), BF), pltpu.VMEM((D, ROWS), BF), bad],
        cost_estimate=cost(8 * ROWS * 512 * D, 4 * MIB, ROWS * HEADS * 512),
        compiler_params=params,
        name="cross",
    )(
        intersection_list.transpose(0, 2, 3, 1).reshape(2, KC, NB),
        land_bands,
        cross_q,
        partner,
        cross_out[0],
    )

    west, east, update = lax.optimization_barrier((west, east, update))
    top, bottom = [
        jnp.concatenate(
            [x[at * CELLS : (at + 1) * CELLS], *[side[at * SIDE : (at + 1) * SIDE] for side in (west, east)]],
            axis=0,
        )
        for at in (0, NB - 1)
    ]
    north = lax.ppermute(bottom, "tile", forward)
    south = lax.ppermute(top, "tile", backward)

    inner, edge_keys, edge_va = pl.pallas_call(
        kernel_window,
        in_specs=[SMEM] + [VMEM] * 12,
        out_specs=[VMEM] * 3,
        out_shape=[array(ROWS, D), array(4 * GROUP, D), array(PAIRS * VROWS, 4 * GROUP)],
        scratch_shapes=[
            pltpu.VMEM((NB * GROUP, D), BF),
            pltpu.VMEM((PAIRS * VROWS, NB * GROUP), BF),
            pltpu.VMEM((D, ROWS), BF),
            bad,
        ],
        cost_estimate=cost(6 << 30, 12 * MIB, ROWS * HEADS * WINDOW),
        compiler_params=pltpu.CompilerParams(vmem_limit_bytes=28 * MIB),
        name="window",
    )(
        land_bands,
        west,
        east,
        gains,
        qkv_weight[0],
        q,
        k,
        v,
        update,
        x,
        out_weight[0],
        up_weight[0],
        down_weight[0],
    )

    result = pl.pallas_call(
        kernel_last,
        in_specs=[SMEM] + [VMEM] * 12 + [ANY],
        out_specs=ANY,
        out_shape=array(ROWS, D),
        input_output_aliases={13: 0},
        scratch_shapes=[
            pltpu.VMEM((2 * WINDOW, D), BF),
            pltpu.VMEM((PAIRS * VROWS, 2 * WINDOW), BF),
            pltpu.VMEM((D, 2 * CELLS), BF),
            pltpu.VMEM((2 * CELLS, D), BF),
            bad,
            pltpu.SemaphoreType.DMA((2,)),
        ],
        cost_estimate=cost(2 << 30, 8 * MIB, ROWS * HEADS * 256),
        compiler_params=params,
        name="last",
    )(
        land_bands,
        north,
        south,
        edge_keys,
        edge_va,
        q,
        update,
        x,
        gains,
        qkv_weight[0],
        out_weight[0],
        up_weight[0],
        down_weight[0],
        inner,
    )
    return result.reshape(1, NB * BR, RX, D)


def solution(mesh):
    placed = (
        P("comp", "tile", "face", None),
        P("comp", None, None),
        P("comp", None, None),
        P("comp", None, None),
        P("comp", None, None),
        P("comp", None, None),
        P("comp", None, None),
        P("comp", None, None),
        P("comp", None, None),
        P(None, "tile", "face", None),
        P(),
    )
    return jax.shard_map(
        per_device,
        mesh=mesh,
        in_specs=placed,
        out_specs=P("comp", "tile", "face", None),
        check_vma=False,
    )
```

```python
import jax
import jax.numpy as jnp
from jax import lax
from jax.experimental import pallas as pl
from jax.experimental.pallas import tpu as pltpu
from jax.sharding import PartitionSpec as P

D = 512
FF = 2048
HEADS = 8
PAIRS = HEADS // 2
LANES = 128
RX = 16
BR = 8
NB = 8
KC = 4
CELLS = BR * RX
ROWS = NB * CELLS
SIDE = BR * BR
GROUP = CELLS + 2 * SIDE
WINDOW = 3 * GROUP
EXTRA = 16
VROWS = LANES + EXTRA

EPSILON = 1e-05
Q_SCALE = 1.4426950408889634 / 8.0
LIMIT = 2.0**100
BF = jnp.bfloat16
F32 = jnp.float32
MIB = 1 << 20


def norm_round(values, gain):
    mean_square = jnp.mean(values * values, axis=-1, keepdims=True)
    return (values * lax.rsqrt(mean_square + EPSILON) * gain.astype(F32)).astype(BF)


def mm(a, b):
    return jnp.dot(a, b, preferred_element_type=F32)


def mm_nt(a, b):
    return lax.dot_general(a, b, (((1,), (1,)), ((), ())), preferred_element_type=F32)


def mm_tn(a, b):
    return lax.dot_general(a, b, (((0,), (0,)), ((), ())), preferred_element_type=F32)


def mm_tt(a, b):
    return lax.dot_general(a, b, (((0,), (1,)), ((), ())), preferred_element_type=F32)


def augment(values_t, flag, out_ref, lane):
    keep = flag.astype(F32).astype(BF)
    for p in range(PAIRS):
        rows = values_t[p * LANES : (p + 1) * LANES]
        out_ref[pl.ds(p * VROWS, LANES), pl.ds(lane, CELLS)] = rows * keep
        out_ref[pl.ds(p * VROWS + LANES, EXTRA), pl.ds(lane, CELLS)] = (
            jnp.ones((EXTRA, CELLS), BF) * keep
        )


def score(pair, keys):
    low = lax.broadcasted_iota(jnp.int32, pair.shape, 1) < LANES // 2
    zero = jnp.zeros_like(pair)
    stacked = jnp.concatenate([jnp.where(low, pair, zero), jnp.where(low, zero, pair)], axis=0)
    return mm_nt(keys, stacked)


def blend(values_t, terms, extra):
    return share_out(mm(values_t, terms), extra)


def share_out(both, extra):
    sums = both[LANES : LANES + 8]
    share = 1.0 / (sums + extra)
    half = LANES // 2
    result = jnp.concatenate(
        [both[:half, :CELLS] * share[:1, :CELLS], both[half:LANES, CELLS:] * share[:1, CELLS:]],
        axis=0,
    )
    return result.astype(BF), sums


def products(count, queries, keys, values):
    def terms_of(i, p):
        return jnp.exp2(score(queries(i, p), keys(i, p))).astype(BF)

    steps = [(i, p) for i in range(count) for p in range(PAIRS)]
    following = terms_of(*steps[0])
    for n, (i, p) in enumerate(steps):
        terms = following
        if n + 1 < len(steps):
            following = terms_of(*steps[n + 1])
        yield i, p, mm(values(i, p), terms)


def attention(count, queries, keys, values, penalties, lane, out_ref, bad_ref, sides=None):
    bad_ref[...] = jnp.zeros_like(bad_ref)

    some_keys, some_values, held = sides or (keys, values, lambda i, p: 0.0)
    for i, p, both in products(count, queries, some_keys, some_values):
        result, sums = share_out(both + held(i, p), 1.0)
        out_ref[pl.ds(p * LANES, LANES), pl.ds(lane(i), CELLS)] = result
        bad_ref[...] += jnp.where(sums < LIMIT, 0.0, 1.0)

    @pl.when(jnp.sum(bad_ref[...]) > 0.0)
    def _():
        def band(i, carry):
            for p in range(PAIRS):
                scores = score(queries(i, p), keys(i, p))
                at = 0
                pieces = []
                for rows, penalty in penalties(i):
                    pieces.append(scores[at : at + rows] + penalty)
                    at += rows
                scores = jnp.concatenate(pieces, axis=0)
                highest = jnp.maximum(jnp.max(scores, axis=0, keepdims=True), 0.0)
                terms = jnp.exp2(scores - highest).astype(BF)
                result, _ = blend(values(i, p), terms, jnp.exp2(-highest))
                out_ref[pl.ds(p * LANES, LANES), pl.ds(lane(i), CELLS)] = result
            return carry

        lax.fori_loop(0, count, band, 0)


def aligned(i, size):
    return i * size if isinstance(i, int) else pl.multiple_of(i * size, size)


def kernel_cross_kv(x_ref, gain_ref, weight_ref, out_ref):
    cross_input = norm_round(x_ref[...].astype(F32), gain_ref[1:2, :])
    out_ref[:, :D] = mm(cross_input, weight_ref[:, :D]).astype(BF)
    out_ref[:, D:] = mm_tt(weight_ref[:, D:], cross_input).astype(BF)


def kernel_own(x_ref, gain_ref, qkv_ref, cq_ref, q_ref, k_ref, v_ref, c_ref):
    values = x_ref[...].astype(F32)
    mean_square = jnp.mean(values * values, axis=-1, keepdims=True)
    unit = values * lax.rsqrt(mean_square + EPSILON)
    attn_input = (unit * gain_ref[0:1, :].astype(F32)).astype(BF)
    cross_input = (unit * gain_ref[1:2, :].astype(F32)).astype(BF)
    q_ref[...] = (mm(attn_input, qkv_ref[:, :D]) * Q_SCALE).astype(BF)
    k_ref[...] = mm(attn_input, qkv_ref[:, D : 2 * D]).astype(BF)
    v_ref[...] = mm_tt(qkv_ref[:, 2 * D :], attn_input).astype(BF)
    c_ref[...] = (mm(cross_input, cq_ref[...]) * Q_SCALE).astype(BF)


def kernel_cross(links_ref, land_ref, q_ref, kv_ref, cross_w_ref, out_ref, va_ref, cross_ref, bad_ref):
    component = lax.axis_index("comp")
    own_land = land_ref[lax.axis_index("tile"), lax.axis_index("face")]
    floor = jnp.where(component == 1, 0, own_land)

    for j in range(NB):
        row, lane = (j // 4) * D, D + (j % 4) * CELLS
        augment(kv_ref[row : row + D, lane : lane + CELLS], j >= floor, va_ref, j * CELLS)

    def picks(i):
        return [links_ref[component, k, i] for k in range(KC)]

    def queries(i, p):
        return q_ref[pl.ds(aligned(i, CELLS), CELLS), pl.ds(p * LANES, LANES)]

    def keys(i, p):
        return jnp.concatenate(
            [kv_ref[pl.ds(aligned(j, CELLS), CELLS), pl.ds(p * LANES, LANES)] for j in picks(i)],
            axis=0,
        )

    def values(i, p):
        return jnp.concatenate(
            [va_ref[pl.ds(p * VROWS, VROWS), pl.ds(aligned(j, CELLS), CELLS)] for j in picks(i)],
            axis=1,
        )

    def penalties(i):
        return [(CELLS, jnp.where(j >= floor, 0.0, -1e30)) for j in picks(i)]

    def lane(i):
        return aligned(i, CELLS)

    attention(NB, queries, keys, values, penalties, lane, cross_ref, bad_ref)
    out_ref[...] = mm_tn(cross_ref[...], cross_w_ref[...])


def place(land_ref):
    is_air = lax.axis_index("comp") == 0
    tile_row = lax.axis_index("tile")
    tile_col = lax.axis_index("face")
    columns = (tile_col, (tile_col + 7) % 8, (tile_col + 1) % 8)

    def flags(r):
        inside_row = jnp.where(r == 0, tile_row - 1, jnp.where(r == NB + 1, tile_row + 1, tile_row))
        lat_ok = (inside_row >= 0) & (inside_row < 8)
        safe_row = jnp.clip(inside_row, 0, 7)
        index = jnp.where(r == 0, NB - 1, jnp.where(r == NB + 1, 0, r - 1))
        return [lat_ok & (is_air | (index >= land_ref[safe_row, c])) for c in columns]

    return is_air, flags


def project(rows_x, gain_ref, qkv_ref):
    normed = norm_round(rows_x.astype(F32), gain_ref[0:1, :])
    keys = mm(normed, qkv_ref[:, D : 2 * D]).astype(BF)
    return keys, mm_tt(qkv_ref[:, 2 * D :], normed).astype(BF)


def side_flag(flags, r):
    _, west_ok, east_ok = flags(r)
    west_lane = lax.broadcasted_iota(jnp.int32, (1, CELLS), 1) < SIDE
    return jnp.where(west_lane, west_ok.astype(F32), east_ok.astype(F32))


def window_penalties(flags, i):
    pieces = []
    for b in range(3):
        for rows, flag in zip((CELLS, SIDE, SIDE), flags(i + b)):
            pieces.append((rows, jnp.where(flag, 0.0, -1e30)))
    return pieces


def finish(index, own_land, is_air, win_t, update, x_rows, gain_ref, out_w_ref, up_ref, down_ref):
    live = jnp.where(is_air | (index >= own_land), 1.0, 0.0)
    middle = x_rows.astype(F32) + live * (mm_tn(win_t, out_w_ref[...]) + update)
    mlp_input = norm_round(middle, gain_ref[2:3, :])
    gate = 0.5 * mm(mlp_input, up_ref[...])
    hidden = (gate + gate * jnp.tanh(gate)).astype(BF)
    return (middle + live * mm(hidden, down_ref[...])).astype(BF)


def kernel_near(land_ref, q_ref, k_ref, v_ref, part_ref, va_ref):
    _, flags = place(land_ref)
    for i in range(NB):
        at = slice(i * CELLS, (i + 1) * CELLS)
        augment(v_ref[:, at], flags(i + 1)[0], va_ref, i * CELLS)

    def queries(n, p):
        return q_ref[(n + 1) * CELLS : (n + 2) * CELLS, p * LANES : (p + 1) * LANES]

    def keys(n, p):
        return k_ref[n * CELLS : (n + 3) * CELLS, p * LANES : (p + 1) * LANES]

    def values(n, p):
        return va_ref[p * VROWS : (p + 1) * VROWS, n * CELLS : (n + 3) * CELLS]

    for n, p, both in products(NB - 2, queries, keys, values):
        part_ref[n * PAIRS + p] = both


def kernel_window(
    land_ref,
    west_ref,
    east_ref,
    gain_ref,
    qkv_ref,
    q_ref,
    k_ref,
    v_ref,
    part_ref,
    update_ref,
    x_ref,
    out_w_ref,
    up_ref,
    down_ref,
    out_ref,
    edge_keys_ref,
    edge_va_ref,
    keys_ref,
    va_ref,
    win_ref,
    bad_ref,
):
    is_air, flags = place(land_ref)

    def put(r, offset, keys, values_t, flag):
        at = (r - 1) * GROUP + offset
        keys_ref[pl.ds(at, CELLS), :] = keys
        augment(values_t, flag, va_ref, at)

    blocks = 2
    for b in range(blocks):
        members = range(1 + b * NB // blocks, 1 + (b + 1) * NB // blocks)
        rows_x = []
        for r in members:
            rows_x += [ref[(r - 1) * SIDE : r * SIDE, :] for ref in (west_ref, east_ref)]
        keys, values_t = project(jnp.concatenate(rows_x, axis=0), gain_ref, qkv_ref)
        for n, r in enumerate(members):
            at = slice(n * CELLS, (n + 1) * CELLS)
            put(r, CELLS, keys[at], values_t[:, at], side_flag(flags, r))
    for i in range(NB):
        at = slice(i * CELLS, (i + 1) * CELLS)
        put(i + 1, 0, k_ref[at, :], v_ref[:, at], flags(i + 1)[0])
    for n, at in enumerate((0, (NB - 2) * GROUP)):
        to = slice(n * 2 * GROUP, (n + 1) * 2 * GROUP)
        edge_keys_ref[to, :] = keys_ref[at : at + 2 * GROUP, :]
        edge_va_ref[:, to] = va_ref[:, at : at + 2 * GROUP]

    def queries(n, p):
        return q_ref[pl.ds(aligned(n, CELLS) + CELLS, CELLS), pl.ds(p * LANES, LANES)]

    def keys_of(n, p):
        return keys_ref[pl.ds(aligned(n, GROUP), WINDOW), pl.ds(p * LANES, LANES)]

    def values_of(n, p):
        return va_ref[pl.ds(p * VROWS, VROWS), pl.ds(aligned(n, GROUP), WINDOW)]

    def penalties(n):
        return window_penalties(flags, n + 1)

    def lane(n):
        return aligned(n, CELLS) + CELLS

    def side_keys(n, p):
        at = [(n + b) * GROUP + CELLS for b in range(3)]
        return jnp.concatenate(
            [keys_ref[a : a + CELLS, p * LANES : (p + 1) * LANES] for a in at], axis=0
        )

    def side_values(n, p):
        at = [(n + b) * GROUP + CELLS for b in range(3)]
        return jnp.concatenate(
            [va_ref[p * VROWS : (p + 1) * VROWS, a : a + CELLS] for a in at], axis=1
        )

    def held(n, p):
        return part_ref[n * PAIRS + p]

    sides = (side_keys, side_values, held)
    attention(NB - 2, queries, keys_of, values_of, penalties, lane, win_ref, bad_ref, sides)

    own_land = land_ref[lax.axis_index("tile"), lax.axis_index("face")]
    chunk = (NB - 2) * CELLS // 2
    for c in range(2):
        start = CELLS + c * chunk
        at = slice(start, start + chunk)
        index = (start + lax.broadcasted_iota(jnp.int32, (chunk, 1), 0)) // CELLS
        out_ref[at, :] = finish(
            index,
            own_land,
            is_air,
            win_ref[:, at],
            update_ref[at, :],
            x_ref[at, :],
            gain_ref,
            out_w_ref,
            up_ref,
            down_ref,
        )


def kernel_last(
    land_ref,
    north_ref,
    south_ref,
    edge_keys_ref,
    edge_va_ref,
    q_ref,
    update_ref,
    x_ref,
    gain_ref,
    qkv_ref,
    out_w_ref,
    up_ref,
    down_ref,
    held_hbm,
    out_hbm,
    keys_ref,
    va_ref,
    win_ref,
    rows_ref,
    bad_ref,
    sem,
):
    del held_hbm
    is_air, flags = place(land_ref)
    rows_x = jnp.concatenate([north_ref[...], south_ref[...]], axis=0)
    new_keys, new_values = project(rows_x, gain_ref, qkv_ref)
    for n in range(2):
        new, held = n * WINDOW + n * 2 * GROUP, n * WINDOW + (1 - n) * GROUP
        src = slice(n * 2 * GROUP, (n + 1) * 2 * GROUP)
        keys_ref[new : new + GROUP, :] = new_keys[n * GROUP : (n + 1) * GROUP]
        keys_ref[held : held + 2 * GROUP, :] = edge_keys_ref[src, :]
        va_ref[:, held : held + 2 * GROUP] = edge_va_ref[:, src]
        r = n * (NB + 1)
        at = n * GROUP
        augment(new_values[:, at : at + CELLS], flags(r)[0], va_ref, new)
        augment(new_values[:, at + CELLS : at + GROUP], side_flag(flags, r), va_ref, new + CELLS)

    def queries(n, p):
        return q_ref[pl.ds(aligned(n, ROWS - CELLS), CELLS), pl.ds(p * LANES, LANES)]

    def keys_of(n, p):
        return keys_ref[pl.ds(aligned(n, WINDOW), WINDOW), pl.ds(p * LANES, LANES)]

    def values_of(n, p):
        return va_ref[pl.ds(p * VROWS, VROWS), pl.ds(aligned(n, WINDOW), WINDOW)]

    def penalties(n):
        return window_penalties(flags, n * (NB - 1))

    def lane(n):
        return aligned(n, CELLS)

    attention(2, queries, keys_of, values_of, penalties, lane, win_ref, bad_ref)

    def edge_rows(ref):
        return jnp.concatenate([ref[:CELLS, :], ref[ROWS - CELLS :, :]], axis=0)

    own_land = land_ref[lax.axis_index("tile"), lax.axis_index("face")]
    index = lax.broadcasted_iota(jnp.int32, (2 * CELLS, 1), 0) // CELLS * (NB - 1)
    rows_ref[...] = finish(
        index,
        own_land,
        is_air,
        win_ref[...],
        edge_rows(update_ref),
        edge_rows(x_ref),
        gain_ref,
        out_w_ref,
        up_ref,
        down_ref,
    )
    copies = []
    for n in range(2):
        copy = pltpu.make_async_copy(
            rows_ref.at[pl.ds(n * CELLS, CELLS)],
            out_hbm.at[pl.ds(n * (ROWS - CELLS), CELLS)],
            sem.at[n],
        )
        copy.start()
        copies.append(copy)
    for copy in copies:
        copy.wait()


VMEM = pl.BlockSpec(memory_space=pltpu.VMEM)
ANY = pl.BlockSpec(memory_space=pl.ANY)
SMEM = pl.BlockSpec(memory_space=pltpu.SMEM)


def array(*shape, dtype=BF):
    return jax.ShapeDtypeStruct(shape, dtype)


def cost(macs, size, exps=0):
    return pl.CostEstimate(flops=2 * macs, bytes_accessed=size, transcendentals=exps)


def per_device(
    tokens,
    norm_gains,
    qkv_weight,
    out_weight,
    cross_query,
    cross_kv,
    cross_out,
    up_weight,
    down_weight,
    intersection_list,
    land_bands,
):
    grid_x = tokens[0]
    x = grid_x.reshape(ROWS, D)
    gains = norm_gains[0]
    forward = [(i, (i + 1) % 8) for i in range(8)]
    backward = [((i + 1) % 8, i) for i in range(8)]
    east_edge, west_edge, x_first = lax.optimization_barrier(
        (grid_x[:, RX - BR :], grid_x[:, :BR], x)
    )
    west = lax.ppermute(east_edge, "face", forward).reshape(NB * SIDE, D)
    east = lax.ppermute(west_edge, "face", backward).reshape(NB * SIDE, D)

    half = ROWS // 2
    block = pl.BlockSpec((half, D), lambda i: (i, 0))
    params = pltpu.CompilerParams(vmem_limit_bytes=24 * MIB)
    pair_out = pl.pallas_call(
        kernel_cross_kv,
        grid=(2,),
        in_specs=[
            block,
            pl.BlockSpec((3, D), lambda i: (0, 0)),
            pl.BlockSpec((D, 2 * D), lambda i: (0, 0)),
        ],
        out_specs=pl.BlockSpec((half, 2 * D), lambda i: (i, 0)),
        out_shape=array(ROWS, 2 * D),
        cost_estimate=cost(ROWS * D * 2 * D, 4 * MIB),
        compiler_params=params,
        name="cross_kv",
    )(x_first, gains, cross_kv[0])
    partner = lax.ppermute(pair_out, "comp", [(0, 1), (1, 0)])

    q, k, v, cross_q = pl.pallas_call(
        kernel_own,
        grid=(2,),
        in_specs=[
            block,
            pl.BlockSpec((3, D), lambda i: (0, 0)),
            pl.BlockSpec((D, 3 * D), lambda i: (0, 0)),
            pl.BlockSpec((D, D), lambda i: (0, 0)),
        ],
        out_specs=[block, block, pl.BlockSpec((D, half), lambda i: (0, i)), block],
        out_shape=[array(ROWS, D), array(ROWS, D), array(D, ROWS), array(ROWS, D)],
        cost_estimate=cost(ROWS * D * 4 * D, 7 * MIB),
        compiler_params=params,
        name="own",
    )(x_first, gains, qkv_weight[0], cross_query[0])

    bad = pltpu.VMEM((8, 2 * CELLS), F32)
    update = pl.pallas_call(
        kernel_cross,
        in_specs=[SMEM] * 2 + [VMEM] * 3,
        out_specs=VMEM,
        out_shape=jax.ShapeDtypeStruct((ROWS, D), F32),
        scratch_shapes=[pltpu.VMEM((PAIRS * VROWS, ROWS), BF), pltpu.VMEM((D, ROWS), BF), bad],
        cost_estimate=cost(8 * ROWS * 512 * D, 4 * MIB, ROWS * HEADS * 512),
        compiler_params=params,
        name="cross",
    )(
        intersection_list.transpose(0, 2, 3, 1).reshape(2, KC, NB),
        land_bands,
        cross_q,
        partner,
        cross_out[0],
    )

    part = pl.pallas_call(
        kernel_near,
        in_specs=[SMEM] + [VMEM] * 3,
        out_specs=VMEM,
        out_shape=jax.ShapeDtypeStruct(((NB - 2) * PAIRS, VROWS, 2 * CELLS), F32),
        scratch_shapes=[pltpu.VMEM((PAIRS * VROWS, ROWS), BF)],
        cost_estimate=cost(6 * ROWS * 384 * D, 7 * MIB, ROWS * HEADS * 384),
        compiler_params=params,
        name="near",
    )(land_bands, q, k, v)

    west, east, update, part = lax.optimization_barrier((west, east, update, part))
    top, bottom = [
        jnp.concatenate(
            [x[at * CELLS : (at + 1) * CELLS], *[side[at * SIDE : (at + 1) * SIDE] for side in (west, east)]],
            axis=0,
        )
        for at in (0, NB - 1)
    ]
    north = lax.ppermute(bottom, "tile", forward)
    south = lax.ppermute(top, "tile", backward)

    inner, edge_keys, edge_va = pl.pallas_call(
        kernel_window,
        in_specs=[SMEM] + [VMEM] * 13,
        out_specs=[VMEM] * 3,
        out_shape=[array(ROWS, D), array(4 * GROUP, D), array(PAIRS * VROWS, 4 * GROUP)],
        scratch_shapes=[
            pltpu.VMEM((NB * GROUP, D), BF),
            pltpu.VMEM((PAIRS * VROWS, NB * GROUP), BF),
            pltpu.VMEM((D, ROWS), BF),
            bad,
        ],
        cost_estimate=cost(6 << 30, 12 * MIB, ROWS * HEADS * WINDOW),
        compiler_params=pltpu.CompilerParams(vmem_limit_bytes=28 * MIB),
        name="window",
    )(
        land_bands,
        west,
        east,
        gains,
        qkv_weight[0],
        q,
        k,
        v,
        part,
        update,
        x,
        out_weight[0],
        up_weight[0],
        down_weight[0],
    )

    result = pl.pallas_call(
        kernel_last,
        in_specs=[SMEM] + [VMEM] * 12 + [ANY],
        out_specs=ANY,
        out_shape=array(ROWS, D),
        input_output_aliases={13: 0},
        scratch_shapes=[
            pltpu.VMEM((2 * WINDOW, D), BF),
            pltpu.VMEM((PAIRS * VROWS, 2 * WINDOW), BF),
            pltpu.VMEM((D, 2 * CELLS), BF),
            pltpu.VMEM((2 * CELLS, D), BF),
            bad,
            pltpu.SemaphoreType.DMA((2,)),
        ],
        cost_estimate=cost(2 << 30, 8 * MIB, ROWS * HEADS * 256),
        compiler_params=params,
        name="last",
    )(
        land_bands,
        north,
        south,
        edge_keys,
        edge_va,
        q,
        update,
        x,
        gains,
        qkv_weight[0],
        out_weight[0],
        up_weight[0],
        down_weight[0],
        inner,
    )
    return result.reshape(1, NB * BR, RX, D)


def solution(mesh):
    placed = (
        P("comp", "tile", "face", None),
        P("comp", None, None),
        P("comp", None, None),
        P("comp", None, None),
        P("comp", None, None),
        P("comp", None, None),
        P("comp", None, None),
        P("comp", None, None),
        P("comp", None, None),
        P(None, "tile", "face", None),
        P(),
    )
    return jax.shard_map(
        per_device,
        mesh=mesh,
        in_specs=placed,
        out_specs=P("comp", "tile", "face", None),
        check_vma=False,
    )
```

```python
import jax
import jax.numpy as jnp
from jax import lax
from jax.experimental import pallas as pl
from jax.experimental.pallas import tpu as pltpu
from jax.sharding import PartitionSpec as P

D = 512
FF = 2048
HEADS = 8
PAIRS = HEADS // 2
LANES = 128
RX = 16
BR = 8
NB = 8
KC = 4
CELLS = BR * RX
ROWS = NB * CELLS
SIDE = BR * BR
GROUP = CELLS + 2 * SIDE
WINDOW = 3 * GROUP
EXTRA = 16
VROWS = LANES + EXTRA

EPSILON = 1e-05
Q_SCALE = 1.4426950408889634 / 8.0
LIMIT = 2.0**100
BF = jnp.bfloat16
F32 = jnp.float32
MIB = 1 << 20


def norm_round(values, gain):
    mean_square = jnp.mean(values * values, axis=-1, keepdims=True)
    return (values * lax.rsqrt(mean_square + EPSILON) * gain.astype(F32)).astype(BF)


def mm(a, b):
    return jnp.dot(a, b, preferred_element_type=F32)


def mm_nt(a, b):
    return lax.dot_general(a, b, (((1,), (1,)), ((), ())), preferred_element_type=F32)


def mm_tn(a, b):
    return lax.dot_general(a, b, (((0,), (0,)), ((), ())), preferred_element_type=F32)


def mm_tt(a, b):
    return lax.dot_general(a, b, (((0,), (1,)), ((), ())), preferred_element_type=F32)


def augment(values_t, flag, out_ref, lane):
    keep = flag.astype(F32).astype(BF)
    for p in range(PAIRS):
        rows = values_t[p * LANES : (p + 1) * LANES]
        out_ref[pl.ds(p * VROWS, LANES), pl.ds(lane, CELLS)] = rows * keep
        out_ref[pl.ds(p * VROWS + LANES, EXTRA), pl.ds(lane, CELLS)] = (
            jnp.ones((EXTRA, CELLS), BF) * keep
        )


def score(pair, keys):
    low = lax.broadcasted_iota(jnp.int32, pair.shape, 1) < LANES // 2
    zero = jnp.zeros_like(pair)
    stacked = jnp.concatenate([jnp.where(low, pair, zero), jnp.where(low, zero, pair)], axis=0)
    return mm_nt(keys, stacked)


def blend(values_t, terms, extra):
    both = mm(values_t, terms)
    sums = both[LANES : LANES + 8]
    share = 1.0 / (sums + extra)
    half = LANES // 2
    result = jnp.concatenate(
        [both[:half, :CELLS] * share[:1, :CELLS], both[half:LANES, CELLS:] * share[:1, CELLS:]],
        axis=0,
    )
    return result.astype(BF), sums


def attention(count, queries, keys, values, penalties, lane, out_ref, bad_ref):
    bad_ref[...] = jnp.zeros_like(bad_ref)

    def terms_of(i, p):
        return jnp.exp2(score(queries(i, p), keys(i, p))).astype(BF)

    steps = [(i, p) for i in range(count) for p in range(PAIRS)]
    following = terms_of(*steps[0])
    for n, (i, p) in enumerate(steps):
        terms = following
        if n + 1 < len(steps):
            following = terms_of(*steps[n + 1])
        result, sums = blend(values(i, p), terms, 1.0)
        out_ref[pl.ds(p * LANES, LANES), pl.ds(lane(i), CELLS)] = result
        bad_ref[...] += jnp.where(sums < LIMIT, 0.0, 1.0)

    @pl.when(jnp.sum(bad_ref[...]) > 0.0)
    def _():
        def band(i, carry):
            for p in range(PAIRS):
                scores = score(queries(i, p), keys(i, p))
                at = 0
                pieces = []
                for rows, penalty in penalties(i):
                    pieces.append(scores[at : at + rows] + penalty)
                    at += rows
                scores = jnp.concatenate(pieces, axis=0)
                highest = jnp.maximum(jnp.max(scores, axis=0, keepdims=True), 0.0)
                terms = jnp.exp2(scores - highest).astype(BF)
                result, _ = blend(values(i, p), terms, jnp.exp2(-highest))
                out_ref[pl.ds(p * LANES, LANES), pl.ds(lane(i), CELLS)] = result
            return carry

        lax.fori_loop(0, count, band, 0)


def aligned(i, size):
    return i * size if isinstance(i, int) else pl.multiple_of(i * size, size)


def kernel_cross_kv(x_ref, gain_ref, weight_ref, out_ref):
    cross_input = norm_round(x_ref[...].astype(F32), gain_ref[1:2, :])
    out_ref[:, :D] = mm(cross_input, weight_ref[:, :D]).astype(BF)
    out_ref[:, D:] = mm_tt(weight_ref[:, D:], cross_input).astype(BF)


def kernel_own(x_ref, gain_ref, qkv_ref, cq_ref, q_ref, k_ref, v_ref, c_ref):
    values = x_ref[...].astype(F32)
    mean_square = jnp.mean(values * values, axis=-1, keepdims=True)
    unit = values * lax.rsqrt(mean_square + EPSILON)
    attn_input = (unit * gain_ref[0:1, :].astype(F32)).astype(BF)
    cross_input = (unit * gain_ref[1:2, :].astype(F32)).astype(BF)
    q_ref[...] = (mm(attn_input, qkv_ref[:, :D]) * Q_SCALE).astype(BF)
    k_ref[...] = mm(attn_input, qkv_ref[:, D : 2 * D]).astype(BF)
    v_ref[...] = mm_tt(qkv_ref[:, 2 * D :], attn_input).astype(BF)
    c_ref[...] = (mm(cross_input, cq_ref[...]) * Q_SCALE).astype(BF)


def kernel_cross(links_ref, land_ref, q_ref, kv_ref, cross_w_ref, out_ref, va_ref, cross_ref, bad_ref):
    component = lax.axis_index("comp")
    own_land = land_ref[lax.axis_index("tile"), lax.axis_index("face")]
    floor = jnp.where(component == 1, 0, own_land)

    for j in range(NB):
        row, lane = (j // 4) * D, D + (j % 4) * CELLS
        augment(kv_ref[row : row + D, lane : lane + CELLS], j >= floor, va_ref, j * CELLS)

    def picks(i):
        return [links_ref[component, k, i] for k in range(KC)]

    def queries(i, p):
        return q_ref[pl.ds(aligned(i, CELLS), CELLS), pl.ds(p * LANES, LANES)]

    def keys(i, p):
        return jnp.concatenate(
            [kv_ref[pl.ds(aligned(j, CELLS), CELLS), pl.ds(p * LANES, LANES)] for j in picks(i)],
            axis=0,
        )

    def values(i, p):
        return jnp.concatenate(
            [va_ref[pl.ds(p * VROWS, VROWS), pl.ds(aligned(j, CELLS), CELLS)] for j in picks(i)],
            axis=1,
        )

    def penalties(i):
        return [(CELLS, jnp.where(j >= floor, 0.0, -1e30)) for j in picks(i)]

    def lane(i):
        return aligned(i, CELLS)

    attention(NB, queries, keys, values, penalties, lane, cross_ref, bad_ref)
    out_ref[...] = mm_tn(cross_ref[...], cross_w_ref[...])


def place(land_ref):
    is_air = lax.axis_index("comp") == 0
    tile_row = lax.axis_index("tile")
    tile_col = lax.axis_index("face")
    columns = (tile_col, (tile_col + 7) % 8, (tile_col + 1) % 8)

    def flags(r):
        inside_row = jnp.where(r == 0, tile_row - 1, jnp.where(r == NB + 1, tile_row + 1, tile_row))
        lat_ok = (inside_row >= 0) & (inside_row < 8)
        safe_row = jnp.clip(inside_row, 0, 7)
        index = jnp.where(r == 0, NB - 1, jnp.where(r == NB + 1, 0, r - 1))
        return [lat_ok & (is_air | (index >= land_ref[safe_row, c])) for c in columns]

    return is_air, flags


def project(rows_x, gain_ref, qkv_ref):
    normed = norm_round(rows_x.astype(F32), gain_ref[0:1, :])
    keys = mm(normed, qkv_ref[:, D : 2 * D]).astype(BF)
    return keys, mm_tt(qkv_ref[:, 2 * D :], normed).astype(BF)


def side_flag(flags, r):
    _, west_ok, east_ok = flags(r)
    west_lane = lax.broadcasted_iota(jnp.int32, (1, CELLS), 1) < SIDE
    return jnp.where(west_lane, west_ok.astype(F32), east_ok.astype(F32))


def window_penalties(flags, i):
    pieces = []
    for b in range(3):
        for rows, flag in zip((CELLS, SIDE, SIDE), flags(i + b)):
            pieces.append((rows, jnp.where(flag, 0.0, -1e30)))
    return pieces


def finish(pieces, own_land, is_air, gain_ref, out_w_ref, up_ref, down_ref):
    front = []
    for index, win_t, update, x_rows in pieces:
        live = jnp.where(is_air | (index >= own_land), 1.0, 0.0)
        middle = x_rows.astype(F32) + live * (mm_tn(win_t, out_w_ref[...]) + update)
        front.append((live, middle, norm_round(middle, gain_ref[2:3, :])))
    gates = [0.5 * mm(mlp_input, up_ref[...]) for _, _, mlp_input in front]
    results = []
    for (live, middle, _), gate in zip(front, gates):
        hidden = (gate + gate * jnp.tanh(gate)).astype(BF)
        results.append((middle + live * mm(hidden, down_ref[...])).astype(BF))
    return results


def kernel_window(
    land_ref,
    west_ref,
    east_ref,
    gain_ref,
    qkv_ref,
    q_ref,
    k_ref,
    v_ref,
    update_ref,
    x_ref,
    out_w_ref,
    up_ref,
    down_ref,
    out_ref,
    edge_keys_ref,
    edge_va_ref,
    keys_ref,
    va_ref,
    win_ref,
    bad_ref,
):
    is_air, flags = place(land_ref)

    def put(r, offset, keys, values_t, flag):
        at = (r - 1) * GROUP + offset
        keys_ref[pl.ds(at, CELLS), :] = keys
        augment(values_t, flag, va_ref, at)

    blocks = 2
    for b in range(blocks):
        members = range(1 + b * NB // blocks, 1 + (b + 1) * NB // blocks)
        rows_x = []
        for r in members:
            rows_x += [ref[(r - 1) * SIDE : r * SIDE, :] for ref in (west_ref, east_ref)]
        keys, values_t = project(jnp.concatenate(rows_x, axis=0), gain_ref, qkv_ref)
        for n, r in enumerate(members):
            at = slice(n * CELLS, (n + 1) * CELLS)
            put(r, CELLS, keys[at], values_t[:, at], side_flag(flags, r))
    for i in range(NB):
        at = slice(i * CELLS, (i + 1) * CELLS)
        put(i + 1, 0, k_ref[at, :], v_ref[:, at], flags(i + 1)[0])
    for n, at in enumerate((0, (NB - 2) * GROUP)):
        to = slice(n * 2 * GROUP, (n + 1) * 2 * GROUP)
        edge_keys_ref[to, :] = keys_ref[at : at + 2 * GROUP, :]
        edge_va_ref[:, to] = va_ref[:, at : at + 2 * GROUP]

    def queries(n, p):
        return q_ref[pl.ds(aligned(n, CELLS) + CELLS, CELLS), pl.ds(p * LANES, LANES)]

    def keys_of(n, p):
        return keys_ref[pl.ds(aligned(n, GROUP), WINDOW), pl.ds(p * LANES, LANES)]

    def values_of(n, p):
        return va_ref[pl.ds(p * VROWS, VROWS), pl.ds(aligned(n, GROUP), WINDOW)]

    def penalties(n):
        return window_penalties(flags, n + 1)

    def lane(n):
        return aligned(n, CELLS) + CELLS

    attention(NB - 2, queries, keys_of, values_of, penalties, lane, win_ref, bad_ref)

    own_land = land_ref[lax.axis_index("tile"), lax.axis_index("face")]
    chunk = (NB - 2) * CELLS // 2
    spans = [slice(CELLS + c * chunk, CELLS + (c + 1) * chunk) for c in range(2)]
    pieces = []
    for at in spans:
        index = (at.start + lax.broadcasted_iota(jnp.int32, (chunk, 1), 0)) // CELLS
        pieces.append((index, win_ref[:, at], update_ref[at, :], x_ref[at, :]))
    results = finish(pieces, own_land, is_air, gain_ref, out_w_ref, up_ref, down_ref)
    for at, rows in zip(spans, results):
        out_ref[at, :] = rows


def kernel_last(
    land_ref,
    north_ref,
    south_ref,
    edge_keys_ref,
    edge_va_ref,
    q_ref,
    update_ref,
    x_ref,
    gain_ref,
    qkv_ref,
    out_w_ref,
    up_ref,
    down_ref,
    held_hbm,
    out_hbm,
    keys_ref,
    va_ref,
    win_ref,
    rows_ref,
    bad_ref,
    sem,
):
    del held_hbm
    is_air, flags = place(land_ref)
    rows_x = jnp.concatenate([north_ref[...], south_ref[...]], axis=0)
    new_keys, new_values = project(rows_x, gain_ref, qkv_ref)
    for n in range(2):
        new, held = n * WINDOW + n * 2 * GROUP, n * WINDOW + (1 - n) * GROUP
        src = slice(n * 2 * GROUP, (n + 1) * 2 * GROUP)
        keys_ref[new : new + GROUP, :] = new_keys[n * GROUP : (n + 1) * GROUP]
        keys_ref[held : held + 2 * GROUP, :] = edge_keys_ref[src, :]
        va_ref[:, held : held + 2 * GROUP] = edge_va_ref[:, src]
        r = n * (NB + 1)
        at = n * GROUP
        augment(new_values[:, at : at + CELLS], flags(r)[0], va_ref, new)
        augment(new_values[:, at + CELLS : at + GROUP], side_flag(flags, r), va_ref, new + CELLS)

    def queries(n, p):
        return q_ref[pl.ds(aligned(n, ROWS - CELLS), CELLS), pl.ds(p * LANES, LANES)]

    def keys_of(n, p):
        return keys_ref[pl.ds(aligned(n, WINDOW), WINDOW), pl.ds(p * LANES, LANES)]

    def values_of(n, p):
        return va_ref[pl.ds(p * VROWS, VROWS), pl.ds(aligned(n, WINDOW), WINDOW)]

    def penalties(n):
        return window_penalties(flags, n * (NB - 1))

    def lane(n):
        return aligned(n, CELLS)

    attention(2, queries, keys_of, values_of, penalties, lane, win_ref, bad_ref)

    def edge_rows(ref):
        return jnp.concatenate([ref[:CELLS, :], ref[ROWS - CELLS :, :]], axis=0)

    own_land = land_ref[lax.axis_index("tile"), lax.axis_index("face")]
    index = lax.broadcasted_iota(jnp.int32, (2 * CELLS, 1), 0) // CELLS * (NB - 1)
    piece = (index, win_ref[...], edge_rows(update_ref), edge_rows(x_ref))
    [rows_ref[...]] = finish([piece], own_land, is_air, gain_ref, out_w_ref, up_ref, down_ref)
    copies = []
    for n in range(2):
        copy = pltpu.make_async_copy(
            rows_ref.at[pl.ds(n * CELLS, CELLS)],
            out_hbm.at[pl.ds(n * (ROWS - CELLS), CELLS)],
            sem.at[n],
        )
        copy.start()
        copies.append(copy)
    for copy in copies:
        copy.wait()


VMEM = pl.BlockSpec(memory_space=pltpu.VMEM)
ANY = pl.BlockSpec(memory_space=pl.ANY)
SMEM = pl.BlockSpec(memory_space=pltpu.SMEM)


def array(*shape, dtype=BF):
    return jax.ShapeDtypeStruct(shape, dtype)


def cost(macs, size, exps=0):
    return pl.CostEstimate(flops=2 * macs, bytes_accessed=size, transcendentals=exps)


def per_device(
    tokens,
    norm_gains,
    qkv_weight,
    out_weight,
    cross_query,
    cross_kv,
    cross_out,
    up_weight,
    down_weight,
    intersection_list,
    land_bands,
):
    grid_x = tokens[0]
    x = grid_x.reshape(ROWS, D)
    gains = norm_gains[0]
    forward = [(i, (i + 1) % 8) for i in range(8)]
    backward = [((i + 1) % 8, i) for i in range(8)]
    east_edge, west_edge, x_first = lax.optimization_barrier(
        (grid_x[:, RX - BR :], grid_x[:, :BR], x)
    )
    west = lax.ppermute(east_edge, "face", forward).reshape(NB * SIDE, D)
    east = lax.ppermute(west_edge, "face", backward).reshape(NB * SIDE, D)

    half = ROWS // 2
    block = pl.BlockSpec((half, D), lambda i: (i, 0))
    params = pltpu.CompilerParams(vmem_limit_bytes=24 * MIB)
    pair_out = pl.pallas_call(
        kernel_cross_kv,
        grid=(2,),
        in_specs=[
            block,
            pl.BlockSpec((3, D), lambda i: (0, 0)),
            pl.BlockSpec((D, 2 * D), lambda i: (0, 0)),
        ],
        out_specs=pl.BlockSpec((half, 2 * D), lambda i: (i, 0)),
        out_shape=array(ROWS, 2 * D),
        cost_estimate=cost(ROWS * D * 2 * D, 4 * MIB),
        compiler_params=params,
        name="cross_kv",
    )(x_first, gains, cross_kv[0])
    partner = lax.ppermute(pair_out, "comp", [(0, 1), (1, 0)])

    q, k, v, cross_q = pl.pallas_call(
        kernel_own,
        grid=(2,),
        in_specs=[
            block,
            pl.BlockSpec((3, D), lambda i: (0, 0)),
            pl.BlockSpec((D, 3 * D), lambda i: (0, 0)),
            pl.BlockSpec((D, D), lambda i: (0, 0)),
        ],
        out_specs=[block, block, pl.BlockSpec((D, half), lambda i: (0, i)), block],
        out_shape=[array(ROWS, D), array(ROWS, D), array(D, ROWS), array(ROWS, D)],
        cost_estimate=cost(ROWS * D * 4 * D, 7 * MIB),
        compiler_params=params,
        name="own",
    )(x_first, gains, qkv_weight[0], cross_query[0])

    bad = pltpu.VMEM((8, 2 * CELLS), F32)
    update = pl.pallas_call(
        kernel_cross,
        in_specs=[SMEM] * 2 + [VMEM] * 3,
        out_specs=VMEM,
        out_shape=jax.ShapeDtypeStruct((ROWS, D), F32),
        scratch_shapes=[pltpu.VMEM((PAIRS * VROWS, ROWS), BF), pltpu.VMEM((D, ROWS), BF), bad],
        cost_estimate=cost(8 * ROWS * 512 * D, 4 * MIB, ROWS * HEADS * 512),
        compiler_params=params,
        name="cross",
    )(
        intersection_list.transpose(0, 2, 3, 1).reshape(2, KC, NB),
        land_bands,
        cross_q,
        partner,
        cross_out[0],
    )

    west, east, update = lax.optimization_barrier((west, east, update))
    top, bottom = [
        jnp.concatenate(
            [x[at * CELLS : (at + 1) * CELLS], *[side[at * SIDE : (at + 1) * SIDE] for side in (west, east)]],
            axis=0,
        )
        for at in (0, NB - 1)
    ]
    north = lax.ppermute(bottom, "tile", forward)
    south = lax.ppermute(top, "tile", backward)

    inner, edge_keys, edge_va = pl.pallas_call(
        kernel_window,
        in_specs=[SMEM] + [VMEM] * 12,
        out_specs=[VMEM] * 3,
        out_shape=[array(ROWS, D), array(4 * GROUP, D), array(PAIRS * VROWS, 4 * GROUP)],
        scratch_shapes=[
            pltpu.VMEM((NB * GROUP, D), BF),
            pltpu.VMEM((PAIRS * VROWS, NB * GROUP), BF),
            pltpu.VMEM((D, ROWS), BF),
            bad,
        ],
        cost_estimate=cost(6 << 30, 12 * MIB, ROWS * HEADS * WINDOW),
        compiler_params=pltpu.CompilerParams(vmem_limit_bytes=28 * MIB),
        name="window",
    )(
        land_bands,
        west,
        east,
        gains,
        qkv_weight[0],
        q,
        k,
        v,
        update,
        x,
        out_weight[0],
        up_weight[0],
        down_weight[0],
    )

    result = pl.pallas_call(
        kernel_last,
        in_specs=[SMEM] + [VMEM] * 12 + [ANY],
        out_specs=ANY,
        out_shape=array(ROWS, D),
        input_output_aliases={13: 0},
        scratch_shapes=[
            pltpu.VMEM((2 * WINDOW, D), BF),
            pltpu.VMEM((PAIRS * VROWS, 2 * WINDOW), BF),
            pltpu.VMEM((D, 2 * CELLS), BF),
            pltpu.VMEM((2 * CELLS, D), BF),
            bad,
            pltpu.SemaphoreType.DMA((2,)),
        ],
        cost_estimate=cost(2 << 30, 8 * MIB, ROWS * HEADS * 256),
        compiler_params=params,
        name="last",
    )(
        land_bands,
        north,
        south,
        edge_keys,
        edge_va,
        q,
        update,
        x,
        gains,
        qkv_weight[0],
        out_weight[0],
        up_weight[0],
        down_weight[0],
        inner,
    )
    return result.reshape(1, NB * BR, RX, D)


def solution(mesh):
    placed = (
        P("comp", "tile", "face", None),
        P("comp", None, None),
        P("comp", None, None),
        P("comp", None, None),
        P("comp", None, None),
        P("comp", None, None),
        P("comp", None, None),
        P("comp", None, None),
        P("comp", None, None),
        P(None, "tile", "face", None),
        P(),
    )
    return jax.shard_map(
        per_device,
        mesh=mesh,
        in_specs=placed,
        out_specs=P("comp", "tile", "face", None),
        check_vma=False,
    )
```

```python
import jax
import jax.numpy as jnp
from jax import lax
from jax.experimental import pallas as pl
from jax.experimental.pallas import tpu as pltpu
from jax.sharding import PartitionSpec as P

D = 512
FF = 2048
HEADS = 8
PAIRS = HEADS // 2
LANES = 128
RX = 16
BR = 8
NB = 8
KC = 4
CELLS = BR * RX
ROWS = NB * CELLS
SIDE = BR * BR
GROUP = CELLS + 2 * SIDE
WINDOW = 3 * GROUP
EXTRA = 16
VROWS = LANES + EXTRA

EPSILON = 1e-05
Q_SCALE = 1.4426950408889634 / 8.0
LIMIT = 2.0**100
BF = jnp.bfloat16
F32 = jnp.float32
MIB = 1 << 20


def norm_round(values, gain):
    mean_square = jnp.mean(values * values, axis=-1, keepdims=True)
    return (values * lax.rsqrt(mean_square + EPSILON) * gain.astype(F32)).astype(BF)


def mm(a, b):
    return jnp.dot(a, b, preferred_element_type=F32)


def mm_nt(a, b):
    return lax.dot_general(a, b, (((1,), (1,)), ((), ())), preferred_element_type=F32)


def mm_tn(a, b):
    return lax.dot_general(a, b, (((0,), (0,)), ((), ())), preferred_element_type=F32)


def mm_tt(a, b):
    return lax.dot_general(a, b, (((0,), (1,)), ((), ())), preferred_element_type=F32)


def augment(values_t, flag, out_ref, lane):
    keep = flag.astype(F32).astype(BF)
    for p in range(PAIRS):
        rows = values_t[p * LANES : (p + 1) * LANES]
        out_ref[pl.ds(p * VROWS, LANES), pl.ds(lane, CELLS)] = rows * keep
        out_ref[pl.ds(p * VROWS + LANES, EXTRA), pl.ds(lane, CELLS)] = (
            jnp.ones((EXTRA, CELLS), BF) * keep
        )


def score(pair, keys):
    low = lax.broadcasted_iota(jnp.int32, pair.shape, 1) < LANES // 2
    zero = jnp.zeros_like(pair)
    stacked = jnp.concatenate([jnp.where(low, pair, zero), jnp.where(low, zero, pair)], axis=0)
    return mm_nt(keys, stacked)


def blend(values_t, terms, extra):
    both = mm(values_t, terms)
    sums = both[LANES : LANES + 8]
    share = 1.0 / (sums + extra)
    half = LANES // 2
    result = jnp.concatenate(
        [both[:half, :CELLS] * share[:1, :CELLS], both[half:LANES, CELLS:] * share[:1, CELLS:]],
        axis=0,
    )
    return result.astype(BF), sums


def attention(count, queries, keys, values, penalties, lane, out_ref, bad_ref, prepare=None):
    bad_ref[...] = jnp.zeros_like(bad_ref)

    def terms_of(i, p):
        return jnp.exp2(score(queries(i, p), keys(i, p))).astype(BF)

    steps = [(i, p) for i in range(count) for p in range(PAIRS)]
    following = terms_of(*steps[0])
    if prepare:
        prepare()
    for n, (i, p) in enumerate(steps):
        terms = following
        if n + 1 < len(steps):
            following = terms_of(*steps[n + 1])
        result, sums = blend(values(i, p), terms, 1.0)
        out_ref[pl.ds(p * LANES, LANES), pl.ds(lane(i), CELLS)] = result
        bad_ref[...] += jnp.where(sums < LIMIT, 0.0, 1.0)

    @pl.when(jnp.sum(bad_ref[...]) > 0.0)
    def _():
        def band(i, carry):
            for p in range(PAIRS):
                scores = score(queries(i, p), keys(i, p))
                at = 0
                pieces = []
                for rows, penalty in penalties(i):
                    pieces.append(scores[at : at + rows] + penalty)
                    at += rows
                scores = jnp.concatenate(pieces, axis=0)
                highest = jnp.maximum(jnp.max(scores, axis=0, keepdims=True), 0.0)
                terms = jnp.exp2(scores - highest).astype(BF)
                result, _ = blend(values(i, p), terms, jnp.exp2(-highest))
                out_ref[pl.ds(p * LANES, LANES), pl.ds(lane(i), CELLS)] = result
            return carry

        lax.fori_loop(0, count, band, 0)


def aligned(i, size):
    return i * size if isinstance(i, int) else pl.multiple_of(i * size, size)


def kernel_cross_kv(x_ref, gain_ref, weight_ref, out_ref):
    cross_input = norm_round(x_ref[...].astype(F32), gain_ref[1:2, :])
    out_ref[:, :D] = mm(cross_input, weight_ref[:, :D]).astype(BF)
    out_ref[:, D:] = mm_tt(weight_ref[:, D:], cross_input).astype(BF)


def kernel_own(x_ref, gain_ref, qkv_ref, cq_ref, q_ref, k_ref, v_ref, c_ref):
    values = x_ref[...].astype(F32)
    mean_square = jnp.mean(values * values, axis=-1, keepdims=True)
    unit = values * lax.rsqrt(mean_square + EPSILON)
    attn_input = (unit * gain_ref[0:1, :].astype(F32)).astype(BF)
    cross_input = (unit * gain_ref[1:2, :].astype(F32)).astype(BF)
    q_ref[...] = (mm(attn_input, qkv_ref[:, :D]) * Q_SCALE).astype(BF)
    k_ref[...] = mm(attn_input, qkv_ref[:, D : 2 * D]).astype(BF)
    v_ref[...] = mm_tt(qkv_ref[:, 2 * D :], attn_input).astype(BF)
    c_ref[...] = (mm(cross_input, cq_ref[...]) * Q_SCALE).astype(BF)


def kernel_cross(links_ref, land_ref, q_ref, kv_ref, cross_w_ref, out_ref, va_ref, cross_ref, bad_ref):
    component = lax.axis_index("comp")
    own_land = land_ref[lax.axis_index("tile"), lax.axis_index("face")]
    floor = jnp.where(component == 1, 0, own_land)

    def prepare():
        for j in range(NB):
            row, lane = (j // 4) * D, D + (j % 4) * CELLS
            augment(kv_ref[row : row + D, lane : lane + CELLS], j >= floor, va_ref, j * CELLS)

    def picks(i):
        return [links_ref[component, k, i] for k in range(KC)]

    def queries(i, p):
        return q_ref[pl.ds(aligned(i, CELLS), CELLS), pl.ds(p * LANES, LANES)]

    def keys(i, p):
        return jnp.concatenate(
            [kv_ref[pl.ds(aligned(j, CELLS), CELLS), pl.ds(p * LANES, LANES)] for j in picks(i)],
            axis=0,
        )

    def values(i, p):
        return jnp.concatenate(
            [va_ref[pl.ds(p * VROWS, VROWS), pl.ds(aligned(j, CELLS), CELLS)] for j in picks(i)],
            axis=1,
        )

    def penalties(i):
        return [(CELLS, jnp.where(j >= floor, 0.0, -1e30)) for j in picks(i)]

    def lane(i):
        return aligned(i, CELLS)

    attention(NB, queries, keys, values, penalties, lane, cross_ref, bad_ref, prepare)
    out_ref[...] = mm_tn(cross_ref[...], cross_w_ref[...])


def place(land_ref):
    is_air = lax.axis_index("comp") == 0
    tile_row = lax.axis_index("tile")
    tile_col = lax.axis_index("face")
    columns = (tile_col, (tile_col + 7) % 8, (tile_col + 1) % 8)

    def flags(r):
        inside_row = jnp.where(r == 0, tile_row - 1, jnp.where(r == NB + 1, tile_row + 1, tile_row))
        lat_ok = (inside_row >= 0) & (inside_row < 8)
        safe_row = jnp.clip(inside_row, 0, 7)
        index = jnp.where(r == 0, NB - 1, jnp.where(r == NB + 1, 0, r - 1))
        return [lat_ok & (is_air | (index >= land_ref[safe_row, c])) for c in columns]

    return is_air, flags


def project(rows_x, gain_ref, qkv_ref):
    normed = norm_round(rows_x.astype(F32), gain_ref[0:1, :])
    keys = mm(normed, qkv_ref[:, D : 2 * D]).astype(BF)
    return keys, mm_tt(qkv_ref[:, 2 * D :], normed).astype(BF)


def side_flag(flags, r):
    _, west_ok, east_ok = flags(r)
    west_lane = lax.broadcasted_iota(jnp.int32, (1, CELLS), 1) < SIDE
    return jnp.where(west_lane, west_ok.astype(F32), east_ok.astype(F32))


def window_penalties(flags, i):
    pieces = []
    for b in range(3):
        for rows, flag in zip((CELLS, SIDE, SIDE), flags(i + b)):
            pieces.append((rows, jnp.where(flag, 0.0, -1e30)))
    return pieces


def finish(pieces, own_land, is_air, gain_ref, out_w_ref, up_ref, down_ref):
    front = []
    for index, win_t, update, x_rows in pieces:
        live = jnp.where(is_air | (index >= own_land), 1.0, 0.0)
        middle = x_rows.astype(F32) + live * (mm_tn(win_t, out_w_ref[...]) + update)
        front.append((live, middle, norm_round(middle, gain_ref[2:3, :])))
    gates = [0.5 * mm(mlp_input, up_ref[...]) for _, _, mlp_input in front]
    results = []
    for (live, middle, _), gate in zip(front, gates):
        hidden = (gate + gate * jnp.tanh(gate)).astype(BF)
        results.append((middle + live * mm(hidden, down_ref[...])).astype(BF))
    return results


def kernel_window(
    land_ref,
    west_ref,
    east_ref,
    gain_ref,
    qkv_ref,
    q_ref,
    k_ref,
    v_ref,
    update_ref,
    x_ref,
    out_w_ref,
    up_ref,
    down_ref,
    out_ref,
    edge_keys_ref,
    edge_va_ref,
    keys_ref,
    va_ref,
    win_ref,
    bad_ref,
):
    is_air, flags = place(land_ref)

    def put(r, offset, keys, values_t, flag):
        at = (r - 1) * GROUP + offset
        keys_ref[pl.ds(at, CELLS), :] = keys
        augment(values_t, flag, va_ref, at)

    def normed_block(members):
        rows_x = []
        for r in members:
            rows_x += [ref[(r - 1) * SIDE : r * SIDE, :] for ref in (west_ref, east_ref)]
        return norm_round(jnp.concatenate(rows_x, axis=0).astype(F32), gain_ref[0:1, :])

    def put_own(own):
        for i in own:
            at = slice(i * CELLS, (i + 1) * CELLS)
            put(i + 1, 0, k_ref[at, :], v_ref[:, at], flags(i + 1)[0])

    def put_sides(members, keys, values_t):
        for n, r in enumerate(members):
            at = slice(n * CELLS, (n + 1) * CELLS)
            put(r, CELLS, keys[at], values_t[:, at], side_flag(flags, r))

    near, far = range(1, 1 + NB // 2), range(1 + NB // 2, 1 + NB)
    near_rows = normed_block(near)
    near_keys = mm(near_rows, qkv_ref[:, D : 2 * D]).astype(BF)
    far_rows = normed_block(far)
    near_values = mm_tt(qkv_ref[:, 2 * D :], near_rows).astype(BF)
    put_own(range(NB // 2))
    far_keys = mm(far_rows, qkv_ref[:, D : 2 * D]).astype(BF)
    put_sides(near, near_keys, near_values)
    far_values = mm_tt(qkv_ref[:, 2 * D :], far_rows).astype(BF)
    put_own(range(NB // 2, NB))
    put_sides(far, far_keys, far_values)

    def queries(n, p):
        return q_ref[pl.ds(aligned(n, CELLS) + CELLS, CELLS), pl.ds(p * LANES, LANES)]

    def keys_of(n, p):
        return keys_ref[pl.ds(aligned(n, GROUP), WINDOW), pl.ds(p * LANES, LANES)]

    def values_of(n, p):
        return va_ref[pl.ds(p * VROWS, VROWS), pl.ds(aligned(n, GROUP), WINDOW)]

    def penalties(n):
        return window_penalties(flags, n + 1)

    def lane(n):
        return aligned(n, CELLS) + CELLS

    attention(NB - 2, queries, keys_of, values_of, penalties, lane, win_ref, bad_ref)
    for n, at in enumerate((0, (NB - 2) * GROUP)):
        to = slice(n * 2 * GROUP, (n + 1) * 2 * GROUP)
        edge_keys_ref[to, :] = keys_ref[at : at + 2 * GROUP, :]
        edge_va_ref[:, to] = va_ref[:, at : at + 2 * GROUP]

    own_land = land_ref[lax.axis_index("tile"), lax.axis_index("face")]
    chunk = (NB - 2) * CELLS // 2
    spans = [slice(CELLS + c * chunk, CELLS + (c + 1) * chunk) for c in range(2)]
    pieces = []
    for at in spans:
        index = (at.start + lax.broadcasted_iota(jnp.int32, (chunk, 1), 0)) // CELLS
        pieces.append((index, win_ref[:, at], update_ref[at, :], x_ref[at, :]))
    results = finish(pieces, own_land, is_air, gain_ref, out_w_ref, up_ref, down_ref)
    for at, rows in zip(spans, results):
        out_ref[at, :] = rows


def kernel_last(
    land_ref,
    north_ref,
    south_ref,
    edge_keys_ref,
    edge_va_ref,
    q_ref,
    update_ref,
    x_ref,
    gain_ref,
    qkv_ref,
    out_w_ref,
    up_ref,
    down_ref,
    held_hbm,
    out_hbm,
    keys_ref,
    va_ref,
    win_ref,
    rows_ref,
    bad_ref,
    sem,
):
    del held_hbm
    is_air, flags = place(land_ref)
    rows_x = jnp.concatenate([north_ref[...], south_ref[...]], axis=0)
    new_keys, new_values = project(rows_x, gain_ref, qkv_ref)
    for n in range(2):
        new, held = n * WINDOW + n * 2 * GROUP, n * WINDOW + (1 - n) * GROUP
        src = slice(n * 2 * GROUP, (n + 1) * 2 * GROUP)
        keys_ref[new : new + GROUP, :] = new_keys[n * GROUP : (n + 1) * GROUP]
        keys_ref[held : held + 2 * GROUP, :] = edge_keys_ref[src, :]
        va_ref[:, held : held + 2 * GROUP] = edge_va_ref[:, src]
        r = n * (NB + 1)
        at = n * GROUP
        augment(new_values[:, at : at + CELLS], flags(r)[0], va_ref, new)
        augment(new_values[:, at + CELLS : at + GROUP], side_flag(flags, r), va_ref, new + CELLS)

    def queries(n, p):
        return q_ref[pl.ds(aligned(n, ROWS - CELLS), CELLS), pl.ds(p * LANES, LANES)]

    def keys_of(n, p):
        return keys_ref[pl.ds(aligned(n, WINDOW), WINDOW), pl.ds(p * LANES, LANES)]

    def values_of(n, p):
        return va_ref[pl.ds(p * VROWS, VROWS), pl.ds(aligned(n, WINDOW), WINDOW)]

    def penalties(n):
        return window_penalties(flags, n * (NB - 1))

    def lane(n):
        return aligned(n, CELLS)

    attention(2, queries, keys_of, values_of, penalties, lane, win_ref, bad_ref)

    def edge_rows(ref):
        return jnp.concatenate([ref[:CELLS, :], ref[ROWS - CELLS :, :]], axis=0)

    own_land = land_ref[lax.axis_index("tile"), lax.axis_index("face")]
    index = lax.broadcasted_iota(jnp.int32, (2 * CELLS, 1), 0) // CELLS * (NB - 1)
    piece = (index, win_ref[...], edge_rows(update_ref), edge_rows(x_ref))
    [rows_ref[...]] = finish([piece], own_land, is_air, gain_ref, out_w_ref, up_ref, down_ref)
    copies = []
    for n in range(2):
        copy = pltpu.make_async_copy(
            rows_ref.at[pl.ds(n * CELLS, CELLS)],
            out_hbm.at[pl.ds(n * (ROWS - CELLS), CELLS)],
            sem.at[n],
        )
        copy.start()
        copies.append(copy)
    for copy in copies:
        copy.wait()


VMEM = pl.BlockSpec(memory_space=pltpu.VMEM)
ANY = pl.BlockSpec(memory_space=pl.ANY)
SMEM = pl.BlockSpec(memory_space=pltpu.SMEM)


def array(*shape, dtype=BF):
    return jax.ShapeDtypeStruct(shape, dtype)


def cost(macs, size, exps=0):
    return pl.CostEstimate(flops=2 * macs, bytes_accessed=size, transcendentals=exps)


def per_device(
    tokens,
    norm_gains,
    qkv_weight,
    out_weight,
    cross_query,
    cross_kv,
    cross_out,
    up_weight,
    down_weight,
    intersection_list,
    land_bands,
):
    grid_x = tokens[0]
    x = grid_x.reshape(ROWS, D)
    gains = norm_gains[0]
    forward = [(i, (i + 1) % 8) for i in range(8)]
    backward = [((i + 1) % 8, i) for i in range(8)]
    east_edge, west_edge, x_first = lax.optimization_barrier(
        (grid_x[:, RX - BR :], grid_x[:, :BR], x)
    )
    west = lax.ppermute(east_edge, "face", forward).reshape(NB * SIDE, D)
    east = lax.ppermute(west_edge, "face", backward).reshape(NB * SIDE, D)

    half = ROWS // 2
    block = pl.BlockSpec((half, D), lambda i: (i, 0))
    params = pltpu.CompilerParams(vmem_limit_bytes=24 * MIB)
    pair_out = pl.pallas_call(
        kernel_cross_kv,
        grid=(2,),
        in_specs=[
            block,
            pl.BlockSpec((3, D), lambda i: (0, 0)),
            pl.BlockSpec((D, 2 * D), lambda i: (0, 0)),
        ],
        out_specs=pl.BlockSpec((half, 2 * D), lambda i: (i, 0)),
        out_shape=array(ROWS, 2 * D),
        cost_estimate=cost(ROWS * D * 2 * D, 4 * MIB),
        compiler_params=params,
        name="cross_kv",
    )(x_first, gains, cross_kv[0])
    partner = lax.ppermute(pair_out, "comp", [(0, 1), (1, 0)])

    q, k, v, cross_q = pl.pallas_call(
        kernel_own,
        grid=(2,),
        in_specs=[
            block,
            pl.BlockSpec((3, D), lambda i: (0, 0)),
            pl.BlockSpec((D, 3 * D), lambda i: (0, 0)),
            pl.BlockSpec((D, D), lambda i: (0, 0)),
        ],
        out_specs=[block, block, pl.BlockSpec((D, half), lambda i: (0, i)), block],
        out_shape=[array(ROWS, D), array(ROWS, D), array(D, ROWS), array(ROWS, D)],
        cost_estimate=cost(ROWS * D * 4 * D, 7 * MIB),
        compiler_params=params,
        name="own",
    )(x_first, gains, qkv_weight[0], cross_query[0])

    bad = pltpu.VMEM((8, 2 * CELLS), F32)
    update = pl.pallas_call(
        kernel_cross,
        in_specs=[SMEM] * 2 + [VMEM] * 3,
        out_specs=VMEM,
        out_shape=jax.ShapeDtypeStruct((ROWS, D), F32),
        scratch_shapes=[pltpu.VMEM((PAIRS * VROWS, ROWS), BF), pltpu.VMEM((D, ROWS), BF), bad],
        cost_estimate=cost(8 * ROWS * 512 * D, 4 * MIB, ROWS * HEADS * 512),
        compiler_params=params,
        name="cross",
    )(
        intersection_list.transpose(0, 2, 3, 1).reshape(2, KC, NB),
        land_bands,
        cross_q,
        partner,
        cross_out[0],
    )

    west, east, update = lax.optimization_barrier((west, east, update))
    top, bottom = [
        jnp.concatenate(
            [x[at * CELLS : (at + 1) * CELLS], *[side[at * SIDE : (at + 1) * SIDE] for side in (west, east)]],
            axis=0,
        )
        for at in (0, NB - 1)
    ]
    north = lax.ppermute(bottom, "tile", forward)
    south = lax.ppermute(top, "tile", backward)

    inner, edge_keys, edge_va = pl.pallas_call(
        kernel_window,
        in_specs=[SMEM] + [VMEM] * 12,
        out_specs=[VMEM] * 3,
        out_shape=[array(ROWS, D), array(4 * GROUP, D), array(PAIRS * VROWS, 4 * GROUP)],
        scratch_shapes=[
            pltpu.VMEM((NB * GROUP, D), BF),
            pltpu.VMEM((PAIRS * VROWS, NB * GROUP), BF),
            pltpu.VMEM((D, ROWS), BF),
            bad,
        ],
        cost_estimate=cost(6 << 30, 12 * MIB, ROWS * HEADS * WINDOW),
        compiler_params=pltpu.CompilerParams(vmem_limit_bytes=28 * MIB),
        name="window",
    )(
        land_bands,
        west,
        east,
        gains,
        qkv_weight[0],
        q,
        k,
        v,
        update,
        x,
        out_weight[0],
        up_weight[0],
        down_weight[0],
    )

    result = pl.pallas_call(
        kernel_last,
        in_specs=[SMEM] + [VMEM] * 12 + [ANY],
        out_specs=ANY,
        out_shape=array(ROWS, D),
        input_output_aliases={13: 0},
        scratch_shapes=[
            pltpu.VMEM((2 * WINDOW, D), BF),
            pltpu.VMEM((PAIRS * VROWS, 2 * WINDOW), BF),
            pltpu.VMEM((D, 2 * CELLS), BF),
            pltpu.VMEM((2 * CELLS, D), BF),
            bad,
            pltpu.SemaphoreType.DMA((2,)),
        ],
        cost_estimate=cost(2 << 30, 8 * MIB, ROWS * HEADS * 256),
        compiler_params=params,
        name="last",
    )(
        land_bands,
        north,
        south,
        edge_keys,
        edge_va,
        q,
        update,
        x,
        gains,
        qkv_weight[0],
        out_weight[0],
        up_weight[0],
        down_weight[0],
        inner,
    )
    return result.reshape(1, NB * BR, RX, D)


def solution(mesh):
    placed = (
        P("comp", "tile", "face", None),
        P("comp", None, None),
        P("comp", None, None),
        P("comp", None, None),
        P("comp", None, None),
        P("comp", None, None),
        P("comp", None, None),
        P("comp", None, None),
        P("comp", None, None),
        P(None, "tile", "face", None),
        P(),
    )
    return jax.shard_map(
        per_device,
        mesh=mesh,
        in_specs=placed,
        out_specs=P("comp", "tile", "face", None),
        check_vma=False,
    )
```

```python
import jax
import jax.numpy as jnp
from jax import lax
from jax.experimental import pallas as pl
from jax.experimental.pallas import tpu as pltpu
from jax.sharding import PartitionSpec as P

D = 512
FF = 2048
HEADS = 8
PAIRS = HEADS // 2
LANES = 128
RX = 16
BR = 8
NB = 8
KC = 4
CELLS = BR * RX
ROWS = NB * CELLS
SIDE = BR * BR
GROUP = CELLS + 2 * SIDE
WINDOW = 3 * GROUP
EXTRA = 16
VROWS = LANES + EXTRA

EPSILON = 1e-05
Q_SCALE = 1.4426950408889634 / 8.0
LIMIT = 2.0**100
BF = jnp.bfloat16
F32 = jnp.float32
MIB = 1 << 20


def norm_round(values, gain):
    mean_square = jnp.mean(values * values, axis=-1, keepdims=True)
    return (values * lax.rsqrt(mean_square + EPSILON) * gain.astype(F32)).astype(BF)


def mm(a, b):
    return jnp.dot(a, b, preferred_element_type=F32)


def mm_nt(a, b):
    return lax.dot_general(a, b, (((1,), (1,)), ((), ())), preferred_element_type=F32)


def mm_tn(a, b):
    return lax.dot_general(a, b, (((0,), (0,)), ((), ())), preferred_element_type=F32)


def mm_tt(a, b):
    return lax.dot_general(a, b, (((0,), (1,)), ((), ())), preferred_element_type=F32)


def augment(values_t, flag, out_ref, lane):
    keep = flag.astype(F32).astype(BF)
    for p in range(PAIRS):
        rows = values_t[p * LANES : (p + 1) * LANES]
        out_ref[pl.ds(p * VROWS, LANES), pl.ds(lane, CELLS)] = rows * keep
        out_ref[pl.ds(p * VROWS + LANES, EXTRA), pl.ds(lane, CELLS)] = (
            jnp.ones((EXTRA, CELLS), BF) * keep
        )


def score(pair, keys):
    low = lax.broadcasted_iota(jnp.int32, pair.shape, 1) < LANES // 2
    zero = jnp.zeros_like(pair)
    stacked = jnp.concatenate([jnp.where(low, pair, zero), jnp.where(low, zero, pair)], axis=0)
    return mm_nt(keys, stacked)


def blend(values_t, terms, extra):
    both = mm(values_t, terms)
    sums = both[LANES : LANES + 8]
    share = 1.0 / (sums + extra)
    half = LANES // 2
    result = jnp.concatenate(
        [both[:half, :CELLS] * share[:1, :CELLS], both[half:LANES, CELLS:] * share[:1, CELLS:]],
        axis=0,
    )
    return result.astype(BF), sums


def attention(count, queries, keys, values, penalties, lane, out_ref, bad_ref, prepare=None):
    bad_ref[...] = jnp.zeros_like(bad_ref)

    def terms_of(i, p):
        return jnp.exp2(score(queries(i, p), keys(i, p))).astype(BF)

    steps = [(i, p) for i in range(count) for p in range(PAIRS)]
    following = terms_of(*steps[0])
    if prepare:
        prepare()
    for n, (i, p) in enumerate(steps):
        terms = following
        if n + 1 < len(steps):
            following = terms_of(*steps[n + 1])
        result, sums = blend(values(i, p), terms, 1.0)
        out_ref[pl.ds(p * LANES, LANES), pl.ds(lane(i), CELLS)] = result
        bad_ref[...] += jnp.where(sums < LIMIT, 0.0, 1.0)

    @pl.when(jnp.sum(bad_ref[...]) > 0.0)
    def _():
        def band(i, carry):
            for p in range(PAIRS):
                scores = score(queries(i, p), keys(i, p))
                at = 0
                pieces = []
                for rows, penalty in penalties(i):
                    pieces.append(scores[at : at + rows] + penalty)
                    at += rows
                scores = jnp.concatenate(pieces, axis=0)
                highest = jnp.maximum(jnp.max(scores, axis=0, keepdims=True), 0.0)
                terms = jnp.exp2(scores - highest).astype(BF)
                result, _ = blend(values(i, p), terms, jnp.exp2(-highest))
                out_ref[pl.ds(p * LANES, LANES), pl.ds(lane(i), CELLS)] = result
            return carry

        lax.fori_loop(0, count, band, 0)


def aligned(i, size):
    return i * size if isinstance(i, int) else pl.multiple_of(i * size, size)


def kernel_cross_kv(x_ref, gain_ref, weight_ref, out_ref):
    cross_input = norm_round(x_ref[...].astype(F32), gain_ref[1:2, :])
    out_ref[:, :D] = mm(cross_input, weight_ref[:, :D]).astype(BF)
    out_ref[:, D:] = mm_tt(weight_ref[:, D:], cross_input).astype(BF)


def kernel_own(x_ref, gain_ref, qkv_ref, cq_ref, q_ref, k_ref, v_ref, c_ref):
    values = x_ref[...].astype(F32)
    mean_square = jnp.mean(values * values, axis=-1, keepdims=True)
    unit = values * lax.rsqrt(mean_square + EPSILON)
    attn_input = (unit * gain_ref[0:1, :].astype(F32)).astype(BF)
    cross_input = (unit * gain_ref[1:2, :].astype(F32)).astype(BF)
    q_ref[...] = (mm(attn_input, qkv_ref[:, :D]) * Q_SCALE).astype(BF)
    k_ref[...] = mm(attn_input, qkv_ref[:, D : 2 * D]).astype(BF)
    v_ref[...] = mm_tt(qkv_ref[:, 2 * D :], attn_input).astype(BF)
    c_ref[...] = (mm(cross_input, cq_ref[...]) * Q_SCALE).astype(BF)


def kernel_cross(links_ref, land_ref, q_ref, kv_ref, cross_w_ref, out_ref, va_ref, cross_ref, bad_ref):
    component = lax.axis_index("comp")
    own_land = land_ref[lax.axis_index("tile"), lax.axis_index("face")]
    floor = jnp.where(component == 1, 0, own_land)

    def prepare():
        for j in range(NB):
            row, lane = (j // 4) * D, D + (j % 4) * CELLS
            augment(kv_ref[row : row + D, lane : lane + CELLS], j >= floor, va_ref, j * CELLS)

    def picks(i):
        return [links_ref[component, k, i] for k in range(KC)]

    def queries(i, p):
        return q_ref[pl.ds(aligned(i, CELLS), CELLS), pl.ds(p * LANES, LANES)]

    def keys(i, p):
        return jnp.concatenate(
            [kv_ref[pl.ds(aligned(j, CELLS), CELLS), pl.ds(p * LANES, LANES)] for j in picks(i)],
            axis=0,
        )

    def values(i, p):
        return jnp.concatenate(
            [va_ref[pl.ds(p * VROWS, VROWS), pl.ds(aligned(j, CELLS), CELLS)] for j in picks(i)],
            axis=1,
        )

    def penalties(i):
        return [(CELLS, jnp.where(j >= floor, 0.0, -1e30)) for j in picks(i)]

    def lane(i):
        return aligned(i, CELLS)

    attention(NB, queries, keys, values, penalties, lane, cross_ref, bad_ref, prepare)
    out_ref[...] = mm_tn(cross_ref[...], cross_w_ref[...])


def place(land_ref):
    is_air = lax.axis_index("comp") == 0
    tile_row = lax.axis_index("tile")
    tile_col = lax.axis_index("face")
    columns = (tile_col, (tile_col + 7) % 8, (tile_col + 1) % 8)

    def flags(r):
        inside_row = jnp.where(r == 0, tile_row - 1, jnp.where(r == NB + 1, tile_row + 1, tile_row))
        lat_ok = (inside_row >= 0) & (inside_row < 8)
        safe_row = jnp.clip(inside_row, 0, 7)
        index = jnp.where(r == 0, NB - 1, jnp.where(r == NB + 1, 0, r - 1))
        return [lat_ok & (is_air | (index >= land_ref[safe_row, c])) for c in columns]

    return is_air, flags


def project(rows_x, gain_ref, qkv_ref):
    normed = norm_round(rows_x.astype(F32), gain_ref[0:1, :])
    keys = mm(normed, qkv_ref[:, D : 2 * D]).astype(BF)
    return keys, mm_tt(qkv_ref[:, 2 * D :], normed).astype(BF)


def side_flag(flags, r):
    _, west_ok, east_ok = flags(r)
    west_lane = lax.broadcasted_iota(jnp.int32, (1, CELLS), 1) < SIDE
    return jnp.where(west_lane, west_ok.astype(F32), east_ok.astype(F32))


def window_penalties(flags, i):
    pieces = []
    for b in range(3):
        for rows, flag in zip((CELLS, SIDE, SIDE), flags(i + b)):
            pieces.append((rows, jnp.where(flag, 0.0, -1e30)))
    return pieces


def finish(pieces, own_land, is_air, gain_ref, out_w_ref, up_ref, down_ref):
    front = []
    for index, win_t, update, x_rows in pieces:
        live = jnp.where(is_air | (index >= own_land), 1.0, 0.0)
        middle = x_rows.astype(F32) + live * (mm_tn(win_t, out_w_ref[...]) + update)
        front.append((live, middle, norm_round(middle, gain_ref[2:3, :])))
    gates = [0.5 * mm(mlp_input, up_ref[...]) for _, _, mlp_input in front]
    results = []
    for (live, middle, _), gate in zip(front, gates):
        hidden = (gate + gate * jnp.tanh(gate)).astype(BF)
        results.append((middle + live * mm(hidden, down_ref[...])).astype(BF))
    return results


def kernel_window(
    land_ref,
    west_ref,
    east_ref,
    gain_ref,
    qkv_ref,
    q_ref,
    k_ref,
    v_ref,
    update_ref,
    x_ref,
    out_w_ref,
    up_ref,
    down_ref,
    out_ref,
    edge_keys_ref,
    edge_va_ref,
    keys_ref,
    va_ref,
    win_ref,
    bad_ref,
):
    is_air, flags = place(land_ref)

    def put(r, offset, keys, values_t, flag):
        at = (r - 1) * GROUP + offset
        keys_ref[pl.ds(at, CELLS), :] = keys
        augment(values_t, flag, va_ref, at)

    def normed_block(members):
        rows_x = []
        for r in members:
            rows_x += [ref[(r - 1) * SIDE : r * SIDE, :] for ref in (west_ref, east_ref)]
        return norm_round(jnp.concatenate(rows_x, axis=0).astype(F32), gain_ref[0:1, :])

    def put_own(own):
        for i in own:
            at = slice(i * CELLS, (i + 1) * CELLS)
            put(i + 1, 0, k_ref[at, :], v_ref[:, at], flags(i + 1)[0])

    def put_sides(members, keys, values_t):
        for n, r in enumerate(members):
            at = slice(n * CELLS, (n + 1) * CELLS)
            put(r, CELLS, keys[at], values_t[:, at], side_flag(flags, r))

    near, far = range(1, 1 + NB // 2), range(1 + NB // 2, 1 + NB)
    near_rows = normed_block(near)
    near_keys = mm(near_rows, qkv_ref[:, D : 2 * D]).astype(BF)
    far_rows = normed_block(far)
    near_values = mm_tt(qkv_ref[:, 2 * D :], near_rows).astype(BF)
    put_own(range(NB // 2))
    far_keys = mm(far_rows, qkv_ref[:, D : 2 * D]).astype(BF)
    put_sides(near, near_keys, near_values)
    far_values = mm_tt(qkv_ref[:, 2 * D :], far_rows).astype(BF)
    put_own(range(NB // 2, NB))
    put_sides(far, far_keys, far_values)

    def queries(n, p):
        return q_ref[pl.ds(aligned(n, CELLS) + CELLS, CELLS), pl.ds(p * LANES, LANES)]

    def keys_of(n, p):
        return keys_ref[pl.ds(aligned(n, GROUP), WINDOW), pl.ds(p * LANES, LANES)]

    def values_of(n, p):
        return va_ref[pl.ds(p * VROWS, VROWS), pl.ds(aligned(n, GROUP), WINDOW)]

    def penalties(n):
        return window_penalties(flags, n + 1)

    def lane(n):
        return aligned(n, CELLS) + CELLS

    attention(NB - 2, queries, keys_of, values_of, penalties, lane, win_ref, bad_ref)
    for n, at in enumerate((0, (NB - 2) * GROUP)):
        to = slice(n * 2 * GROUP, (n + 1) * 2 * GROUP)
        edge_keys_ref[to, :] = keys_ref[at : at + 2 * GROUP, :]
        edge_va_ref[:, to] = va_ref[:, at : at + 2 * GROUP]

    own_land = land_ref[lax.axis_index("tile"), lax.axis_index("face")]
    chunk = (NB - 2) * CELLS
    spans = [slice(CELLS, CELLS + chunk)]
    pieces = []
    for at in spans:
        index = (at.start + lax.broadcasted_iota(jnp.int32, (chunk, 1), 0)) // CELLS
        pieces.append((index, win_ref[:, at], update_ref[at, :], x_ref[at, :]))
    results = finish(pieces, own_land, is_air, gain_ref, out_w_ref, up_ref, down_ref)
    for at, rows in zip(spans, results):
        out_ref[at, :] = rows


def kernel_last(
    land_ref,
    north_ref,
    south_ref,
    edge_keys_ref,
    edge_va_ref,
    q_ref,
    update_ref,
    x_ref,
    gain_ref,
    qkv_ref,
    out_w_ref,
    up_ref,
    down_ref,
    held_hbm,
    out_hbm,
    keys_ref,
    va_ref,
    win_ref,
    rows_ref,
    bad_ref,
    sem,
):
    del held_hbm
    is_air, flags = place(land_ref)
    rows_x = jnp.concatenate([north_ref[...], south_ref[...]], axis=0)
    normed = norm_round(rows_x.astype(F32), gain_ref[0:1, :])
    new_keys = mm(normed, qkv_ref[:, D : 2 * D]).astype(BF)
    for n in range(2):
        held = n * WINDOW + (1 - n) * GROUP
        src = slice(n * 2 * GROUP, (n + 1) * 2 * GROUP)
        keys_ref[held : held + 2 * GROUP, :] = edge_keys_ref[src, :]
        va_ref[:, held : held + 2 * GROUP] = edge_va_ref[:, src]
    new_values = mm_tt(qkv_ref[:, 2 * D :], normed).astype(BF)
    for n in range(2):
        new = n * WINDOW + n * 2 * GROUP
        keys_ref[new : new + GROUP, :] = new_keys[n * GROUP : (n + 1) * GROUP]
        r = n * (NB + 1)
        at = n * GROUP
        augment(new_values[:, at : at + CELLS], flags(r)[0], va_ref, new)
        augment(new_values[:, at + CELLS : at + GROUP], side_flag(flags, r), va_ref, new + CELLS)

    def queries(n, p):
        return q_ref[pl.ds(aligned(n, ROWS - CELLS), CELLS), pl.ds(p * LANES, LANES)]

    def keys_of(n, p):
        return keys_ref[pl.ds(aligned(n, WINDOW), WINDOW), pl.ds(p * LANES, LANES)]

    def values_of(n, p):
        return va_ref[pl.ds(p * VROWS, VROWS), pl.ds(aligned(n, WINDOW), WINDOW)]

    def penalties(n):
        return window_penalties(flags, n * (NB - 1))

    def lane(n):
        return aligned(n, CELLS)

    attention(2, queries, keys_of, values_of, penalties, lane, win_ref, bad_ref)

    def edge_rows(ref):
        return jnp.concatenate([ref[:CELLS, :], ref[ROWS - CELLS :, :]], axis=0)

    own_land = land_ref[lax.axis_index("tile"), lax.axis_index("face")]
    index = lax.broadcasted_iota(jnp.int32, (2 * CELLS, 1), 0) // CELLS * (NB - 1)
    piece = (index, win_ref[...], edge_rows(update_ref), edge_rows(x_ref))
    [rows_ref[...]] = finish([piece], own_land, is_air, gain_ref, out_w_ref, up_ref, down_ref)
    copies = []
    for n in range(2):
        copy = pltpu.make_async_copy(
            rows_ref.at[pl.ds(n * CELLS, CELLS)],
            out_hbm.at[pl.ds(n * (ROWS - CELLS), CELLS)],
            sem.at[n],
        )
        copy.start()
        copies.append(copy)
    for copy in copies:
        copy.wait()


VMEM = pl.BlockSpec(memory_space=pltpu.VMEM)
ANY = pl.BlockSpec(memory_space=pl.ANY)
SMEM = pl.BlockSpec(memory_space=pltpu.SMEM)


def array(*shape, dtype=BF):
    return jax.ShapeDtypeStruct(shape, dtype)


def cost(macs, size, exps=0):
    return pl.CostEstimate(flops=2 * macs, bytes_accessed=size, transcendentals=exps)


def per_device(
    tokens,
    norm_gains,
    qkv_weight,
    out_weight,
    cross_query,
    cross_kv,
    cross_out,
    up_weight,
    down_weight,
    intersection_list,
    land_bands,
):
    grid_x = tokens[0]
    x = grid_x.reshape(ROWS, D)
    gains = norm_gains[0]
    forward = [(i, (i + 1) % 8) for i in range(8)]
    backward = [((i + 1) % 8, i) for i in range(8)]
    east_edge, west_edge, x_first = lax.optimization_barrier(
        (grid_x[:, RX - BR :], grid_x[:, :BR], x)
    )
    west = lax.ppermute(east_edge, "face", forward).reshape(NB * SIDE, D)
    east = lax.ppermute(west_edge, "face", backward).reshape(NB * SIDE, D)

    half = ROWS // 2
    block = pl.BlockSpec((half, D), lambda i: (i, 0))
    params = pltpu.CompilerParams(vmem_limit_bytes=24 * MIB)
    pair_out = pl.pallas_call(
        kernel_cross_kv,
        grid=(2,),
        in_specs=[
            block,
            pl.BlockSpec((3, D), lambda i: (0, 0)),
            pl.BlockSpec((D, 2 * D), lambda i: (0, 0)),
        ],
        out_specs=pl.BlockSpec((half, 2 * D), lambda i: (i, 0)),
        out_shape=array(ROWS, 2 * D),
        cost_estimate=cost(ROWS * D * 2 * D, 4 * MIB),
        compiler_params=params,
        name="cross_kv",
    )(x_first, gains, cross_kv[0])
    partner = lax.ppermute(pair_out, "comp", [(0, 1), (1, 0)])

    q, k, v, cross_q = pl.pallas_call(
        kernel_own,
        grid=(2,),
        in_specs=[
            block,
            pl.BlockSpec((3, D), lambda i: (0, 0)),
            pl.BlockSpec((D, 3 * D), lambda i: (0, 0)),
            pl.BlockSpec((D, D), lambda i: (0, 0)),
        ],
        out_specs=[block, block, pl.BlockSpec((D, half), lambda i: (0, i)), block],
        out_shape=[array(ROWS, D), array(ROWS, D), array(D, ROWS), array(ROWS, D)],
        cost_estimate=cost(ROWS * D * 4 * D, 7 * MIB),
        compiler_params=params,
        name="own",
    )(x_first, gains, qkv_weight[0], cross_query[0])

    bad = pltpu.VMEM((8, 2 * CELLS), F32)
    update = pl.pallas_call(
        kernel_cross,
        in_specs=[SMEM] * 2 + [VMEM] * 3,
        out_specs=VMEM,
        out_shape=jax.ShapeDtypeStruct((ROWS, D), F32),
        scratch_shapes=[pltpu.VMEM((PAIRS * VROWS, ROWS), BF), pltpu.VMEM((D, ROWS), BF), bad],
        cost_estimate=cost(8 * ROWS * 512 * D, 4 * MIB, ROWS * HEADS * 512),
        compiler_params=params,
        name="cross",
    )(
        intersection_list.transpose(0, 2, 3, 1).reshape(2, KC, NB),
        land_bands,
        cross_q,
        partner,
        cross_out[0],
    )

    west, east, update = lax.optimization_barrier((west, east, update))
    top, bottom = [
        jnp.concatenate(
            [x[at * CELLS : (at + 1) * CELLS], *[side[at * SIDE : (at + 1) * SIDE] for side in (west, east)]],
            axis=0,
        )
        for at in (0, NB - 1)
    ]
    north = lax.ppermute(bottom, "tile", forward)
    south = lax.ppermute(top, "tile", backward)

    inner, edge_keys, edge_va = pl.pallas_call(
        kernel_window,
        in_specs=[SMEM] + [VMEM] * 12,
        out_specs=[VMEM] * 3,
        out_shape=[array(ROWS, D), array(4 * GROUP, D), array(PAIRS * VROWS, 4 * GROUP)],
        scratch_shapes=[
            pltpu.VMEM((NB * GROUP, D), BF),
            pltpu.VMEM((PAIRS * VROWS, NB * GROUP), BF),
            pltpu.VMEM((D, ROWS), BF),
            bad,
        ],
        cost_estimate=cost(6 << 30, 12 * MIB, ROWS * HEADS * WINDOW),
        compiler_params=pltpu.CompilerParams(vmem_limit_bytes=28 * MIB),
        name="window",
    )(
        land_bands,
        west,
        east,
        gains,
        qkv_weight[0],
        q,
        k,
        v,
        update,
        x,
        out_weight[0],
        up_weight[0],
        down_weight[0],
    )

    result = pl.pallas_call(
        kernel_last,
        in_specs=[SMEM] + [VMEM] * 12 + [ANY],
        out_specs=ANY,
        out_shape=array(ROWS, D),
        input_output_aliases={13: 0},
        scratch_shapes=[
            pltpu.VMEM((2 * WINDOW, D), BF),
            pltpu.VMEM((PAIRS * VROWS, 2 * WINDOW), BF),
            pltpu.VMEM((D, 2 * CELLS), BF),
            pltpu.VMEM((2 * CELLS, D), BF),
            bad,
            pltpu.SemaphoreType.DMA((2,)),
        ],
        cost_estimate=cost(2 << 30, 8 * MIB, ROWS * HEADS * 256),
        compiler_params=params,
        name="last",
    )(
        land_bands,
        north,
        south,
        edge_keys,
        edge_va,
        q,
        update,
        x,
        gains,
        qkv_weight[0],
        out_weight[0],
        up_weight[0],
        down_weight[0],
        inner,
    )
    return result.reshape(1, NB * BR, RX, D)


def solution(mesh):
    placed = (
        P("comp", "tile", "face", None),
        P("comp", None, None),
        P("comp", None, None),
        P("comp", None, None),
        P("comp", None, None),
        P("comp", None, None),
        P("comp", None, None),
        P("comp", None, None),
        P("comp", None, None),
        P(None, "tile", "face", None),
        P(),
    )
    return jax.shard_map(
        per_device,
        mesh=mesh,
        in_specs=placed,
        out_specs=P("comp", "tile", "face", None),
        check_vma=False,
    )
```
